32 devices in a mesh: kv: 2 (over x), wide: 16 (over z, y, core).
Axes of the slice: x: 2, y: 2, z: 4, core: 2. Of those that a mesh axis runs over, the one named last changes fastest.
Arguments:
- hidden_input: bfloat16 [48, 16384], P(None, 'kv'), may hold values from -6 to 6
- input_norm_gain: float32 [16384], P('kv'), may hold values from 0.25 to 1.75
- joint_projection_weight: bfloat16 [16384, 18432], P('kv', 'wide'), may hold values from -0.046875 to 0.046875
- output_weight: bfloat16 [16384, 16384], P('kv', 'wide'), may hold values from -0.046875 to 0.046875
- key_cache: bfloat16 [48, 8, 512, 128], P('wide', 'kv'), may hold values from -210 to 210
- value_cache: bfloat16 [48, 8, 512, 128], P('wide', 'kv'), may hold values from -6 to 6
- joint_down_weight: bfloat16 [16, 16384, 24], P('wide', 'kv'), may hold values from -0.046875 to 0.046875
- query_up_weight: bfloat16 [16, 8, 16384], P('wide', None, 'kv'), may hold values from -2 to 2
- key_value_up_weight: bfloat16 [16, 2, 8, 1024], P('wide', None, None, 'kv'), may hold values from -2 to 2
- output_down_weight: bfloat16 [16, 16384, 8], P('wide', 'kv'), may hold values from -0.046875 to 0.046875
- output_up_weight: bfloat16 [16, 8, 16384], P('wide'), may hold values from -2 to 2
- row_adapter_index: int32 [48], replicated, may hold values from 0 to 15
- adapter_owner_slot: int32 [16], replicated, may hold values from 0 to 15, each once
- lengths: int32 [48], P('wide'), may hold values from 64 to 512, as said below
Outputs:
- out: bfloat16 [48, 16384], P('kv', 'wide')
The draws below stay inside these ranges and needn't reach their ends.
Inputs may be any that keep to these rules, and one draw needn't show every extreme that they name: Row lengths; at least one row has exactly 512. `adapter_owner_slot`: each adapter's owner slot, a permutation.
All inputs are finite; a program needn't handle non-finite values.
Results may differ from the reference program's by a relative error of at most 0.019.
The reference program's roundings to bfloat16 on the way count: a program that leaves them out, or rounds other values in their place, can miss the bound.
Values may be sent and summed in bfloat16 or wider, within the bound.
No kernel may reach another device: no remote copies, remote signals or barrier semaphores. Data moves between devices by JAX's collectives and lax.ppermute only.
A program may use at most 128 MiB of HBM per device.

```python
import math
import jax
import jax.numpy as jnp
import numpy as np
from jax import lax

MODEL_WIDTH = 16384
QUERY_HEADS = 128
KEY_HEADS = 8
HEAD_SIZE = 128
ADAPTER_RANK = 8
CACHE = 512
GROUP = 16
QKV = 18432
ADAPTER_TOTAL = 16
BATCH = 48


def draw_lengths(key, part):
    lens = jax.random.randint(key, (BATCH,), CACHE // 8, CACHE + 1)
    full_row = jax.random.randint(jax.random.fold_in(key, 7), (), 0, BATCH)
    return jnp.where(jnp.arange(BATCH) == full_row, CACHE, lens).astype(jnp.int32)


def draw_key_cache(key, part):
    array_shape = (BATCH, KEY_HEADS, CACHE, HEAD_SIZE)
    base_output = jax.random.normal(key, array_shape, jnp.float32)
    return base_output.astype(jnp.bfloat16)


def set_ends(values, key, least, high):
    spot = [jax.random.randint(jax.random.fold_in(key, axis), (), 0, length) for axis, length in enumerate(values.shape)]
    main_axis = values.shape.index(max(values.shape))
    beside = spot[:main_axis] + [(spot[main_axis] + 1) % values.shape[main_axis]] + spot[main_axis + 1:]
    return values.at[tuple(spot)].set(least).at[tuple(beside)].set(high)


def level_of(stream_key, extent, shards, least, high):
    gain, own = 1.0, jax.random.fold_in(stream_key, 6)
    for axis_at, blocks in shards:
        heights = jnp.exp(jax.random.uniform(jax.random.fold_in(own, axis_at), (blocks,), jnp.float32, least / len(shards), high / len(shards)))
        gain = gain * jnp.repeat(heights, extent[axis_at] // blocks).reshape([-1 if axis == axis_at else 1 for axis in range(len(extent))])
    return gain


def rank_bounds(number_of, slope):
    portions = [(1 << 20) // math.isqrt(standing ** slope) + 1 for standing in range(1, number_of + 1)]
    scale = 1 + sum(portions) // (1 << 30)
    return np.cumsum(np.array([max(1, weight // scale) for weight in portions]))


def ranked(own_key, dims, count, lean):
    grid = rank_bounds(count, lean)
    lot = jax.random.randint(jax.random.fold_in(own_key, 1), dims, 0, int(grid[count - 1]))
    rank = jnp.searchsorted(jnp.asarray(grid, jnp.int32), lot, side="right")
    return jax.random.permutation(jax.random.fold_in(own_key, 2), count)[rank].astype(jnp.int32)


def normal_values(stream_key, shape, scale, most, pieces=(), kind=jnp.bfloat16):
    entries = jax.random.normal(stream_key, shape, jnp.float32) * scale
    if len(pieces) > 0:
        entries = level_of(stream_key, shape, pieces, -0.22, 0.18) * entries
    return jnp.clip(entries, min=-most, max=most).astype(kind)


def setup_inputs(seed: int = 0) -> dict:
    key_of = jax.random.split(jax.random.key(seed), 15)
    hidden_input = normal_values(key_of[0], (BATCH, MODEL_WIDTH), 1.0, 6.0, ((1, 2),))
    input_norm_gain = jnp.clip(1.0 + 0.15 * jax.random.normal(key_of[1], (MODEL_WIDTH,), jnp.float32), 0.25, 1.75)
    joint_projection_weight = normal_values(key_of[2], (MODEL_WIDTH, QKV), MODEL_WIDTH ** -0.5, 0.046875, ((0, 2), (1, 16)))
    output_weight = normal_values(key_of[3], (QUERY_HEADS * HEAD_SIZE, MODEL_WIDTH), (QUERY_HEADS * HEAD_SIZE) ** -0.5, 0.046875, ((0, 2), (1, 16)))
    key_cache = draw_key_cache(jax.random.fold_in(key_of[14], 71), 0)
    value_cache = normal_values(key_of[5], (BATCH, KEY_HEADS, CACHE, HEAD_SIZE), 1.0, 6.0, ((0, 16), (1, 2)))
    joint_down_weight = normal_values(key_of[6], (ADAPTER_TOTAL, MODEL_WIDTH, 3 * ADAPTER_RANK), MODEL_WIDTH ** -0.5, 0.046875, ((0, 16), (1, 2)))
    query_up_weight = normal_values(key_of[7], (ADAPTER_TOTAL, ADAPTER_RANK, QUERY_HEADS * HEAD_SIZE), ADAPTER_RANK ** -0.5, 2.0, ((0, 16), (2, 2)))
    key_value_up_weight = normal_values(key_of[8], (ADAPTER_TOTAL, 2, ADAPTER_RANK, KEY_HEADS * HEAD_SIZE), ADAPTER_RANK ** -0.5, 2.0, ((0, 16), (3, 2)))
    output_down_weight = normal_values(key_of[9], (ADAPTER_TOTAL, QUERY_HEADS * HEAD_SIZE, ADAPTER_RANK), (QUERY_HEADS * HEAD_SIZE) ** -0.5, 0.046875, ((0, 16), (1, 2)))
    output_up_weight = normal_values(key_of[10], (ADAPTER_TOTAL, ADAPTER_RANK, MODEL_WIDTH), ADAPTER_RANK ** -0.5, 2.0, ((0, 16),))
    row_adapter_index = set_ends(ranked(key_of[11], (BATCH,), ADAPTER_TOTAL, 2), jax.random.fold_in(key_of[11], 3), 0, ADAPTER_TOTAL - 1).astype(jnp.int32)
    adapter_owner_slot = jax.random.permutation(key_of[12], ADAPTER_TOTAL).astype(jnp.int32)
    lengths = draw_lengths(jax.random.fold_in(key_of[14], 71), 0)
    return {"hidden_input": hidden_input, "input_norm_gain": input_norm_gain, "joint_projection_weight": joint_projection_weight, "output_weight": output_weight, "key_cache": key_cache, "value_cache": value_cache, "joint_down_weight": joint_down_weight, "query_up_weight": query_up_weight, "key_value_up_weight": key_value_up_weight, "output_down_weight": output_down_weight, "output_up_weight": output_up_weight, "row_adapter_index": row_adapter_index, "adapter_owner_slot": adapter_owner_slot, "lengths": lengths}


rope_base = 500000.0
adapter_scale = 2.0

def rotate(values, positions):
    half = values.shape[-1] // 2
    freq = rope_base ** (-jnp.arange(half, dtype=jnp.float32) * 2.0 / values.shape[-1])
    angle = positions.astype(jnp.float32)[:, None] * freq[None, :]
    array_shape = (angle.shape[0],) + (1,) * (values.ndim - 2) + (half,)
    cosine = jnp.cos(angle).reshape(array_shape)
    sine = jnp.sin(angle).reshape(array_shape)
    first = values[..., :half]
    second = values[..., half:]
    return jnp.concatenate([first * cosine - second * sine, second * cosine + first * sine], axis=-1)

def reference(hidden_input, input_norm_gain, joint_projection_weight, output_weight, key_cache, value_cache, joint_down_weight, query_up_weight, key_value_up_weight, output_down_weight, output_up_weight, row_adapter_index, adapter_owner_slot, lengths):
    widened = hidden_input.astype(jnp.float32)
    scale = lax.rsqrt(lax.optimization_barrier(jnp.sum(widened * widened, axis=1)) / MODEL_WIDTH + 1e-05)
    scaled_hidden = (widened * input_norm_gain.astype(jnp.float32)[None, :]).astype(jnp.bfloat16)
    owner_slots = adapter_owner_slot[row_adapter_index].astype(jnp.int32)
    base_output = jnp.dot(scaled_hidden, joint_projection_weight, preferred_element_type=jnp.float32) * scale[:, None]
    reduced_everywhere = jnp.einsum('qy,tya->qta', scaled_hidden.astype(jnp.float32), joint_down_weight.astype(jnp.float32))
    reduced_hidden = jnp.take_along_axis(reduced_everywhere, owner_slots[:, None, None], axis=1)[:, 0]
    reduced_hidden = (reduced_hidden * scale[:, None]).astype(jnp.bfloat16).astype(jnp.float32)
    query_change = jnp.einsum('xq,xqi->xi', reduced_hidden[:, :ADAPTER_RANK], query_up_weight[owner_slots].astype(jnp.float32))
    key_change = jnp.einsum('xq,xqi->xi', reduced_hidden[:, ADAPTER_RANK:2 * ADAPTER_RANK], key_value_up_weight[owner_slots, 0].astype(jnp.float32))
    value_change = jnp.einsum('xq,xqi->xi', reduced_hidden[:, 2 * ADAPTER_RANK:], key_value_up_weight[owner_slots, 1].astype(jnp.float32))
    batch_rows = hidden_input.shape[0]
    adapter_change = jnp.concatenate([query_change.reshape(batch_rows, KEY_HEADS, -1), key_change.reshape(batch_rows, KEY_HEADS, -1), value_change.reshape(batch_rows, KEY_HEADS, -1)], axis=2)
    merged_output = base_output.reshape(batch_rows, KEY_HEADS, -1) + adapter_scale * adapter_change
    width = GROUP * HEAD_SIZE
    query_vector = rotate(merged_output[:, :, :width].reshape(batch_rows, KEY_HEADS, GROUP, HEAD_SIZE), lengths).astype(jnp.bfloat16).astype(jnp.float32)
    fresh_key = rotate(merged_output[:, :, width:width + HEAD_SIZE], lengths).astype(jnp.bfloat16).astype(jnp.float32)
    value_new = merged_output[:, :, width + HEAD_SIZE:].astype(jnp.bfloat16).astype(jnp.float32)
    inverse_root = jnp.sqrt(jnp.float32(HEAD_SIZE))
    scores = jnp.einsum('bkgd,bkld->bkgl', query_vector, key_cache.astype(jnp.float32)) / inverse_root
    valid = jnp.arange(CACHE, dtype=jnp.int32)[None, :] < lengths[:, None]
    scores = jnp.where(valid[:, None, None, :], scores, -jnp.inf)
    fresh_score = jnp.einsum('ajtm,ajm->ajt', query_vector, fresh_key) / inverse_root
    top = jnp.maximum(lax.optimization_barrier(jnp.max(scores, axis=-1)), fresh_score)
    expd = jnp.exp(scores - top[..., None])
    exp_new = jnp.exp(fresh_score - top)
    total = lax.optimization_barrier(jnp.sum(expd, axis=-1)) + exp_new
    probs = (expd / total[..., None]).astype(jnp.bfloat16).astype(jnp.float32)
    prob_new = (exp_new / total).astype(jnp.bfloat16).astype(jnp.float32)
    attention_output = jnp.einsum('bkgl,bkld->bkgd', probs, value_cache.astype(jnp.float32)) + prob_new[..., None] * value_new[:, :, None, :]
    attention_output = attention_output.astype(jnp.bfloat16).reshape(batch_rows, QUERY_HEADS * HEAD_SIZE)
    output_baseline = jnp.dot(attention_output, output_weight, preferred_element_type=jnp.float32)
    output_everywhere = jnp.einsum('iv,gvl->igl', attention_output.astype(jnp.float32), output_down_weight.astype(jnp.float32))
    output_reduced = jnp.take_along_axis(output_everywhere, owner_slots[:, None, None], axis=1)[:, 0].astype(jnp.bfloat16).astype(jnp.float32)
    output_change = jnp.einsum('pc,pcw->pw', output_reduced, output_up_weight[owner_slots].astype(jnp.float32))
    return (output_baseline + adapter_scale * output_change).astype(jnp.bfloat16)
```

```python
import jax
import jax.numpy as jnp
from jax import lax
from jax.sharding import PartitionSpec as P

MODEL_WIDTH = 16384


rope_base = 500000.0
adapter_scale = 2.0


def rotate(values, positions):
    half = values.shape[-1] // 2
    freq = rope_base ** (-jnp.arange(half, dtype=jnp.float32) * 2.0 / values.shape[-1])
    angle = positions.astype(jnp.float32)[:, None] * freq[None, :]
    array_shape = (angle.shape[0],) + (1,) * (values.ndim - 2) + (half,)
    cosine = jnp.cos(angle).reshape(array_shape)
    sine = jnp.sin(angle).reshape(array_shape)
    first = values[..., :half]
    second = values[..., half:]
    return jnp.concatenate(
        [first * cosine - second * sine, second * cosine + first * sine], axis=-1
    )


def arrange(query_change, key_change, value_change, local_key_value):
    count = query_change.shape[0]
    joined = jnp.concatenate(
        [
            query_change.reshape(count, local_key_value, -1),
            key_change.reshape(count, local_key_value, -1),
            value_change.reshape(count, local_key_value, -1),
        ],
        axis=2,
    )
    return joined.reshape(count, -1)


def general_path(
    hidden_input,
    input_norm_gain,
    joint_projection_weight,
    output_weight,
    key_cache,
    value_cache,
    joint_down_weight,
    query_up_weight,
    key_value_up_weight,
    output_down_weight,
    output_up_weight,
    row_adapter_index,
    adapter_owner_slot,
    lengths,
):
    local_rows = lengths.shape[0]
    local_key_value = key_cache.shape[1]
    head_dim = key_cache.shape[3]
    rank_width = query_up_weight.shape[1]
    wide_pos = lax.axis_index("wide")
    kv_pos = lax.axis_index("kv")
    row_start = wide_pos * local_rows
    table = (
        row_adapter_index[:, None]
        == jnp.arange(adapter_owner_slot.shape[0], dtype=jnp.int32)[None, :]
    )
    row_slot = jnp.sum(jnp.where(table, adapter_owner_slot[None, :], 0), axis=1)
    mine = (row_slot == wide_pos).astype(jnp.float32)
    widened = hidden_input.astype(jnp.float32)
    scaled_hidden = (widened * input_norm_gain[None, :]).astype(jnp.bfloat16)
    partial_sq = jnp.sum(widened * widened, axis=1)
    partial_reduced = jnp.dot(
        scaled_hidden, joint_down_weight[0], preferred_element_type=jnp.float32
    )
    total_sq, reduced_hidden = lax.psum((partial_sq, partial_reduced), "kv")
    scale = lax.rsqrt(total_sq / MODEL_WIDTH + 1e-05)
    shrink_bf = (reduced_hidden * scale[:, None] * mine[:, None]).astype(jnp.bfloat16)
    base_part = jnp.dot(scaled_hidden, joint_projection_weight, preferred_element_type=jnp.float32)
    regrouped = lax.all_to_all(base_part, "wide", split_axis=0, concat_axis=1, tiled=True)
    grouped_heads = lax.psum_scatter(regrouped, "kv", scatter_dimension=1, tiled=True)
    row_scale = lax.dynamic_slice_in_dim(scale, row_start, local_rows)
    grouped_heads = grouped_heads * row_scale[:, None]
    shrinks = lax.all_gather(shrink_bf[None], "wide", axis=0, tiled=True)
    query_sheet = lax.all_gather(query_up_weight, "wide", axis=0, tiled=True)
    key_value_sheet = lax.all_gather(key_value_up_weight, "wide", axis=0, tiled=True)
    own_rows = lax.dynamic_slice_in_dim(shrinks, row_start, local_rows, 1)
    query_change = jnp.einsum(
        "nbr,nrc->bc", own_rows[:, :, :rank_width], query_sheet, preferred_element_type=jnp.float32
    )
    key_change = jnp.einsum(
        "nbr,nrc->bc",
        own_rows[:, :, rank_width : 2 * rank_width],
        key_value_sheet[:, 0],
        preferred_element_type=jnp.float32,
    )
    value_change = jnp.einsum(
        "nbr,nrc->bc",
        own_rows[:, :, 2 * rank_width :],
        key_value_sheet[:, 1],
        preferred_element_type=jnp.float32,
    )
    adapter_change = arrange(query_change, key_change, value_change, local_key_value)
    merged_output = (grouped_heads + adapter_scale * adapter_change).reshape(
        local_rows, local_key_value, -1
    )
    width = merged_output.shape[2] - 2 * head_dim
    heads_per = width // head_dim
    query_vector = rotate(
        merged_output[:, :, :width].reshape(local_rows, local_key_value, heads_per, head_dim),
        lengths,
    ).astype(jnp.bfloat16)
    fresh_key = rotate(merged_output[:, :, width : width + head_dim], lengths).astype(jnp.bfloat16)
    value_new = merged_output[:, :, width + head_dim :].astype(jnp.bfloat16)
    inverse_root = jnp.sqrt(jnp.float32(head_dim))
    scores = (
        jnp.einsum("rkgd,rkld->rkgl", query_vector, key_cache, preferred_element_type=jnp.float32)
        / inverse_root
    )
    valid = jnp.arange(key_cache.shape[2], dtype=jnp.int32)[None, :] < lengths[:, None]
    scores = jnp.where(valid[:, None, None, :], scores, -jnp.inf)
    fresh_score = (
        jnp.einsum("rkgd,rkd->rkg", query_vector, fresh_key, preferred_element_type=jnp.float32)
        / inverse_root
    )
    top = jnp.maximum(jnp.max(scores, axis=-1), fresh_score)
    expd = jnp.exp(scores - top[..., None])
    exp_new = jnp.exp(fresh_score - top)
    total = jnp.sum(expd, axis=-1) + exp_new
    probs = (expd / total[..., None]).astype(jnp.bfloat16)
    prob_new = (exp_new / total).astype(jnp.bfloat16)
    attention_output = jnp.einsum(
        "rkgl,rkld->rkgd", probs, value_cache, preferred_element_type=jnp.float32
    )
    attention_output = (
        attention_output
        + prob_new.astype(jnp.float32)[..., None] * value_new.astype(jnp.float32)[:, :, None, :]
    )
    attention_output = attention_output.astype(jnp.bfloat16).reshape(local_rows, -1)
    out_cols = output_weight.shape[1]
    slice_portion = lax.all_gather(attention_output, "wide", axis=0, tiled=True)
    mixed = jnp.concatenate(
        [
            jnp.dot(slice_portion, output_weight, preferred_element_type=jnp.float32),
            jnp.dot(slice_portion, output_down_weight[0], preferred_element_type=jnp.float32),
        ],
        axis=1,
    )
    output_baseline = lax.psum_scatter(
        mixed[:, :out_cols].astype(jnp.bfloat16), "kv", scatter_dimension=0, tiled=True
    ).astype(jnp.float32)
    output_reduced = lax.psum(mixed[:, out_cols:], "kv")
    block = output_baseline.shape[0]
    own_shrink = lax.dynamic_slice_in_dim(
        output_reduced * mine[:, None], kv_pos * block, block, 0
    ).astype(jnp.bfloat16)
    weight_sheet = output_up_weight[0]
    output_change = lax.psum_scatter(
        jnp.dot(weight_sheet.T, own_shrink.T, preferred_element_type=jnp.float32),
        "wide",
        scatter_dimension=0,
        tiled=True,
    )
    return (output_baseline + adapter_scale * output_change.T).astype(jnp.bfloat16)


def staged_path(
    hidden_input,
    input_norm_gain,
    joint_projection_weight,
    output_weight,
    key_cache,
    value_cache,
    joint_down_weight,
    query_up_weight,
    key_value_up_weight,
    output_down_weight,
    output_up_weight,
    row_adapter_index,
    adapter_owner_slot,
    lengths,
):
    f32, bf16 = jnp.float32, jnp.bfloat16
    batch = hidden_input.shape[0]
    rows = lengths.shape[0]
    heads = key_cache.shape[1]
    head_dim = key_cache.shape[3]
    rank = query_up_weight.shape[1]
    cols = joint_projection_weight.shape[1]
    out_cols = output_weight.shape[1]
    blocks = cols // head_dim
    group = 2 * blocks - 2
    wide = batch // rows
    kv_pos = lax.axis_index("kv")
    wide_pos = lax.axis_index("wide")
    core = wide_pos & 1
    y = (wide_pos >> 1) & 1
    z = wide_pos >> 2
    right = (z >> 1) == kv_pos

    def is_right(i):
        return ((i % wide) >> 3) == i // wide

    def swap(x, mask, source=None, target=None):
        pairs = [(i, i ^ mask) for i in range(2 * wide)]
        if source is not None:
            pairs = [p for p in pairs if is_right(p[0]) == source]
        if target is not None:
            pairs = [p for p in pairs if is_right(p[1]) == target]
        return lax.ppermute(x, ("kv", "wide"), pairs)

    def pick(x, i, axis=0):
        return lax.dynamic_index_in_dim(x, i, axis, keepdims=False)

    table = row_adapter_index[:, None] == jnp.arange(wide, dtype=jnp.int32)[None, :]
    slot = jnp.sum(jnp.where(table, adapter_owner_slot[None, :], 0), axis=1)

    def reorder(x):
        rest = x.shape[1:]
        x = x.reshape((4, 2, 2 * rows) + rest)
        return jnp.swapaxes(x, 0, 1).reshape((batch,) + rest)

    slot_r = reorder(slot)
    mine_r = (slot_r == wide_pos).astype(f32)
    mine = (slot == wide_pos).astype(f32)

    sheet = jnp.concatenate(
        [
            query_up_weight[0].reshape(rank, heads, -1),
            key_value_up_weight[0, 0].reshape(rank, heads, -1),
            key_value_up_weight[0, 1].reshape(rank, heads, -1),
        ],
        axis=2,
    )
    sheet = sheet.reshape(rank, 2, 2, 2, cols).transpose(3, 1, 2, 0, 4)
    pair = jnp.concatenate([pick(sheet, core), swap(pick(sheet, 1 - core), 1)], axis=2)
    same, flip = pick(pair, z & 1), pick(pair, 1 - (z & 1))
    ups = jnp.stack(
        [same, swap(flip, 4, target=True), swap(same, 8, target=True), swap(flip, 12, target=True)]
    )
    ups_y = swap(ups, 2, target=True)
    up_of = [
        jnp.concatenate([ups[:, b].reshape(-1, cols), ups_y[:, b].reshape(-1, cols)], axis=0)
        for b in range(2)
    ]
    lane = jnp.arange(wide, dtype=jnp.int32)
    owner = wide_pos ^ (((lane >> 1) & 3) * 4 + (lane >> 3) * 2 + (lane & 1))

    def spread(values, slots):
        hit = slots[:, None] == owner[None, :]
        return jnp.where(hit[:, :, None], values[:, None, :], 0).reshape(values.shape[0], -1)

    widened = hidden_input.astype(f32)
    gained = reorder((widened * input_norm_gain[None, :]).astype(bf16))
    square = reorder(jnp.sum(widened * widened, axis=1))
    reduced = jnp.dot(gained, joint_down_weight[0], preferred_element_type=f32)
    small = jnp.concatenate([reduced, square[:, None]], axis=1) * mine_r[:, None]

    def sum_all(v):
        v = v + swap(v, 1)
        v = (v + swap(v, 4)) + (swap(v, 8) + swap(v, 12))
        return (v + swap(v, 2)) + (swap(v, 16) + swap(v, 18))

    small = sum_all(small)
    scale = lax.rsqrt(small[:, 3 * rank] / MODEL_WIDTH + 1e-05)
    shrink = (small[:, : 3 * rank] * scale[:, None]).astype(bf16)

    half = batch // 2
    partial = jnp.dot(gained, joint_projection_weight, preferred_element_type=f32).astype(bf16)
    keep = lax.dynamic_slice_in_dim(partial, y * half, half)
    give = lax.dynamic_slice_in_dim(partial, (1 - y) * half, half)
    from_x = swap(keep, 16, target=True)
    from_xy = swap(give, 18, target=True)
    from_y = swap(give, 2, target=True)
    scale_h = lax.dynamic_slice_in_dim(scale, y * half, half)[:, None]
    shrink_h = lax.dynamic_slice_in_dim(shrink, y * half, half)
    slot_h = lax.dynamic_slice_in_dim(slot_r, y * half, half)
    spread_of = [spread(shrink_h[:, t * rank : (t + 1) * rank], slot_h) for t in range(3)]
    last = core == 1

    def delta(b):
        sheet_b = pick(jnp.stack(up_of), b)
        cut = cols - 2 * head_dim
        q_part = jnp.dot(spread_of[0], sheet_b[:, :cut], preferred_element_type=f32)
        k_lhs = jnp.where(last, spread_of[1], spread_of[0])
        v_lhs = jnp.where(last, spread_of[2], spread_of[0])
        k_part = jnp.dot(k_lhs, sheet_b[:, cut : cut + head_dim], preferred_element_type=f32)
        v_part = jnp.dot(v_lhs, sheet_b[:, cut + head_dim :], preferred_element_type=f32)
        return jnp.concatenate([q_part, k_part, v_part], axis=1)

    own = (keep.astype(f32) + from_x.astype(f32)) * scale_h + adapter_scale * delta(y)
    other = (from_y.astype(f32) + from_xy.astype(f32)) * scale_h + adapter_scale * delta(1 - y)
    first = jnp.where(y == 0, own, other)
    second = jnp.where(y == 0, other, own)
    merged = jnp.stack([first, second]).astype(bf16)
    merged = merged.reshape(2, 4, 2 * rows, blocks, head_dim).transpose(1, 0, 3, 2, 4)
    to = [pick(merged, z ^ d) for d in range(4)]
    from_1 = swap(to[1], 4, source=True)
    from_2 = swap(to[2], 8, source=True)
    from_3 = swap(to[3], 12, source=True)
    near = jnp.stack([jnp.where(right, to[0], from_2), jnp.where(right, from_1, from_3)])
    far = swap(near, 1)
    parts = [jnp.where(core == 0, near, far), jnp.where(core == 0, far, near)]
    parts = [
        lax.dynamic_slice_in_dim(jnp.where((z & 1) == 0, p, p[::-1]), core * rows, rows, 3)
        for p in parts
    ]
    joined = jnp.concatenate(parts, axis=2).astype(f32)
    joined = joined.reshape(heads, 2 * blocks, rows, head_dim).transpose(2, 0, 1, 3)
    query_vector = rotate(joined[:, :, :group], lengths).astype(bf16)
    fresh_key = rotate(joined[:, :, group], lengths).astype(bf16)
    value_new = joined[:, :, group + 1].astype(bf16)

    inverse_root = jnp.sqrt(f32(head_dim))
    scores = jnp.einsum("rkgd,rkld->rkgl", query_vector, key_cache, preferred_element_type=f32)
    scores = scores / inverse_root
    valid = jnp.arange(key_cache.shape[2], dtype=jnp.int32)[None, :] < lengths[:, None]
    scores = jnp.where(valid[:, None, None, :], scores, -jnp.inf)
    fresh_score = (
        jnp.einsum("rkgd,rkd->rkg", query_vector, fresh_key, preferred_element_type=f32)
        / inverse_root
    )
    top = jnp.maximum(jnp.max(scores, axis=-1), fresh_score)
    expd = jnp.exp(scores - top[..., None])
    exp_new = jnp.exp(fresh_score - top)
    total = jnp.sum(expd, axis=-1) + exp_new
    probs = (expd / total[..., None]).astype(bf16)
    prob_new = (exp_new / total).astype(bf16)
    attended = jnp.einsum("rkgl,rkld->rkgd", probs, value_cache, preferred_element_type=f32)
    attended = (
        attended + prob_new.astype(f32)[..., None] * value_new.astype(f32)[:, :, None, :]
    )
    attended = attended.astype(bf16).reshape(rows, -1)

    o_sheet = output_up_weight[0].reshape(rank, 4, 2, 2, out_cols).transpose(3, 1, 2, 0, 4)
    o_pair = jnp.concatenate([pick(o_sheet, core), swap(pick(o_sheet, 1 - core), 1)], axis=2)
    o_ups = jnp.stack(
        [pick(o_pair, z)] + [swap(pick(o_pair, z ^ d), 4 * d) for d in range(1, 4)]
    )
    o_near = pick(o_ups, y, 1)
    o_far = swap(pick(o_ups, 1 - y, 1), 2)
    o_up = jnp.concatenate(
        [o_near.reshape(-1, out_cols), o_far.reshape(-1, out_cols)], axis=0
    )

    piece = attended[None]
    piece = jnp.concatenate([piece, swap(piece, 4), swap(piece, 8), swap(piece, 12)], axis=0)
    piece = jnp.concatenate([piece, swap(piece, 2)], axis=0)
    piece = jnp.concatenate([piece, swap(piece, 1)], axis=0)
    rel = jnp.arange(wide, dtype=jnp.int32) ^ wide_pos
    place = (rel & 1) * 8 + ((rel >> 1) & 1) * 4 + (rel >> 2)
    everyone = jnp.take(piece, place, axis=0).reshape(batch, -1)

    o_reduced = jnp.dot(everyone, output_down_weight[0], preferred_element_type=f32)
    o_reduced = sum_all(o_reduced * mine[:, None])
    mixed = jnp.dot(everyone, output_weight, preferred_element_type=f32)
    keep_out = lax.dynamic_slice_in_dim(mixed, kv_pos * half, half)
    give_out = lax.dynamic_slice_in_dim(mixed, (1 - kv_pos) * half, half).astype(bf16)
    from_out = swap(give_out, 16)
    o_shrink = lax.dynamic_slice_in_dim(o_reduced, kv_pos * half, half).astype(bf16)
    slot_o = lax.dynamic_slice_in_dim(slot, kv_pos * half, half)
    change = jnp.dot(spread(o_shrink, slot_o), o_up, preferred_element_type=f32)
    return (keep_out + from_out.astype(f32) + adapter_scale * change).astype(bf16)


def on_device(*arrays):
    lengths, key_cache, weight = arrays[13], arrays[4], arrays[2]
    batch, rows, heads = arrays[0].shape[0], lengths.shape[0], key_cache.shape[1]
    staged = batch == 16 * rows and heads == 4 and 2 * weight.shape[1] == 18 * key_cache.shape[3]
    return (staged_path if staged else general_path)(*arrays)


def solution(mesh):
    in_specs = (
        P(None, "kv"),
        P("kv"),
        P("kv", "wide"),
        P("kv", "wide"),
        P("wide", "kv", None, None),
        P("wide", "kv", None, None),
        P("wide", "kv", None),
        P("wide", None, "kv"),
        P("wide", None, None, "kv"),
        P("wide", "kv", None),
        P("wide", None, None),
        P(),
        P(),
        P("wide"),
    )
    out_specs = P("kv", "wide")
    return jax.shard_map(
        on_device, mesh=mesh, in_specs=in_specs, out_specs=out_specs, check_vma=False
    )
```

```python
import jax
import jax.numpy as jnp
from jax import lax
from jax.experimental import pallas as pl
from jax.experimental.pallas import tpu as pltpu
from jax.sharding import PartitionSpec as P

MODEL_WIDTH = 16384


rope_base = 500000.0
adapter_scale = 2.0


def rotate(values, positions):
    half = values.shape[-1] // 2
    freq = rope_base ** (-jnp.arange(half, dtype=jnp.float32) * 2.0 / values.shape[-1])
    angle = positions.astype(jnp.float32)[:, None] * freq[None, :]
    array_shape = (angle.shape[0],) + (1,) * (values.ndim - 2) + (half,)
    cosine = jnp.cos(angle).reshape(array_shape)
    sine = jnp.sin(angle).reshape(array_shape)
    first = values[..., :half]
    second = values[..., half:]
    return jnp.concatenate(
        [first * cosine - second * sine, second * cosine + first * sine], axis=-1
    )


def arrange(query_change, key_change, value_change, local_key_value):
    count = query_change.shape[0]
    joined = jnp.concatenate(
        [
            query_change.reshape(count, local_key_value, -1),
            key_change.reshape(count, local_key_value, -1),
            value_change.reshape(count, local_key_value, -1),
        ],
        axis=2,
    )
    return joined.reshape(count, -1)


def general_path(
    hidden_input,
    input_norm_gain,
    joint_projection_weight,
    output_weight,
    key_cache,
    value_cache,
    joint_down_weight,
    query_up_weight,
    key_value_up_weight,
    output_down_weight,
    output_up_weight,
    row_adapter_index,
    adapter_owner_slot,
    lengths,
):
    local_rows = lengths.shape[0]
    local_key_value = key_cache.shape[1]
    head_dim = key_cache.shape[3]
    rank_width = query_up_weight.shape[1]
    wide_pos = lax.axis_index("wide")
    kv_pos = lax.axis_index("kv")
    row_start = wide_pos * local_rows
    table = (
        row_adapter_index[:, None]
        == jnp.arange(adapter_owner_slot.shape[0], dtype=jnp.int32)[None, :]
    )
    row_slot = jnp.sum(jnp.where(table, adapter_owner_slot[None, :], 0), axis=1)
    mine = (row_slot == wide_pos).astype(jnp.float32)
    widened = hidden_input.astype(jnp.float32)
    scaled_hidden = (widened * input_norm_gain[None, :]).astype(jnp.bfloat16)
    partial_sq = jnp.sum(widened * widened, axis=1)
    partial_reduced = jnp.dot(
        scaled_hidden, joint_down_weight[0], preferred_element_type=jnp.float32
    )
    total_sq, reduced_hidden = lax.psum((partial_sq, partial_reduced), "kv")
    scale = lax.rsqrt(total_sq / MODEL_WIDTH + 1e-05)
    shrink_bf = (reduced_hidden * scale[:, None] * mine[:, None]).astype(jnp.bfloat16)
    base_part = jnp.dot(scaled_hidden, joint_projection_weight, preferred_element_type=jnp.float32)
    regrouped = lax.all_to_all(base_part, "wide", split_axis=0, concat_axis=1, tiled=True)
    grouped_heads = lax.psum_scatter(regrouped, "kv", scatter_dimension=1, tiled=True)
    row_scale = lax.dynamic_slice_in_dim(scale, row_start, local_rows)
    grouped_heads = grouped_heads * row_scale[:, None]
    shrinks = lax.all_gather(shrink_bf[None], "wide", axis=0, tiled=True)
    query_sheet = lax.all_gather(query_up_weight, "wide", axis=0, tiled=True)
    key_value_sheet = lax.all_gather(key_value_up_weight, "wide", axis=0, tiled=True)
    own_rows = lax.dynamic_slice_in_dim(shrinks, row_start, local_rows, 1)
    query_change = jnp.einsum(
        "nbr,nrc->bc", own_rows[:, :, :rank_width], query_sheet, preferred_element_type=jnp.float32
    )
    key_change = jnp.einsum(
        "nbr,nrc->bc",
        own_rows[:, :, rank_width : 2 * rank_width],
        key_value_sheet[:, 0],
        preferred_element_type=jnp.float32,
    )
    value_change = jnp.einsum(
        "nbr,nrc->bc",
        own_rows[:, :, 2 * rank_width :],
        key_value_sheet[:, 1],
        preferred_element_type=jnp.float32,
    )
    adapter_change = arrange(query_change, key_change, value_change, local_key_value)
    merged_output = (grouped_heads + adapter_scale * adapter_change).reshape(
        local_rows, local_key_value, -1
    )
    width = merged_output.shape[2] - 2 * head_dim
    heads_per = width // head_dim
    query_vector = rotate(
        merged_output[:, :, :width].reshape(local_rows, local_key_value, heads_per, head_dim),
        lengths,
    ).astype(jnp.bfloat16)
    fresh_key = rotate(merged_output[:, :, width : width + head_dim], lengths).astype(jnp.bfloat16)
    value_new = merged_output[:, :, width + head_dim :].astype(jnp.bfloat16)
    inverse_root = jnp.sqrt(jnp.float32(head_dim))
    scores = (
        jnp.einsum("rkgd,rkld->rkgl", query_vector, key_cache, preferred_element_type=jnp.float32)
        / inverse_root
    )
    valid = jnp.arange(key_cache.shape[2], dtype=jnp.int32)[None, :] < lengths[:, None]
    scores = jnp.where(valid[:, None, None, :], scores, -jnp.inf)
    fresh_score = (
        jnp.einsum("rkgd,rkd->rkg", query_vector, fresh_key, preferred_element_type=jnp.float32)
        / inverse_root
    )
    top = jnp.maximum(jnp.max(scores, axis=-1), fresh_score)
    expd = jnp.exp(scores - top[..., None])
    exp_new = jnp.exp(fresh_score - top)
    total = jnp.sum(expd, axis=-1) + exp_new
    probs = (expd / total[..., None]).astype(jnp.bfloat16)
    prob_new = (exp_new / total).astype(jnp.bfloat16)
    attention_output = jnp.einsum(
        "rkgl,rkld->rkgd", probs, value_cache, preferred_element_type=jnp.float32
    )
    attention_output = (
        attention_output
        + prob_new.astype(jnp.float32)[..., None] * value_new.astype(jnp.float32)[:, :, None, :]
    )
    attention_output = attention_output.astype(jnp.bfloat16).reshape(local_rows, -1)
    out_cols = output_weight.shape[1]
    slice_portion = lax.all_gather(attention_output, "wide", axis=0, tiled=True)
    mixed = jnp.concatenate(
        [
            jnp.dot(slice_portion, output_weight, preferred_element_type=jnp.float32),
            jnp.dot(slice_portion, output_down_weight[0], preferred_element_type=jnp.float32),
        ],
        axis=1,
    )
    output_baseline = lax.psum_scatter(
        mixed[:, :out_cols].astype(jnp.bfloat16), "kv", scatter_dimension=0, tiled=True
    ).astype(jnp.float32)
    output_reduced = lax.psum(mixed[:, out_cols:], "kv")
    block = output_baseline.shape[0]
    own_shrink = lax.dynamic_slice_in_dim(
        output_reduced * mine[:, None], kv_pos * block, block, 0
    ).astype(jnp.bfloat16)
    weight_sheet = output_up_weight[0]
    output_change = lax.psum_scatter(
        jnp.dot(weight_sheet.T, own_shrink.T, preferred_element_type=jnp.float32),
        "wide",
        scatter_dimension=0,
        tiled=True,
    )
    return (output_baseline + adapter_scale * output_change.T).astype(jnp.bfloat16)


WHOLE = pl.BlockSpec(memory_space=pltpu.VMEM)
SCALARS = pl.BlockSpec(memory_space=pltpu.SMEM)


def prepare(place, hidden_input, gain, owned, swapped, adapters, owners, cols):
    count, width = hidden_input.shape
    entries = owned[0].shape[0]
    rank, heads_width = owned[1].shape
    head_dim = 128
    lanes = 128
    heads = owned[2].shape[2] // head_dim
    group_width = heads_width // heads
    each = count // 3
    chunk = 1024
    held = (hidden_input, gain, *owned, *swapped)

    def kernel(place_ref, owner_ref, index_ref, *refs):
        inputs, outputs = refs[: len(held)], refs[len(held) : len(held) + 5]
        buffers, sem = refs[len(held) + 5 : -1], refs[-1]
        same_ref, flip_ref, small_ref, slot_ref, mine_ref = outputs
        copies = [
            pltpu.make_async_copy(src, dst, sem.at[i])
            for i, (src, dst) in enumerate(zip(inputs, buffers))
        ]
        for copy in copies:
            copy.start()
        x_ref, gain_ref = buffers[:2]
        down_refs, q_refs, kv_refs = buffers[2::3], buffers[3::3], buffers[4::3]

        row = lax.broadcasted_iota(jnp.int32, (count, count), 0)
        column = lax.broadcasted_iota(jnp.int32, (count, count), 1)
        across = jnp.where(row == column, index_ref[...].astype(jnp.float32), 0.0)
        index = jnp.sum(across, axis=1, keepdims=True).astype(jnp.int32)
        slot = jnp.zeros((count, 1), jnp.int32)
        for a in range(owners.shape[0]):
            slot = jnp.where(index == a, owner_ref[a], slot)
        slot_ref[...] = slot
        mine = [(slot == (place_ref[1] ^ dcore)).astype(jnp.float32) for dcore in range(2)]
        for dcore in range(2):
            mine_ref[:, dcore : dcore + 1] = mine[dcore]

        for copy in copies:
            copy.wait()
        total = jnp.zeros((count, 1), jnp.float32)
        reduced = [jnp.zeros((count, entries), jnp.float32) for _ in range(2)]
        for at in range(0, width, chunk):
            part = slice(at, at + chunk)
            x = x_ref[:, part].astype(jnp.float32)
            total = total + jnp.sum(x * x, axis=1, keepdims=True)
            gained = (x * gain_ref[:, part]).astype(jnp.bfloat16)
            for dcore in range(2):
                reduced[dcore] = reduced[dcore] + lax.dot_general(
                    gained, down_refs[dcore][:, part], (((1,), (1,)), ((), ())),
                    preferred_element_type=jnp.float32,
                )
        small_ref[...] = jnp.zeros_like(small_ref)
        small_ref[:, :entries] = reduced[0] * mine[0] + reduced[1] * mine[1]
        small_ref[:, entries : entries + 1] = total * (mine[0] + mine[1])
        small = small_ref[...]

        for ref in (same_ref, flip_ref):
            ref[:, cols:] = jnp.zeros((4 * rank, 3 * lanes), ref.dtype)
            for g in range(3):
                code_three(ref, slice(0, each), cols + g * lanes, small[g * each : (g + 1) * each])

        def write(core, zb, ref):
            for yb in range(2):
                h = zb * 2 + yb
                rows = slice(yb * 2 * rank, (yb + 1) * 2 * rank)
                at = h * group_width
                spans = [(at, at + cols), (at + cols, at + group_width)][core]
                joined = jnp.concatenate([q[:, spans[0] : spans[1]] for q in q_refs], axis=0)
                rest = spans[1] - spans[0]
                ref[rows, :rest] = joined
                if core == 1:
                    for t in range(2):
                        part = slice(h * head_dim, (h + 1) * head_dim)
                        ref[rows, rest + t * head_dim : rest + (t + 1) * head_dim] = (
                            jnp.concatenate([kv[t, :, part] for kv in kv_refs], axis=0)
                        )

        for core in range(2):
            for low in range(2):

                @pl.when((place_ref[0] == core) & ((place_ref[2] & 1) == low))
                def _():
                    write(core, low, same_ref)
                    write(core, 1 - low, flip_ref)

    message = jax.ShapeDtypeStruct((4 * rank, cols + 3 * lanes), owned[1].dtype)
    return pl.pallas_call(
        kernel,
        in_specs=[SCALARS, SCALARS, WHOLE] + [pl.BlockSpec(memory_space=pl.ANY)] * len(held),
        out_specs=[WHOLE] * 5,
        out_shape=[
            message,
            message,
            jax.ShapeDtypeStruct((count, 32), jnp.float32),
            jax.ShapeDtypeStruct((count, 1), jnp.int32),
            jax.ShapeDtypeStruct((count, 2), jnp.float32),
        ],
        scratch_shapes=[pltpu.VMEM(v.shape, v.dtype) for v in held]
        + [pltpu.SemaphoreType.DMA((len(held),))],
        compiler_params=pltpu.CompilerParams(vmem_limit_bytes=60 * 2**20),
    )(place, owners, adapters, *held)


def stream_product(rows_in, gain, weight, start, stop, before, marker):
    count, cols = rows_in.shape[0], weight.shape[1]
    chunk = 512
    steps = (stop - start) // chunk
    held = pl.BlockSpec(memory_space=pl.ANY)
    operands, specs = [rows_in, weight, marker], [WHOLE, held, held]
    for more in (gain, before):
        if more is not None:
            operands += [more]
            specs += [WHOLE]

    def kernel(*refs):
        x_ref, w_ref = refs[:2]
        out_ref, buf, sem = refs[-3:]

        def fetch(i):
            return pltpu.make_async_copy(
                w_ref.at[pl.ds(start + i * chunk, chunk)], buf.at[i], sem.at[i]
            )

        for i in range(steps):
            fetch(i).start()
        if before is None:
            out_ref[...] = jnp.zeros_like(out_ref)
        else:
            out_ref[...] = refs[len(operands) - 1][...]

        def body(i, carry):
            at = pl.multiple_of(start + i * chunk, chunk)
            x = x_ref[:, pl.ds(at, chunk)]
            if gain is not None:
                x = (x.astype(jnp.float32) * refs[3][:, pl.ds(at, chunk)]).astype(jnp.bfloat16)
            fetch(i).wait()
            out_ref[...] += jnp.dot(x, buf[i], preferred_element_type=jnp.float32)
            return carry

        lax.fori_loop(0, steps, body, 0)

    return pl.pallas_call(
        kernel,
        in_specs=specs,
        out_specs=WHOLE,
        out_shape=jax.ShapeDtypeStruct((count, cols), jnp.float32),
        scratch_shapes=[
            pltpu.VMEM((steps, chunk, cols), weight.dtype),
            pltpu.SemaphoreType.DMA((steps,)),
        ],
        cost_estimate=pl.CostEstimate(
            flops=2 * count * cols * (stop - start),
            bytes_accessed=2 * cols * (stop - start),
            transcendentals=0,
        ),
        compiler_params=pltpu.CompilerParams(vmem_limit_bytes=47 * 2**20),
    )(*operands)


def code_three(ref, rows, at, v):
    width = v.shape[1]
    for t in range(3):
        top = v.astype(jnp.bfloat16)
        ref[rows, at + t * width : at + (t + 1) * width] = top
        v = v - top.astype(jnp.float32)


def pack_y(place, parts, small, cols):
    tall, wide_cols = parts[0].shape
    count, entries = small.shape
    lanes = 128
    each = count // 3
    rows = tall // 2

    def kernel(place_ref, a_ref, b_ref, c_ref, d_ref, small_ref, away_ref, keep_ref, sum_ref):
        total = small_ref[...]
        for ref in (b_ref, c_ref, d_ref):
            coded = jnp.concatenate(
                [
                    ref[:each, cols + g * lanes : cols + g * lanes + 3 * entries]
                    for g in range(3)
                ],
                axis=0,
            ).astype(jnp.float32)
            total = total + (
                (coded[:, :entries] + coded[:, entries : 2 * entries]) + coded[:, 2 * entries :]
            )
        sum_ref[...] = total

        def write(yb):
            for dz, ref in enumerate((a_ref, b_ref, c_ref, d_ref)):
                keep_ref[dz] = ref[yb * rows : (yb + 1) * rows, :cols]
                away_ref[dz * rows : (dz + 1) * rows, :cols] = ref[
                    (1 - yb) * rows : (2 - yb) * rows, :cols
                ]

        @pl.when(place_ref[3] == 0)
        def _():
            write(0)

        @pl.when(place_ref[3] == 1)
        def _():
            write(1)

        away_ref[:, cols:] = jnp.zeros_like(away_ref[:, cols:])
        code_three(away_ref, slice(0, count), cols, total)

    dtype = parts[0].dtype
    return pl.pallas_call(
        kernel,
        in_specs=[SCALARS] + [WHOLE] * 5,
        out_specs=[WHOLE] * 3,
        out_shape=[
            jax.ShapeDtypeStruct((4 * rows, cols + lanes), dtype),
            jax.ShapeDtypeStruct((4, rows, cols), dtype),
            jax.ShapeDtypeStruct(small.shape, jnp.float32),
        ],
        compiler_params=pltpu.CompilerParams(vmem_limit_bytes=8 * 2**20),
    )(place, *parts, small)


def merge(place, partial, small, received, near, far, slot):
    count, cols = partial.shape
    lanes = 128
    blocks = cols // lanes
    each = count // 4
    entries = 24
    rank = entries // 3

    def kernel(place_ref, p_ref, small_ref, r_ref, near_ref, far_ref, slot_ref, out_ref, acc_ref):
        other = r_ref[:, cols : cols + 96].astype(jnp.float32)
        small = small_ref[...] + ((other[:, :32] + other[:, 32:64]) + other[:, 64:96])
        scale = lax.rsqrt(small[:, entries : entries + 1] / MODEL_WIDTH + 1e-05)
        shrink = (small * scale).astype(jnp.bfloat16)
        lane = lax.broadcasted_iota(jnp.int32, (count, lanes), 1)
        owner = place_ref[1] ^ (((lane >> 4) & 3) * 4 + (lane >> 6) * 2 + ((lane >> 3) & 1))
        hit = slot_ref[...] == owner
        entry = lax.broadcasted_iota(jnp.int32, (32, lanes), 0)
        to = lax.broadcasted_iota(jnp.int32, (32, lanes), 1) & (rank - 1)

        def spread(t):
            chosen = (entry == to + t * rank).astype(jnp.bfloat16)
            value = jnp.dot(shrink, chosen, preferred_element_type=jnp.float32)
            return jnp.where(hit, value, 0.0).astype(jnp.bfloat16)

        last = place_ref[0] == 1
        parts = [spread(t) for t in range(3)]
        cut = cols - 2 * lanes
        spans = ((0, cut, parts[0]), (cut, cut + lanes, parts[1]), (cut + lanes, cols, parts[2]))
        for lo, hi, own in spans:
            left = parts[0] if lo == 0 else jnp.where(last, own, parts[0])
            up = jnp.concatenate(
                [near_ref[dz, :, lo:hi] for dz in range(4)] + [far_ref[:, lo:hi]], axis=0
            )
            change = jnp.dot(left, up, preferred_element_type=jnp.float32)
            base = p_ref[:, lo:hi] + r_ref[:, lo:hi].astype(jnp.float32)
            acc_ref[:, lo:hi] = base * scale + adapter_scale * change
        for a in range(4):
            for b in range(blocks):
                out_ref[a, b] = acc_ref[
                    a * each : (a + 1) * each, b * lanes : (b + 1) * lanes
                ].astype(out_ref.dtype)

    return pl.pallas_call(
        kernel,
        in_specs=[SCALARS] + [WHOLE] * 6,
        out_specs=WHOLE,
        out_shape=jax.ShapeDtypeStruct((4, blocks, each, lanes), jnp.bfloat16),
        scratch_shapes=[pltpu.VMEM((count, cols), jnp.float32)],
        compiler_params=pltpu.CompilerParams(vmem_limit_bytes=12 * 2**20),
    )(place, partial, small, received, near, far, slot)


def in_order(groups, order, downs, mine):
    pieces, tall, lanes = groups[0].shape
    entries, depth = downs[0].shape
    blocks = depth // lanes
    count = 4 * pieces * (tall // blocks)

    def kernel(
        order_ref, a_ref, b_ref, c_ref, d_ref, near_ref, far_ref, mine_ref, rows_ref, small_ref,
        wide_ref,
    ):
        for g, ref in enumerate((a_ref, b_ref, c_ref, d_ref)):
            for p in range(pieces):
                wide_ref[order_ref[g * pieces + p]] = ref[p].astype(jnp.float32)
        flat = wide_ref.reshape(count * blocks, lanes)
        for j in range(blocks):
            rows_ref[:, j * lanes : (j + 1) * lanes] = flat[
                pl.ds(j, count, stride=blocks), :
            ].astype(rows_ref.dtype)
        near, far = [
            lax.dot_general(
                rows_ref[...], ref[...], (((1,), (1,)), ((), ())),
                preferred_element_type=jnp.float32,
            )
            for ref in (near_ref, far_ref)
        ]
        small_ref[...] = near * mine_ref[:, :1] + far * mine_ref[:, 1:]

    return pl.pallas_call(
        kernel,
        in_specs=[SCALARS] + [WHOLE] * 7,
        out_specs=[WHOLE, WHOLE],
        out_shape=[
            jax.ShapeDtypeStruct((count, depth), groups[0].dtype),
            jax.ShapeDtypeStruct((count, entries), jnp.float32),
        ],
        scratch_shapes=[pltpu.VMEM((4 * pieces, tall, lanes), jnp.float32)],
        cost_estimate=pl.CostEstimate(
            flops=0, bytes_accessed=4 * count * depth, transcendentals=0
        ),
        compiler_params=pltpu.CompilerParams(vmem_limit_bytes=10 * 2**20),
    )(order, *groups, *downs, mine)


def in_three(v):
    out = []
    for _ in range(3):
        top = lax.reduce_precision(v, 8, 7)
        out.append(top.astype(jnp.bfloat16))
        v = v - top
    return jnp.concatenate(out, axis=1)


def from_three(v):
    n = v.shape[1] // 3
    v = v.astype(jnp.float32)
    return (v[:, :n] + v[:, n : 2 * n]) + v[:, 2 * n :]


def staged_path(
    hidden_input,
    input_norm_gain,
    joint_projection_weight,
    output_weight,
    key_cache,
    value_cache,
    joint_down_weight,
    query_up_weight,
    key_value_up_weight,
    output_down_weight,
    output_up_weight,
    row_adapter_index,
    adapter_owner_slot,
    lengths,
):
    f32, bf16 = jnp.float32, jnp.bfloat16
    batch = hidden_input.shape[0]
    rows = lengths.shape[0]
    heads = key_cache.shape[1]
    head_dim = key_cache.shape[3]
    rank = query_up_weight.shape[1]
    cols = joint_projection_weight.shape[1]
    out_cols = output_weight.shape[1]
    blocks = cols // head_dim
    group = 2 * blocks - 2
    wide = batch // rows
    kv_pos = lax.axis_index("kv")
    wide_pos = lax.axis_index("wide")
    core = wide_pos & 1
    y = (wide_pos >> 1) & 1
    z = wide_pos >> 2
    right = (z >> 1) == kv_pos

    def is_right(i):
        return ((i % wide) >> 3) == i // wide

    def swap(x, mask, source=None, target=None):
        pairs = [(i, i ^ mask) for i in range(2 * wide)]
        if source is not None:
            pairs = [p for p in pairs if is_right(p[0]) == source]
        if target is not None:
            pairs = [p for p in pairs if is_right(p[1]) == target]
        return lax.ppermute(x, ("kv", "wide"), pairs)

    def pick(x, i, axis=0):
        return lax.dynamic_index_in_dim(x, i, axis, keepdims=False)

    half = batch // 2
    place = jnp.stack([core, wide_pos, z, y])

    owned = (joint_down_weight[0].T, query_up_weight[0], key_value_up_weight[0])
    gain = input_norm_gain[None]
    same, flip, small, slot, mine = prepare(
        place,
        hidden_input,
        gain,
        owned,
        tuple(swap(v, 1) for v in owned),
        row_adapter_index[None],
        adapter_owner_slot,
        cols,
    )
    parts = [same, swap(flip, 4), swap(same, 8), swap(flip, 12)]
    depth = hidden_input.shape[1]
    cut = depth * 5 // 8
    weight = joint_projection_weight
    partial = stream_product(hidden_input, gain, weight, 0, cut, None, same)
    away, ups, small = pack_y(place, parts, small, cols)
    away, partial = lax.optimization_barrier((away, partial))
    from_y = swap(away, 2)
    partial = stream_product(hidden_input, gain, weight, cut, depth, partial, away)
    small = small + from_three(from_y[:batch, cols : cols + 96])
    message = jnp.concatenate([partial.astype(bf16), in_three(small)], axis=1)
    from_x = swap(message, 16, target=True)
    merged = merge(place, partial, small, from_x, ups, from_y, slot)

    to = [pick(merged, z ^ d) for d in range(4)]
    from_1 = swap(to[1], 4, source=True)
    from_2 = swap(to[2], 8, source=True)
    from_3 = swap(to[3], 12, source=True)
    near = jnp.stack([jnp.where(right, to[0], from_2), jnp.where(right, from_1, from_3)])
    keep = lax.dynamic_slice_in_dim(near, y * 2 * rows, 2 * rows, 2)
    give = lax.dynamic_slice_in_dim(near, (1 - y) * 2 * rows, 2 * rows, 2)
    from_y = swap(give, 2)
    near = jnp.stack([jnp.where(y == 0, keep, from_y), jnp.where(y == 0, from_y, keep)], axis=1)
    far = swap(near, 1)
    parts = [jnp.where(core == 0, near, far), jnp.where(core == 0, far, near)]
    parts = [
        lax.dynamic_slice_in_dim(jnp.where((z & 1) == 0, p, p[::-1]), core * rows, rows, 3)
        for p in parts
    ]
    joined = jnp.concatenate(parts, axis=2).astype(f32)
    joined = joined.reshape(heads, 2 * blocks, rows, head_dim).transpose(2, 0, 1, 3)
    query_vector = rotate(joined[:, :, :group], lengths).astype(bf16)
    fresh_key = rotate(joined[:, :, group], lengths).astype(bf16)
    value_new = joined[:, :, group + 1].astype(bf16)

    inverse_root = jnp.sqrt(f32(head_dim))
    scores = jnp.einsum("rkgd,rkld->rkgl", query_vector, key_cache, preferred_element_type=f32)
    scores = scores / inverse_root
    valid = jnp.arange(key_cache.shape[2], dtype=jnp.int32)[None, :] < lengths[:, None]
    scores = jnp.where(valid[:, None, None, :], scores, -jnp.inf)
    fresh_score = (
        jnp.einsum("rkgd,rkd->rkg", query_vector, fresh_key, preferred_element_type=f32)
        / inverse_root
    )
    top = jnp.maximum(jnp.max(scores, axis=-1), fresh_score)
    expd = jnp.exp(scores - top[..., None])
    exp_new = jnp.exp(fresh_score - top)
    total = jnp.sum(expd, axis=-1) + exp_new
    probs = (expd / total[..., None]).astype(bf16)
    prob_new = (exp_new / total).astype(bf16)
    attended = jnp.einsum("rkgl,rkld->rkgd", probs, value_cache, preferred_element_type=f32)
    attended = (
        attended + prob_new.astype(f32)[..., None] * value_new.astype(f32)[:, :, None, :]
    )
    attended = attended.astype(bf16).reshape(-1, head_dim)

    near = jnp.stack([attended, swap(attended, 4), swap(attended, 8), swap(attended, 12)])
    near_y = swap(near, 2)
    far, far_y = swap(near, 1), swap(near_y, 1)
    offsets = [
        dz * 4 + dy * 2 + dcore for dcore in range(2) for dy in range(2) for dz in range(4)
    ]
    order = wide_pos ^ jnp.array(offsets, jnp.int32)
    o_down = output_down_weight[0].T
    everyone, o_reduced = in_order(
        (near, near_y, far, far_y), order, (o_down, swap(o_down, 1)), mine
    )

    o_sheet = output_up_weight[0].reshape(rank, 4, 2, 2, out_cols).transpose(3, 1, 2, 0, 4)
    o_pair = jnp.concatenate([pick(o_sheet, core), swap(pick(o_sheet, 1 - core), 1)], axis=2)
    o_pair = o_pair.reshape(4, 4 * rank, out_cols)
    o_extra = 3 * batch // 4
    coded = jnp.broadcast_to(
        in_three(o_reduced).reshape(4 * rank, o_extra)[None], (4, 4 * rank, o_extra)
    )
    o_pair = jnp.concatenate([o_pair, coded], axis=2)
    from_z = [swap(pick(o_pair, z ^ d), 4 * d) for d in range(1, 4)]
    mixed = stream_product(everyone, None, output_weight, 0, cut, None, o_pair)
    sums = [from_three(v[:, out_cols:].reshape(batch, 3 * rank)) for v in from_z]
    o_reduced = (o_reduced + sums[0]) + (sums[1] + sums[2])
    o_ups = jnp.stack([pick(o_pair, z)] + from_z)[:, :, :out_cols]
    o_ups = o_ups.reshape(4, 2, 2 * rank, out_cols)
    coded = in_three(o_reduced).reshape(8 * rank, -1)
    away = pick(o_ups, 1 - y, 1).reshape(8 * rank, out_cols)
    away = jnp.concatenate([away, coded], axis=1)
    away, mixed = lax.optimization_barrier((away, mixed))
    from_y = swap(away, 2)
    mixed = stream_product(everyone, None, output_weight, cut, depth, mixed, away)
    o_reduced = o_reduced + from_three(from_y[:, out_cols:].reshape(batch, 3 * rank))

    keep_out = lax.dynamic_slice_in_dim(mixed, kv_pos * half, half)
    give_out = lax.dynamic_slice_in_dim(mixed, (1 - kv_pos) * half, half).astype(bf16)
    o_keep = lax.dynamic_slice_in_dim(o_reduced, kv_pos * half, half)
    o_give = in_three(lax.dynamic_slice_in_dim(o_reduced, (1 - kv_pos) * half, half))
    from_x = swap(jnp.concatenate([give_out, o_give], axis=1), 16)
    o_far = from_y[:, :out_cols]
    o_near = pick(o_ups, y, 1).reshape(8 * rank, out_cols)
    o_up = jnp.concatenate([o_near, o_far], axis=0)
    o_keep = o_keep + from_three(from_x[:, out_cols:])
    lane = jnp.arange(wide, dtype=jnp.int32)
    owner = wide_pos ^ (((lane >> 1) & 3) * 4 + (lane >> 3) * 2 + (lane & 1))
    slot_o = lax.dynamic_slice_in_dim(slot, kv_pos * half, half)
    hit = slot_o == owner[None, :]
    shrink = jnp.where(hit[:, :, None], o_keep.astype(bf16)[:, None, :], 0).reshape(half, -1)
    change = jnp.dot(shrink, o_up, preferred_element_type=f32)
    base = keep_out + from_x[:, :out_cols].astype(f32)
    return (base + adapter_scale * change).astype(bf16)


def on_device(*arrays):
    lengths, key_cache, weight = arrays[13], arrays[4], arrays[2]
    batch, rows, heads = arrays[0].shape[0], lengths.shape[0], key_cache.shape[1]
    staged = batch == 16 * rows and heads == 4 and 2 * weight.shape[1] == 18 * key_cache.shape[3]
    return (staged_path if staged else general_path)(*arrays)


def solution(mesh):
    in_specs = (
        P(None, "kv"),
        P("kv"),
        P("kv", "wide"),
        P("kv", "wide"),
        P("wide", "kv", None, None),
        P("wide", "kv", None, None),
        P("wide", "kv", None),
        P("wide", None, "kv"),
        P("wide", None, None, "kv"),
        P("wide", "kv", None),
        P("wide", None, None),
        P(),
        P(),
        P("wide"),
    )
    out_specs = P("kv", "wide")
    return jax.shard_map(
        on_device, mesh=mesh, in_specs=in_specs, out_specs=out_specs, check_vma=False
    )
```

```python
import jax
import jax.numpy as jnp
from jax import lax
from jax.experimental import pallas as pl
from jax.experimental.pallas import tpu as pltpu
from jax.sharding import PartitionSpec as P

MODEL_WIDTH = 16384


rope_base = 500000.0
adapter_scale = 2.0


def rotate(values, positions):
    half = values.shape[-1] // 2
    freq = rope_base ** (-jnp.arange(half, dtype=jnp.float32) * 2.0 / values.shape[-1])
    angle = positions.astype(jnp.float32)[:, None] * freq[None, :]
    array_shape = (angle.shape[0],) + (1,) * (values.ndim - 2) + (half,)
    cosine = jnp.cos(angle).reshape(array_shape)
    sine = jnp.sin(angle).reshape(array_shape)
    first = values[..., :half]
    second = values[..., half:]
    return jnp.concatenate(
        [first * cosine - second * sine, second * cosine + first * sine], axis=-1
    )


def arrange(query_change, key_change, value_change, local_key_value):
    count = query_change.shape[0]
    joined = jnp.concatenate(
        [
            query_change.reshape(count, local_key_value, -1),
            key_change.reshape(count, local_key_value, -1),
            value_change.reshape(count, local_key_value, -1),
        ],
        axis=2,
    )
    return joined.reshape(count, -1)


def general_path(
    hidden_input,
    input_norm_gain,
    joint_projection_weight,
    output_weight,
    key_cache,
    value_cache,
    joint_down_weight,
    query_up_weight,
    key_value_up_weight,
    output_down_weight,
    output_up_weight,
    row_adapter_index,
    adapter_owner_slot,
    lengths,
):
    local_rows = lengths.shape[0]
    local_key_value = key_cache.shape[1]
    head_dim = key_cache.shape[3]
    rank_width = query_up_weight.shape[1]
    wide_pos = lax.axis_index("wide")
    kv_pos = lax.axis_index("kv")
    row_start = wide_pos * local_rows
    table = (
        row_adapter_index[:, None]
        == jnp.arange(adapter_owner_slot.shape[0], dtype=jnp.int32)[None, :]
    )
    row_slot = jnp.sum(jnp.where(table, adapter_owner_slot[None, :], 0), axis=1)
    mine = (row_slot == wide_pos).astype(jnp.float32)
    widened = hidden_input.astype(jnp.float32)
    scaled_hidden = (widened * input_norm_gain[None, :]).astype(jnp.bfloat16)
    partial_sq = jnp.sum(widened * widened, axis=1)
    partial_reduced = jnp.dot(
        scaled_hidden, joint_down_weight[0], preferred_element_type=jnp.float32
    )
    total_sq, reduced_hidden = lax.psum((partial_sq, partial_reduced), "kv")
    scale = lax.rsqrt(total_sq / MODEL_WIDTH + 1e-05)
    shrink_bf = (reduced_hidden * scale[:, None] * mine[:, None]).astype(jnp.bfloat16)
    base_part = jnp.dot(scaled_hidden, joint_projection_weight, preferred_element_type=jnp.float32)
    regrouped = lax.all_to_all(base_part, "wide", split_axis=0, concat_axis=1, tiled=True)
    grouped_heads = lax.psum_scatter(regrouped, "kv", scatter_dimension=1, tiled=True)
    row_scale = lax.dynamic_slice_in_dim(scale, row_start, local_rows)
    grouped_heads = grouped_heads * row_scale[:, None]
    shrinks = lax.all_gather(shrink_bf[None], "wide", axis=0, tiled=True)
    query_sheet = lax.all_gather(query_up_weight, "wide", axis=0, tiled=True)
    key_value_sheet = lax.all_gather(key_value_up_weight, "wide", axis=0, tiled=True)
    own_rows = lax.dynamic_slice_in_dim(shrinks, row_start, local_rows, 1)
    query_change = jnp.einsum(
        "nbr,nrc->bc", own_rows[:, :, :rank_width], query_sheet, preferred_element_type=jnp.float32
    )
    key_change = jnp.einsum(
        "nbr,nrc->bc",
        own_rows[:, :, rank_width : 2 * rank_width],
        key_value_sheet[:, 0],
        preferred_element_type=jnp.float32,
    )
    value_change = jnp.einsum(
        "nbr,nrc->bc",
        own_rows[:, :, 2 * rank_width :],
        key_value_sheet[:, 1],
        preferred_element_type=jnp.float32,
    )
    adapter_change = arrange(query_change, key_change, value_change, local_key_value)
    merged_output = (grouped_heads + adapter_scale * adapter_change).reshape(
        local_rows, local_key_value, -1
    )
    width = merged_output.shape[2] - 2 * head_dim
    heads_per = width // head_dim
    query_vector = rotate(
        merged_output[:, :, :width].reshape(local_rows, local_key_value, heads_per, head_dim),
        lengths,
    ).astype(jnp.bfloat16)
    fresh_key = rotate(merged_output[:, :, width : width + head_dim], lengths).astype(jnp.bfloat16)
    value_new = merged_output[:, :, width + head_dim :].astype(jnp.bfloat16)
    inverse_root = jnp.sqrt(jnp.float32(head_dim))
    scores = (
        jnp.einsum("rkgd,rkld->rkgl", query_vector, key_cache, preferred_element_type=jnp.float32)
        / inverse_root
    )
    valid = jnp.arange(key_cache.shape[2], dtype=jnp.int32)[None, :] < lengths[:, None]
    scores = jnp.where(valid[:, None, None, :], scores, -jnp.inf)
    fresh_score = (
        jnp.einsum("rkgd,rkd->rkg", query_vector, fresh_key, preferred_element_type=jnp.float32)
        / inverse_root
    )
    top = jnp.maximum(jnp.max(scores, axis=-1), fresh_score)
    expd = jnp.exp(scores - top[..., None])
    exp_new = jnp.exp(fresh_score - top)
    total = jnp.sum(expd, axis=-1) + exp_new
    probs = (expd / total[..., None]).astype(jnp.bfloat16)
    prob_new = (exp_new / total).astype(jnp.bfloat16)
    attention_output = jnp.einsum(
        "rkgl,rkld->rkgd", probs, value_cache, preferred_element_type=jnp.float32
    )
    attention_output = (
        attention_output
        + prob_new.astype(jnp.float32)[..., None] * value_new.astype(jnp.float32)[:, :, None, :]
    )
    attention_output = attention_output.astype(jnp.bfloat16).reshape(local_rows, -1)
    out_cols = output_weight.shape[1]
    slice_portion = lax.all_gather(attention_output, "wide", axis=0, tiled=True)
    mixed = jnp.concatenate(
        [
            jnp.dot(slice_portion, output_weight, preferred_element_type=jnp.float32),
            jnp.dot(slice_portion, output_down_weight[0], preferred_element_type=jnp.float32),
        ],
        axis=1,
    )
    output_baseline = lax.psum_scatter(
        mixed[:, :out_cols].astype(jnp.bfloat16), "kv", scatter_dimension=0, tiled=True
    ).astype(jnp.float32)
    output_reduced = lax.psum(mixed[:, out_cols:], "kv")
    block = output_baseline.shape[0]
    own_shrink = lax.dynamic_slice_in_dim(
        output_reduced * mine[:, None], kv_pos * block, block, 0
    ).astype(jnp.bfloat16)
    weight_sheet = output_up_weight[0]
    output_change = lax.psum_scatter(
        jnp.dot(weight_sheet.T, own_shrink.T, preferred_element_type=jnp.float32),
        "wide",
        scatter_dimension=0,
        tiled=True,
    )
    return (output_baseline + adapter_scale * output_change.T).astype(jnp.bfloat16)


WHOLE = pl.BlockSpec(memory_space=pltpu.VMEM)
SCALARS = pl.BlockSpec(memory_space=pltpu.SMEM)


def code_two(ref, at, v):
    width = v.shape[1]
    groups = v.shape[0] // 16
    down = ref.shape[0] // 16
    for g in range(groups):
        rows = slice(g % down * 16, (g % down + 1) * 16)
        left = v[g * 16 : (g + 1) * 16]
        for t in range(2):
            lane = at + (g // down * 2 + t) * width
            top = left.astype(jnp.bfloat16)
            ref[rows, lane : lane + width] = top
            left = left - top.astype(jnp.float32)


def read_two(ref, at, width, groups):
    down = ref.shape[0] // 16
    out = []
    for g in range(groups):
        rows = slice(g % down * 16, (g % down + 1) * 16)
        lane = at + g // down * 2 * width
        part = ref[rows, lane : lane + 2 * width].astype(jnp.float32)
        out.append(part[:, :width] + part[:, width:])
    return jnp.concatenate(out, axis=0)


def prepare(hidden_input, gain, down, query_up, key_value_up, adapters, owners):
    count, width = hidden_input.shape
    entries = down.shape[0]
    rank, heads_width = query_up.shape
    head_dim = 128
    heads = key_value_up.shape[2] // head_dim
    group_width = heads_width // heads
    span = group_width + 2 * head_dim
    chunk = 1024
    quarter = width // 4
    held = (hidden_input, gain, down, query_up, key_value_up)

    def kernel(
        owner_ref, index_ref, x_in, gain_in, down_in, q_in, kv_in,
        same_ref, flip_ref, small_ref, slot_ref, mine_ref,
        x_ref, gain_ref, down_ref, q_ref, kv_ref, sem,
    ):
        def x_copy(i):
            part = (slice(None), pl.ds(i * quarter, quarter))
            return pltpu.make_async_copy(x_in.at[part], x_ref.at[part], sem.at[i])

        pairs = ((gain_in, gain_ref), (down_in, down_ref), (q_in, q_ref), (kv_in, kv_ref))
        copies = [
            pltpu.make_async_copy(src, dst, sem.at[4 + i]) for i, (src, dst) in enumerate(pairs)
        ]
        x_copies = [x_copy(i) for i in range(4)]
        for copy in copies[:2] + x_copies + copies[2:]:
            copy.start()

        wide_pos = lax.axis_index("wide")
        row = lax.broadcasted_iota(jnp.int32, (count, count), 0)
        column = lax.broadcasted_iota(jnp.int32, (count, count), 1)
        across = jnp.where(row == column, index_ref[...].astype(jnp.float32), 0.0)
        index = jnp.sum(across, axis=1, keepdims=True).astype(jnp.int32)
        slot = jnp.zeros((count, 1), jnp.int32)
        for a in range(owners.shape[0]):
            slot = jnp.where(index == a, owner_ref[a], slot)
        slot_ref[...] = slot
        mine = (slot == wide_pos).astype(jnp.float32)
        mine_ref[...] = mine

        for copy in copies[:2]:
            copy.wait()
        total = jnp.zeros((count, 1), jnp.float32)
        reduced = jnp.zeros((count, entries), jnp.float32)
        for at in range(0, width, chunk):
            part = slice(at, at + chunk)
            if at % quarter == 0:
                x_copies[at // quarter].wait()
            x = x_ref[:, part].astype(jnp.float32)
            total = total + jnp.sum(x * x, axis=1, keepdims=True)
            gained = (x * gain_ref[:, part]).astype(jnp.bfloat16)
            reduced = reduced + lax.dot_general(
                gained, down_ref[:, part], (((1,), (1,)), ((), ())),
                preferred_element_type=jnp.float32,
            )
        small_ref[...] = jnp.zeros_like(small_ref)
        small_ref[:, :entries] = reduced * mine
        small_ref[:, entries : entries + 1] = total * mine
        small = small_ref[...]
        for copy in copies[2:]:
            copy.wait()

        low = (wide_pos >> 2) & 1
        for ref, zb in ((same_ref, low), (flip_ref, 1 - low)):
            ref[:, span:] = jnp.zeros((2 * rank, 256), ref.dtype)
            code_two(ref, span, small)
            q = q_ref[:, pl.ds(pl.multiple_of(zb * 2 * group_width, 128), 2 * group_width)]
            ref[:, :group_width] = jnp.concatenate(
                [q[:, :group_width], q[:, group_width:]], axis=0
            )
            for t in range(2):
                kv = kv_ref[t, :, pl.ds(pl.multiple_of(zb * 2 * head_dim, 128), 2 * head_dim)]
                lane = group_width + t * head_dim
                ref[:, lane : lane + head_dim] = jnp.concatenate(
                    [kv[:, :head_dim], kv[:, head_dim:]], axis=0
                )

    message = jax.ShapeDtypeStruct((2 * rank, span + 256), query_up.dtype)
    return pl.pallas_call(
        kernel,
        in_specs=[SCALARS, WHOLE] + [pl.BlockSpec(memory_space=pl.ANY)] * len(held),
        out_specs=[WHOLE] * 5,
        out_shape=[
            message,
            message,
            jax.ShapeDtypeStruct((count, 32), jnp.float32),
            jax.ShapeDtypeStruct((count, 1), jnp.int32),
            jax.ShapeDtypeStruct((count, 1), jnp.float32),
        ],
        scratch_shapes=[pltpu.VMEM(v.shape, v.dtype) for v in held]
        + [pltpu.SemaphoreType.DMA((8,))],
        compiler_params=pltpu.CompilerParams(vmem_limit_bytes=60 * 2**20),
    )(owners, adapters, *held)


def stream_product(rows_in, gain, weight, start, stop, before, marker):
    count, cols = rows_in.shape[0], weight.shape[1]
    chunk = 512
    steps = (stop - start) // chunk
    held = pl.BlockSpec(memory_space=pl.ANY)
    operands, specs = [rows_in, weight, marker], [WHOLE, held, held]
    for more in (gain, before):
        if more is not None:
            operands += [more]
            specs += [WHOLE]

    def kernel(*refs):
        x_ref, w_ref = refs[:2]
        out_ref, buf, sem = refs[-3:]

        def fetch(i):
            return pltpu.make_async_copy(
                w_ref.at[pl.ds(start + i * chunk, chunk)], buf.at[i], sem.at[i]
            )

        for i in range(steps):
            fetch(i).start()
        if before is None:
            out_ref[...] = jnp.zeros_like(out_ref)
        else:
            out_ref[...] = refs[len(operands) - 1][...]

        def body(i, carry):
            at = pl.multiple_of(start + i * chunk, chunk)
            x = x_ref[:, pl.ds(at, chunk)]
            if gain is not None:
                x = (x.astype(jnp.float32) * refs[3][:, pl.ds(at, chunk)]).astype(jnp.bfloat16)
            fetch(i).wait()
            out_ref[...] += jnp.dot(x, buf[i], preferred_element_type=jnp.float32)
            return carry

        lax.fori_loop(0, steps, body, 0)

    return pl.pallas_call(
        kernel,
        in_specs=specs,
        out_specs=WHOLE,
        out_shape=jax.ShapeDtypeStruct((count, cols), jnp.float32),
        scratch_shapes=[
            pltpu.VMEM((steps, chunk, cols), weight.dtype),
            pltpu.SemaphoreType.DMA((steps,)),
        ],
        cost_estimate=pl.CostEstimate(
            flops=2 * count * cols * (stop - start),
            bytes_accessed=2 * cols * (stop - start),
            transcendentals=0,
        ),
        compiler_params=pltpu.CompilerParams(vmem_limit_bytes=47 * 2**20),
    )(*operands)


def pack_y(parts, small, cols):
    tall = parts[0].shape[0]
    count, entries = small.shape
    rank = tall // 2
    rows = 4 * rank

    def kernel(a_ref, b_ref, c_ref, d_ref, small_ref, away_ref, near_ref, far_ref, sum_ref):
        refs = (a_ref, b_ref, c_ref, d_ref)
        total = small_ref[...]
        for ref in refs[1:]:
            total = total + read_two(ref, 2 * cols, entries, count // 16)
        sum_ref[...] = total
        away_ref[:, 2 * cols :] = jnp.zeros((rows, 128), away_ref.dtype)
        code_two(away_ref, 2 * cols, total)

        wide_pos = lax.axis_index("wide")
        core, y = wide_pos & 1, (wide_pos >> 1) & 1

        def write(yb, cb):
            for out, half in ((near_ref, cb), (far_ref, 1 - cb)):
                out[...] = jnp.concatenate(
                    [
                        ref[yb * rank : (yb + 1) * rank, half * cols : (half + 1) * cols]
                        for ref in refs
                    ],
                    axis=0,
                )
            away_ref[:, : 2 * cols] = jnp.concatenate(
                [ref[(1 - yb) * rank : (2 - yb) * rank, : 2 * cols] for ref in refs], axis=0
            )

        for yb in range(2):
            for cb in range(2):

                @pl.when((y == yb) & (core == cb))
                def _():
                    write(yb, cb)

    dtype = parts[0].dtype
    return pl.pallas_call(
        kernel,
        in_specs=[WHOLE] * 5,
        out_specs=[WHOLE] * 4,
        out_shape=[
            jax.ShapeDtypeStruct((rows, 2 * cols + 128), dtype),
            jax.ShapeDtypeStruct((rows, cols), dtype),
            jax.ShapeDtypeStruct((rows, cols), dtype),
            jax.ShapeDtypeStruct(small.shape, jnp.float32),
        ],
        compiler_params=pltpu.CompilerParams(vmem_limit_bytes=8 * 2**20),
    )(*parts, small)


def merge(partial, small, received, ups, slot):
    count, cols = partial.shape
    lanes = 128
    blocks = cols // lanes
    each = count // 4
    entries = 24
    rank = entries // 3

    def kernel(p_ref, small_ref, r_ref, a_ref, b_ref, c_ref, d_ref, slot_ref, out_ref, acc_ref):
        wide_pos = lax.axis_index("wide")
        other = r_ref[:, cols : cols + 64].astype(jnp.float32)
        small = small_ref[...] + (other[:, :32] + other[:, 32:64])
        scale = lax.rsqrt(small[:, entries : entries + 1] / MODEL_WIDTH + 1e-05)
        shrink = (small * scale).astype(jnp.bfloat16)
        lane = lax.broadcasted_iota(jnp.int32, (count, lanes), 1)
        owner = wide_pos ^ (((lane >> 3) & 3) * 4 + ((lane >> 5) & 1) * 2 + (lane >> 6))
        hit = slot_ref[...] == owner
        entry = lax.broadcasted_iota(jnp.int32, (32, lanes), 0)
        to = lax.broadcasted_iota(jnp.int32, (32, lanes), 1) & (rank - 1)

        def spread(t):
            chosen = (entry == to + t * rank).astype(jnp.bfloat16)
            value = jnp.dot(shrink, chosen, preferred_element_type=jnp.float32)
            return jnp.where(hit, value, 0.0).astype(jnp.bfloat16)

        last = (wide_pos & 1) == 1
        parts = [spread(t) for t in range(3)]
        cut = cols - 2 * lanes
        spans = ((0, cut, parts[0]), (cut, cut + lanes, parts[1]), (cut + lanes, cols, parts[2]))
        for lo, hi, own in spans:
            left = parts[0] if lo == 0 else jnp.where(last, own, parts[0])
            up = jnp.concatenate([ref[:, lo:hi] for ref in (a_ref, b_ref, c_ref, d_ref)], axis=0)
            change = jnp.dot(left, up, preferred_element_type=jnp.float32)
            base = p_ref[:, lo:hi] + r_ref[:, lo:hi].astype(jnp.float32)
            acc_ref[:, lo:hi] = base * scale + adapter_scale * change
        for a in range(4):
            for b in range(blocks):
                out_ref[a, b] = acc_ref[
                    a * each : (a + 1) * each, b * lanes : (b + 1) * lanes
                ].astype(out_ref.dtype)

    return pl.pallas_call(
        kernel,
        in_specs=[WHOLE] * 8,
        out_specs=WHOLE,
        out_shape=jax.ShapeDtypeStruct((4, blocks, each, lanes), jnp.bfloat16),
        scratch_shapes=[pltpu.VMEM((count, cols), jnp.float32)],
        compiler_params=pltpu.CompilerParams(vmem_limit_bytes=12 * 2**20),
    )(partial, small, received, *ups, slot)


def strided_rows(wide_ref, rows_ref, order):
    pieces, tall, lanes = wide_ref.shape
    count, depth = rows_ref.shape
    blocks = depth // lanes
    for at, piece in order:
        wide_ref[at] = piece.astype(jnp.float32)
    flat = wide_ref.reshape(count * blocks, lanes)
    for j in range(blocks):
        rows_ref[:, j * lanes : (j + 1) * lanes] = flat[
            pl.ds(j, count, stride=blocks), :
        ].astype(rows_ref.dtype)


def ordered_product(groups, order, weight, stop, rows):
    pieces, tall, lanes = groups[0].shape
    depth, cols = weight.shape
    count = 4 * pieces * rows
    chunk = 512
    steps = stop // chunk

    def kernel(order_ref, a_ref, b_ref, c_ref, d_ref, w_ref, rows_ref, out_ref, wide_ref, buf, sem):
        copies = [
            pltpu.make_async_copy(w_ref.at[pl.ds(i * chunk, chunk)], buf.at[i], sem.at[i])
            for i in range(steps)
        ]
        for copy in copies:
            copy.start()
        placed = [
            (order_ref[g * pieces + p], ref[p])
            for g, ref in enumerate((a_ref, b_ref, c_ref, d_ref))
            for p in range(pieces)
        ]
        strided_rows(wide_ref, rows_ref, placed)
        total = jnp.zeros((count, cols), jnp.float32)
        out_ref[...] = total

        def body(i, carry):
            pltpu.make_async_copy(
                w_ref.at[pl.ds(i * chunk, chunk)], buf.at[i], sem.at[i]
            ).wait()
            at = pl.multiple_of(i * chunk, chunk)
            out_ref[...] += jnp.dot(
                rows_ref[:, pl.ds(at, chunk)], buf[i], preferred_element_type=jnp.float32
            )
            return carry

        lax.fori_loop(0, steps, body, 0)

    return pl.pallas_call(
        kernel,
        in_specs=[SCALARS] + [WHOLE] * 4 + [pl.BlockSpec(memory_space=pl.ANY)],
        out_specs=[WHOLE, WHOLE],
        out_shape=[
            jax.ShapeDtypeStruct((count, depth), groups[0].dtype),
            jax.ShapeDtypeStruct((count, cols), jnp.float32),
        ],
        scratch_shapes=[
            pltpu.VMEM((4 * pieces, tall, lanes), jnp.float32),
            pltpu.VMEM((steps, chunk, cols), weight.dtype),
            pltpu.SemaphoreType.DMA((steps,)),
        ],
        cost_estimate=pl.CostEstimate(
            flops=2 * count * cols * stop, bytes_accessed=2 * cols * stop, transcendentals=0
        ),
        compiler_params=pltpu.CompilerParams(vmem_limit_bytes=48 * 2**20),
    )(order, *groups, weight)


def pack_o_z(place, slot, pieces, downs, up, rows):
    count, tall, lanes = pieces.shape
    rank, depth = downs[0].shape
    span = up.shape[1] // count
    total = count * rows

    def kernel(place_ref, slot_ref, p_ref, *refs):
        down_refs, up_ref = refs[:4], refs[4]
        out_refs, (wide_ref, rows_ref) = refs[5:9], refs[9:]
        placed = [(place_ref[2] ^ dz, p_ref[dz]) for dz in range(count)]
        strided_rows(wide_ref, rows_ref, placed)
        at = lax.broadcasted_iota(jnp.int32, (total, 1), 0)
        slots = jnp.zeros((total, 1), jnp.int32)
        for r in range(total):
            row = (r // rows * 4 + place_ref[3] * 2 + place_ref[0]) * rows + r % rows
            slots = jnp.where(at == r, slot_ref[row], slots)
        out = jnp.zeros((total, rank), jnp.float32)
        for offset, ref in enumerate(down_refs):
            part = lax.dot_general(
                rows_ref[...], ref[...], (((1,), (1,)), ((), ())),
                preferred_element_type=jnp.float32,
            )
            out = out + jnp.where(slots == (place_ref[1] ^ offset), part, 0.0)
        for dz, ref in enumerate(out_refs):
            at = pl.multiple_of((place_ref[2] ^ dz) * span, lanes)
            ref[:, :span] = up_ref[:, pl.ds(at, span)]
            ref[:, span:] = jnp.zeros((rank, lanes), ref.dtype)
            for rows_at, at in ((0, span), (rank, span + lanes // 2)):
                left = out[rows_at : min(rows_at + rank, total)]
                for t in range(2):
                    top = left.astype(jnp.bfloat16)
                    ref[: left.shape[0], at + t * rank : at + (t + 1) * rank] = top
                    left = left - top.astype(jnp.float32)

    return pl.pallas_call(
        kernel,
        in_specs=[SCALARS, SCALARS] + [WHOLE] * 6,
        out_specs=[WHOLE] * 4,
        out_shape=[jax.ShapeDtypeStruct((rank, span + lanes), up.dtype)] * 4,
        scratch_shapes=[
            pltpu.VMEM((count, tall, lanes), jnp.float32),
            pltpu.VMEM((total, depth), pieces.dtype),
        ],
        cost_estimate=pl.CostEstimate(
            flops=0, bytes_accessed=4 * total * depth, transcendentals=0
        ),
        compiler_params=pltpu.CompilerParams(vmem_limit_bytes=10 * 2**20),
    )(place, slot, pieces, *downs, up)


def pack_o_y(place, parts, total):
    rank = parts[0].shape[0]
    lanes = 128
    span = (parts[0].shape[1] - lanes) // 2

    def kernel(place_ref, a_ref, b_ref, c_ref, d_ref, away_ref, keep_ref, sum_ref):
        refs = (a_ref, b_ref, c_ref, d_ref)

        def decoded(ref, rows, at):
            high, low = [
                ref[rows, at + t * rank : at + (t + 1) * rank].astype(jnp.float32)
                for t in range(2)
            ]
            return high + low

        for at, rows in (
            (0, slice(0, rank)),
            (lanes // 2, slice(0, total - rank)),
        ):
            parts_of = [decoded(ref, rows, 2 * span + at) for ref in refs]
            value = (parts_of[0] + parts_of[1]) + (parts_of[2] + parts_of[3])
            sum_ref[pl.ds(0 if at == 0 else rank, value.shape[0]), :] = value
        away_ref[:, span:] = jnp.zeros((4 * rank, lanes), away_ref.dtype)
        left = sum_ref[...]
        for t in range(2):
            top = left.astype(jnp.bfloat16)
            away_ref[:total, span + t * rank : span + (t + 1) * rank] = top
            left = left - top.astype(jnp.float32)

        def write(yb):
            for dz, ref in enumerate(refs):
                rows = slice(dz * rank, (dz + 1) * rank)
                keep_ref[rows, :] = ref[:, yb * span : (yb + 1) * span]
                away_ref[rows, :span] = ref[:, (1 - yb) * span : (2 - yb) * span]

        for yb in range(2):

            @pl.when(place_ref[3] == yb)
            def _():
                write(yb)

    dtype = parts[0].dtype
    return pl.pallas_call(
        kernel,
        in_specs=[SCALARS] + [WHOLE] * 4,
        out_specs=[WHOLE] * 3,
        out_shape=[
            jax.ShapeDtypeStruct((4 * rank, span + lanes), dtype),
            jax.ShapeDtypeStruct((4 * rank, span), dtype),
            jax.ShapeDtypeStruct((total, rank), jnp.float32),
        ],
        compiler_params=pltpu.CompilerParams(vmem_limit_bytes=8 * 2**20),
    )(place, *parts)


def in_two(v):
    top = lax.reduce_precision(v, 8, 7)
    return jnp.concatenate([top, v - top], axis=1).astype(jnp.bfloat16)


def from_two(v):
    n = v.shape[1] // 2
    v = v.astype(jnp.float32)
    return v[:, :n] + v[:, n:]


def staged_path(
    hidden_input,
    input_norm_gain,
    joint_projection_weight,
    output_weight,
    key_cache,
    value_cache,
    joint_down_weight,
    query_up_weight,
    key_value_up_weight,
    output_down_weight,
    output_up_weight,
    row_adapter_index,
    adapter_owner_slot,
    lengths,
):
    f32, bf16 = jnp.float32, jnp.bfloat16
    batch = hidden_input.shape[0]
    rows = lengths.shape[0]
    heads = key_cache.shape[1]
    head_dim = key_cache.shape[3]
    rank = query_up_weight.shape[1]
    cols = joint_projection_weight.shape[1]
    out_cols = output_weight.shape[1]
    blocks = cols // head_dim
    group = 2 * blocks - 2
    wide = batch // rows
    kv_pos = lax.axis_index("kv")
    wide_pos = lax.axis_index("wide")
    core = wide_pos & 1
    y = (wide_pos >> 1) & 1
    z = wide_pos >> 2
    right = (z >> 1) == kv_pos

    def is_right(i):
        return ((i % wide) >> 3) == i // wide

    def swap(x, mask, source=None, target=None):
        pairs = [(i, i ^ mask) for i in range(2 * wide)]
        if source is not None:
            pairs = [p for p in pairs if is_right(p[0]) == source]
        if target is not None:
            pairs = [p for p in pairs if is_right(p[1]) == target]
        return lax.ppermute(x, ("kv", "wide"), pairs)

    def pick(x, i, axis=0):
        return lax.dynamic_index_in_dim(x, i, axis, keepdims=False)

    half = batch // 2
    place = jnp.stack([core, wide_pos, z, y])

    gain = input_norm_gain[None]
    same, flip, small, slot, mine = prepare(
        hidden_input,
        gain,
        joint_down_weight[0].T,
        query_up_weight[0],
        key_value_up_weight[0],
        row_adapter_index[None],
        adapter_owner_slot,
    )
    parts = [same, swap(flip, 4), swap(same, 8), swap(flip, 12)]
    depth = hidden_input.shape[1]
    cut = depth * 5 // 8
    weight = joint_projection_weight
    partial = stream_product(hidden_input, gain, weight, 0, cut, None, same)
    away, ups_near, ups_far, small = pack_y(parts, small, cols)
    away, partial = lax.optimization_barrier((away, partial))
    from_y = swap(away, 2)
    partial = stream_product(hidden_input, gain, weight, cut, depth, partial, away)
    partial, from_y = lax.optimization_barrier((partial, from_y))
    coded = from_y[:, 2 * cols :].reshape(2, 16, 2, 64).transpose(2, 0, 1, 3).reshape(-1, 64)
    small = small + from_two(coded[:batch])
    small = small + swap(small, 1)
    ups_y = from_y[:, : 2 * cols].reshape(-1, 2, cols)
    ups = (
        ups_near,
        pick(ups_y, core, 1),
        swap(ups_far, 1),
        swap(pick(ups_y, 1 - core, 1), 1),
    )
    message = jnp.concatenate([partial.astype(bf16), in_two(small)], axis=1)
    o_down = output_down_weight[0].T
    message, o_down = lax.optimization_barrier((message, o_down))
    from_x = swap(message, 16, target=True)
    o_down_y = swap(o_down, 2)
    merged = merge(partial, small, from_x, ups, slot)

    to = [pick(merged, z ^ d) for d in range(4)]
    from_1 = swap(to[1], 4, source=True)
    from_2 = swap(to[2], 8, source=True)
    from_3 = swap(to[3], 12, source=True)
    near = jnp.stack([jnp.where(right, to[0], from_2), jnp.where(right, from_1, from_3)])
    keep = lax.dynamic_slice_in_dim(near, y * 2 * rows, 2 * rows, 2)
    give = lax.dynamic_slice_in_dim(near, (1 - y) * 2 * rows, 2 * rows, 2)
    from_y = swap(give, 2)
    near = jnp.stack([jnp.where(y == 0, keep, from_y), jnp.where(y == 0, from_y, keep)], axis=1)
    far = swap(near, 1)
    parts = [jnp.where(core == 0, near, far), jnp.where(core == 0, far, near)]
    parts = [
        lax.dynamic_slice_in_dim(jnp.where((z & 1) == 0, p, p[::-1]), core * rows, rows, 3)
        for p in parts
    ]
    joined = jnp.concatenate(parts, axis=2).astype(f32)
    joined = joined.reshape(heads, 2 * blocks, rows, head_dim).transpose(2, 0, 1, 3)
    query_vector = rotate(joined[:, :, :group], lengths).astype(bf16)
    fresh_key = rotate(joined[:, :, group], lengths).astype(bf16)
    value_new = joined[:, :, group + 1].astype(bf16)

    inverse_root = jnp.sqrt(f32(head_dim))
    scores = jnp.einsum("rkgd,rkld->rkgl", query_vector, key_cache, preferred_element_type=f32)
    scores = scores / inverse_root
    valid = jnp.arange(key_cache.shape[2], dtype=jnp.int32)[None, :] < lengths[:, None]
    scores = jnp.where(valid[:, None, None, :], scores, -jnp.inf)
    fresh_score = (
        jnp.einsum("rkgd,rkd->rkg", query_vector, fresh_key, preferred_element_type=f32)
        / inverse_root
    )
    top = jnp.maximum(jnp.max(scores, axis=-1), fresh_score)
    expd = jnp.exp(scores - top[..., None])
    exp_new = jnp.exp(fresh_score - top)
    total = jnp.sum(expd, axis=-1) + exp_new
    probs = (expd / total[..., None]).astype(bf16)
    prob_new = (exp_new / total).astype(bf16)
    attended = jnp.einsum("rkgl,rkld->rkgd", probs, value_cache, preferred_element_type=f32)
    attended = (
        attended + prob_new.astype(f32)[..., None] * value_new.astype(f32)[:, :, None, :]
    )
    attended = attended.astype(bf16).reshape(-1, head_dim)

    near = jnp.stack([attended, swap(attended, 4), swap(attended, 8), swap(attended, 12)])
    near_y = swap(near, 2)
    o_downs = (o_down, swap(o_down, 1), o_down_y, swap(o_down_y, 1))
    o_z = pack_o_z(place, slot[:, 0], near, o_downs, output_up_weight[0], rows)
    near_y, o_z = lax.optimization_barrier((near_y, o_z))
    from_z = [swap(o_z[1], 4), swap(o_z[2], 8), swap(o_z[3], 12)]
    far, far_y = swap(near, 1), swap(near_y, 1)
    offsets = [
        dz * 4 + dy * 2 + dcore for dcore in range(2) for dy in range(2) for dz in range(4)
    ]
    order = wide_pos ^ jnp.array(offsets, jnp.int32)
    first, second = depth * 3 // 8, depth * 3 // 4
    everyone, mixed = ordered_product(
        (near, near_y, far, far_y), order, output_weight, first, rows
    )
    mixed, from_z = lax.optimization_barrier((mixed, from_z))
    o_away, o_keep, o_rows = pack_o_y(place, [o_z[0]] + from_z, 4 * rows)
    o_far = swap(o_away, 2)
    mixed = stream_product(everyone, None, output_weight, first, second, mixed, o_away)
    mixed, o_far = lax.optimization_barrier((mixed, o_far))
    o_rows = jnp.stack([o_rows, from_two(o_far[: 4 * rows, 2 * out_cols :][:, : 2 * rank])])
    o_up = jnp.concatenate([o_keep, o_far[:, : 2 * out_cols]], axis=0)
    o_up = o_up.reshape(8 * rank, 2, out_cols)
    o_up_c = swap(pick(o_up, 1 - core, 1), 1)
    o_rows_c = swap(o_rows, 1)
    mixed = stream_product(everyone, None, output_weight, second, depth, mixed, o_rows)
    o_up = jnp.concatenate([pick(o_up, core, 1), o_up_c], axis=0)
    o_rows = jnp.stack([o_rows, o_rows_c], axis=1)
    o_rows = jnp.where(y == 0, o_rows, o_rows[::-1])
    o_rows = jnp.where(core == 0, o_rows, o_rows[:, ::-1])
    o_rows = o_rows.reshape(2, 2, 4, rows, rank).transpose(2, 0, 1, 3, 4).reshape(batch, rank)

    keep_out = lax.dynamic_slice_in_dim(mixed, kv_pos * half, half)
    give_out = lax.dynamic_slice_in_dim(mixed, (1 - kv_pos) * half, half).astype(bf16)
    o_keep = lax.dynamic_slice_in_dim(o_rows, kv_pos * half, half)
    o_give = in_two(lax.dynamic_slice_in_dim(o_rows, (1 - kv_pos) * half, half))
    from_x = swap(jnp.concatenate([give_out, o_give], axis=1), 16)
    o_keep = o_keep + from_two(from_x[:, out_cols:])
    lane = jnp.arange(wide, dtype=jnp.int32)
    owner = wide_pos ^ ((lane & 3) * 4 + ((lane >> 2) & 1) * 2 + (lane >> 3))
    slot_o = lax.dynamic_slice_in_dim(slot, kv_pos * half, half)
    hit = slot_o == owner[None, :]
    shrink = jnp.where(hit[:, :, None], o_keep.astype(bf16)[:, None, :], 0).reshape(half, -1)
    change = jnp.dot(shrink, o_up, preferred_element_type=f32)
    base = keep_out + from_x[:, :out_cols].astype(f32)
    return (base + adapter_scale * change).astype(bf16)


def on_device(*arrays):
    lengths, key_cache, weight = arrays[13], arrays[4], arrays[2]
    batch, rows, heads = arrays[0].shape[0], lengths.shape[0], key_cache.shape[1]
    staged = batch == 16 * rows and heads == 4 and 2 * weight.shape[1] == 18 * key_cache.shape[3]
    return (staged_path if staged else general_path)(*arrays)


def solution(mesh):
    in_specs = (
        P(None, "kv"),
        P("kv"),
        P("kv", "wide"),
        P("kv", "wide"),
        P("wide", "kv", None, None),
        P("wide", "kv", None, None),
        P("wide", "kv", None),
        P("wide", None, "kv"),
        P("wide", None, None, "kv"),
        P("wide", "kv", None),
        P("wide", None, None),
        P(),
        P(),
        P("wide"),
    )
    out_specs = P("kv", "wide")
    return jax.shard_map(
        on_device, mesh=mesh, in_specs=in_specs, out_specs=out_specs, check_vma=False
    )
```

```python
import jax
import jax.numpy as jnp
from jax import lax
from jax.experimental import pallas as pl
from jax.experimental.pallas import tpu as pltpu
from jax.sharding import PartitionSpec as P

MODEL_WIDTH = 16384


rope_base = 500000.0
adapter_scale = 2.0


def rotate(values, positions):
    half = values.shape[-1] // 2
    freq = rope_base ** (-jnp.arange(half, dtype=jnp.float32) * 2.0 / values.shape[-1])
    angle = positions.astype(jnp.float32)[:, None] * freq[None, :]
    array_shape = (angle.shape[0],) + (1,) * (values.ndim - 2) + (half,)
    cosine = jnp.cos(angle).reshape(array_shape)
    sine = jnp.sin(angle).reshape(array_shape)
    first = values[..., :half]
    second = values[..., half:]
    return jnp.concatenate(
        [first * cosine - second * sine, second * cosine + first * sine], axis=-1
    )


def arrange(query_change, key_change, value_change, local_key_value):
    count = query_change.shape[0]
    joined = jnp.concatenate(
        [
            query_change.reshape(count, local_key_value, -1),
            key_change.reshape(count, local_key_value, -1),
            value_change.reshape(count, local_key_value, -1),
        ],
        axis=2,
    )
    return joined.reshape(count, -1)


def general_path(
    hidden_input,
    input_norm_gain,
    joint_projection_weight,
    output_weight,
    key_cache,
    value_cache,
    joint_down_weight,
    query_up_weight,
    key_value_up_weight,
    output_down_weight,
    output_up_weight,
    row_adapter_index,
    adapter_owner_slot,
    lengths,
):
    local_rows = lengths.shape[0]
    local_key_value = key_cache.shape[1]
    head_dim = key_cache.shape[3]
    rank_width = query_up_weight.shape[1]
    wide_pos = lax.axis_index("wide")
    kv_pos = lax.axis_index("kv")
    row_start = wide_pos * local_rows
    table = (
        row_adapter_index[:, None]
        == jnp.arange(adapter_owner_slot.shape[0], dtype=jnp.int32)[None, :]
    )
    row_slot = jnp.sum(jnp.where(table, adapter_owner_slot[None, :], 0), axis=1)
    mine = (row_slot == wide_pos).astype(jnp.float32)
    widened = hidden_input.astype(jnp.float32)
    scaled_hidden = (widened * input_norm_gain[None, :]).astype(jnp.bfloat16)
    partial_sq = jnp.sum(widened * widened, axis=1)
    partial_reduced = jnp.dot(
        scaled_hidden, joint_down_weight[0], preferred_element_type=jnp.float32
    )
    total_sq, reduced_hidden = lax.psum((partial_sq, partial_reduced), "kv")
    scale = lax.rsqrt(total_sq / MODEL_WIDTH + 1e-05)
    shrink_bf = (reduced_hidden * scale[:, None] * mine[:, None]).astype(jnp.bfloat16)
    base_part = jnp.dot(scaled_hidden, joint_projection_weight, preferred_element_type=jnp.float32)
    regrouped = lax.all_to_all(base_part, "wide", split_axis=0, concat_axis=1, tiled=True)
    grouped_heads = lax.psum_scatter(regrouped, "kv", scatter_dimension=1, tiled=True)
    row_scale = lax.dynamic_slice_in_dim(scale, row_start, local_rows)
    grouped_heads = grouped_heads * row_scale[:, None]
    shrinks = lax.all_gather(shrink_bf[None], "wide", axis=0, tiled=True)
    query_sheet = lax.all_gather(query_up_weight, "wide", axis=0, tiled=True)
    key_value_sheet = lax.all_gather(key_value_up_weight, "wide", axis=0, tiled=True)
    own_rows = lax.dynamic_slice_in_dim(shrinks, row_start, local_rows, 1)
    query_change = jnp.einsum(
        "nbr,nrc->bc", own_rows[:, :, :rank_width], query_sheet, preferred_element_type=jnp.float32
    )
    key_change = jnp.einsum(
        "nbr,nrc->bc",
        own_rows[:, :, rank_width : 2 * rank_width],
        key_value_sheet[:, 0],
        preferred_element_type=jnp.float32,
    )
    value_change = jnp.einsum(
        "nbr,nrc->bc",
        own_rows[:, :, 2 * rank_width :],
        key_value_sheet[:, 1],
        preferred_element_type=jnp.float32,
    )
    adapter_change = arrange(query_change, key_change, value_change, local_key_value)
    merged_output = (grouped_heads + adapter_scale * adapter_change).reshape(
        local_rows, local_key_value, -1
    )
    width = merged_output.shape[2] - 2 * head_dim
    heads_per = width // head_dim
    query_vector = rotate(
        merged_output[:, :, :width].reshape(local_rows, local_key_value, heads_per, head_dim),
        lengths,
    ).astype(jnp.bfloat16)
    fresh_key = rotate(merged_output[:, :, width : width + head_dim], lengths).astype(jnp.bfloat16)
    value_new = merged_output[:, :, width + head_dim :].astype(jnp.bfloat16)
    inverse_root = jnp.sqrt(jnp.float32(head_dim))
    scores = (
        jnp.einsum("rkgd,rkld->rkgl", query_vector, key_cache, preferred_element_type=jnp.float32)
        / inverse_root
    )
    valid = jnp.arange(key_cache.shape[2], dtype=jnp.int32)[None, :] < lengths[:, None]
    scores = jnp.where(valid[:, None, None, :], scores, -jnp.inf)
    fresh_score = (
        jnp.einsum("rkgd,rkd->rkg", query_vector, fresh_key, preferred_element_type=jnp.float32)
        / inverse_root
    )
    top = jnp.maximum(jnp.max(scores, axis=-1), fresh_score)
    expd = jnp.exp(scores - top[..., None])
    exp_new = jnp.exp(fresh_score - top)
    total = jnp.sum(expd, axis=-1) + exp_new
    probs = (expd / total[..., None]).astype(jnp.bfloat16)
    prob_new = (exp_new / total).astype(jnp.bfloat16)
    attention_output = jnp.einsum(
        "rkgl,rkld->rkgd", probs, value_cache, preferred_element_type=jnp.float32
    )
    attention_output = (
        attention_output
        + prob_new.astype(jnp.float32)[..., None] * value_new.astype(jnp.float32)[:, :, None, :]
    )
    attention_output = attention_output.astype(jnp.bfloat16).reshape(local_rows, -1)
    out_cols = output_weight.shape[1]
    slice_portion = lax.all_gather(attention_output, "wide", axis=0, tiled=True)
    mixed = jnp.concatenate(
        [
            jnp.dot(slice_portion, output_weight, preferred_element_type=jnp.float32),
            jnp.dot(slice_portion, output_down_weight[0], preferred_element_type=jnp.float32),
        ],
        axis=1,
    )
    output_baseline = lax.psum_scatter(
        mixed[:, :out_cols].astype(jnp.bfloat16), "kv", scatter_dimension=0, tiled=True
    ).astype(jnp.float32)
    output_reduced = lax.psum(mixed[:, out_cols:], "kv")
    block = output_baseline.shape[0]
    own_shrink = lax.dynamic_slice_in_dim(
        output_reduced * mine[:, None], kv_pos * block, block, 0
    ).astype(jnp.bfloat16)
    weight_sheet = output_up_weight[0]
    output_change = lax.psum_scatter(
        jnp.dot(weight_sheet.T, own_shrink.T, preferred_element_type=jnp.float32),
        "wide",
        scatter_dimension=0,
        tiled=True,
    )
    return (output_baseline + adapter_scale * output_change.T).astype(jnp.bfloat16)


WHOLE = pl.BlockSpec(memory_space=pltpu.VMEM)
SCALARS = pl.BlockSpec(memory_space=pltpu.SMEM)


def code_two(ref, at, v):
    width = v.shape[1]
    groups = v.shape[0] // 16
    down = ref.shape[0] // 16
    for g in range(groups):
        rows = slice(g % down * 16, (g % down + 1) * 16)
        left = v[g * 16 : (g + 1) * 16]
        for t in range(2):
            lane = at + (g // down * 2 + t) * width
            top = left.astype(jnp.bfloat16)
            ref[rows, lane : lane + width] = top
            left = left - top.astype(jnp.float32)


def read_two(ref, at, width, groups):
    down = ref.shape[0] // 16
    out = []
    for g in range(groups):
        rows = slice(g % down * 16, (g % down + 1) * 16)
        lane = at + g // down * 2 * width
        part = ref[rows, lane : lane + 2 * width].astype(jnp.float32)
        out.append(part[:, :width] + part[:, width:])
    return jnp.concatenate(out, axis=0)


def prepare(hidden_input, gain, down, query_up, key_value_up, adapters, owners):
    count, width = hidden_input.shape
    entries = down.shape[0]
    rank, heads_width = query_up.shape
    head_dim = 128
    heads = key_value_up.shape[2] // head_dim
    group_width = heads_width // heads
    span = group_width + 2 * head_dim
    chunk = 1024
    quarter = width // 4
    held = (hidden_input, gain, down, query_up, key_value_up)

    def kernel(
        owner_ref, index_ref, x_in, gain_in, down_in, q_in, kv_in,
        same_ref, flip_ref, small_ref, slot_ref, mine_ref,
        x_ref, gain_ref, down_ref, q_ref, kv_ref, sem,
    ):
        def x_copy(i):
            part = (slice(None), pl.ds(i * quarter, quarter))
            return pltpu.make_async_copy(x_in.at[part], x_ref.at[part], sem.at[i])

        pairs = ((gain_in, gain_ref), (down_in, down_ref), (q_in, q_ref), (kv_in, kv_ref))
        copies = [
            pltpu.make_async_copy(src, dst, sem.at[4 + i]) for i, (src, dst) in enumerate(pairs)
        ]
        x_copies = [x_copy(i) for i in range(4)]
        for copy in copies[:2] + x_copies + copies[2:]:
            copy.start()

        wide_pos = lax.axis_index("wide")
        row = lax.broadcasted_iota(jnp.int32, (count, count), 0)
        column = lax.broadcasted_iota(jnp.int32, (count, count), 1)
        across = jnp.where(row == column, index_ref[...].astype(jnp.float32), 0.0)
        index = jnp.sum(across, axis=1, keepdims=True).astype(jnp.int32)
        slot = jnp.zeros((count, 1), jnp.int32)
        for a in range(owners.shape[0]):
            slot = jnp.where(index == a, owner_ref[a], slot)
        slot_ref[...] = slot
        mine = (slot == wide_pos).astype(jnp.float32)
        mine_ref[...] = mine

        for copy in copies[:2]:
            copy.wait()
        total = jnp.zeros((count, 1), jnp.float32)
        for at in range(0, width, chunk):
            part = slice(at, at + chunk)
            if at % quarter == 0:
                x_copies[at // quarter].wait()
            x = x_ref[:, part].astype(jnp.float32)
            total = total + jnp.sum(x * x, axis=1, keepdims=True)
            x_ref[:, part] = (x * gain_ref[:, part]).astype(jnp.bfloat16)
        reduced = lax.dot_general(
            x_ref[...], down_ref[...], (((1,), (1,)), ((), ())),
            preferred_element_type=jnp.float32,
        )
        small_ref[...] = jnp.zeros_like(small_ref)
        small_ref[:, :entries] = reduced * mine
        small_ref[:, entries : entries + 1] = total * mine
        small = small_ref[...]
        for copy in copies[2:]:
            copy.wait()

        low = (wide_pos >> 2) & 1
        for ref, zb in ((same_ref, low), (flip_ref, 1 - low)):
            ref[:, span:] = jnp.zeros((2 * rank, 256), ref.dtype)
            code_two(ref, span, small)
            q = q_ref[:, pl.ds(pl.multiple_of(zb * 2 * group_width, 128), 2 * group_width)]
            ref[:, :group_width] = jnp.concatenate(
                [q[:, :group_width], q[:, group_width:]], axis=0
            )
            for t in range(2):
                kv = kv_ref[t, :, pl.ds(pl.multiple_of(zb * 2 * head_dim, 128), 2 * head_dim)]
                lane = group_width + t * head_dim
                ref[:, lane : lane + head_dim] = jnp.concatenate(
                    [kv[:, :head_dim], kv[:, head_dim:]], axis=0
                )

    message = jax.ShapeDtypeStruct((2 * rank, span + 256), query_up.dtype)
    return pl.pallas_call(
        kernel,
        in_specs=[SCALARS, WHOLE] + [pl.BlockSpec(memory_space=pl.ANY)] * len(held),
        out_specs=[WHOLE] * 5,
        out_shape=[
            message,
            message,
            jax.ShapeDtypeStruct((count, 32), jnp.float32),
            jax.ShapeDtypeStruct((count, 1), jnp.int32),
            jax.ShapeDtypeStruct((count, 1), jnp.float32),
        ],
        scratch_shapes=[pltpu.VMEM(v.shape, v.dtype) for v in held]
        + [pltpu.SemaphoreType.DMA((8,))],
        compiler_params=pltpu.CompilerParams(vmem_limit_bytes=60 * 2**20),
    )(owners, adapters, *held)


def stream_product(rows_in, gain, weight, start, stop, before, marker):
    count, cols = rows_in.shape[0], weight.shape[1]
    chunk = 512
    steps = (stop - start) // chunk
    held = pl.BlockSpec(memory_space=pl.ANY)
    operands, specs = [rows_in, weight], [WHOLE, held]
    for more, spec in ((gain, WHOLE), (marker, held), (before, WHOLE)):
        if more is not None:
            operands += [more]
            specs += [spec]

    def kernel(*refs):
        x_ref, w_ref = refs[:2]
        out_ref, buf, sem = refs[-3:]

        def fetch(i):
            return pltpu.make_async_copy(
                w_ref.at[pl.ds(start + i * chunk, chunk)], buf.at[i], sem.at[i]
            )

        for i in range(steps):
            fetch(i).start()
        if before is None:
            out_ref[...] = jnp.zeros_like(out_ref)
        else:
            out_ref[...] = refs[len(operands) - 1][...]

        def body(i, carry):
            at = pl.multiple_of(start + i * chunk, chunk)
            x = x_ref[:, pl.ds(at, chunk)]
            if gain is not None:
                x = (x.astype(jnp.float32) * refs[2][:, pl.ds(at, chunk)]).astype(jnp.bfloat16)
            fetch(i).wait()
            out_ref[...] += jnp.dot(x, buf[i], preferred_element_type=jnp.float32)
            return carry

        lax.fori_loop(0, steps, body, 0)

    return pl.pallas_call(
        kernel,
        in_specs=specs,
        out_specs=WHOLE,
        out_shape=jax.ShapeDtypeStruct((count, cols), jnp.float32),
        scratch_shapes=[
            pltpu.VMEM((steps, chunk, cols), weight.dtype),
            pltpu.SemaphoreType.DMA((steps,)),
        ],
        cost_estimate=pl.CostEstimate(
            flops=2 * count * cols * (stop - start),
            bytes_accessed=2 * cols * (stop - start),
            transcendentals=0,
        ),
        compiler_params=pltpu.CompilerParams(vmem_limit_bytes=47 * 2**20),
    )(*operands)


def pack_y(parts, small, cols):
    tall = parts[0].shape[0]
    count, entries = small.shape
    rank = tall // 2
    rows = 4 * rank

    def kernel(a_ref, b_ref, c_ref, d_ref, small_ref, away_ref, near_ref, far_ref, sum_ref):
        refs = (a_ref, b_ref, c_ref, d_ref)
        total = small_ref[...]
        for ref in refs[1:]:
            total = total + read_two(ref, 2 * cols, entries, count // 16)
        sum_ref[...] = total
        away_ref[:, 2 * cols :] = jnp.zeros((rows, 128), away_ref.dtype)
        code_two(away_ref, 2 * cols, total)

        wide_pos = lax.axis_index("wide")
        core, y = wide_pos & 1, (wide_pos >> 1) & 1

        def write(yb, cb):
            for out, half in ((near_ref, cb), (far_ref, 1 - cb)):
                out[...] = jnp.concatenate(
                    [
                        ref[yb * rank : (yb + 1) * rank, half * cols : (half + 1) * cols]
                        for ref in refs
                    ],
                    axis=0,
                )
            away_ref[:, : 2 * cols] = jnp.concatenate(
                [ref[(1 - yb) * rank : (2 - yb) * rank, : 2 * cols] for ref in refs], axis=0
            )

        for yb in range(2):
            for cb in range(2):

                @pl.when((y == yb) & (core == cb))
                def _():
                    write(yb, cb)

    dtype = parts[0].dtype
    return pl.pallas_call(
        kernel,
        in_specs=[WHOLE] * 5,
        out_specs=[WHOLE] * 4,
        out_shape=[
            jax.ShapeDtypeStruct((rows, 2 * cols + 128), dtype),
            jax.ShapeDtypeStruct((rows, cols), dtype),
            jax.ShapeDtypeStruct((rows, cols), dtype),
            jax.ShapeDtypeStruct(small.shape, jnp.float32),
        ],
        compiler_params=pltpu.CompilerParams(vmem_limit_bytes=8 * 2**20),
    )(*parts, small)


def merge(partial, small, received, ups, slot):
    count, cols = partial.shape
    lanes = 128
    blocks = cols // lanes
    each = count // 4
    entries = 24
    rank = entries // 3

    def kernel(p_ref, small_ref, r_ref, a_ref, b_ref, c_ref, d_ref, slot_ref, out_ref, acc_ref, tall_ref):
        wide_pos = lax.axis_index("wide")
        other = r_ref[:, cols : cols + 64].astype(jnp.float32)
        small = small_ref[...] + (other[:, :32] + other[:, 32:64])
        scale = lax.rsqrt(small[:, entries : entries + 1] / MODEL_WIDTH + 1e-05)
        shrink = (small * scale).astype(jnp.bfloat16)
        lane = lax.broadcasted_iota(jnp.int32, (count, lanes), 1)
        owner = wide_pos ^ (((lane >> 3) & 3) * 4 + ((lane >> 5) & 1) * 2 + (lane >> 6))
        hit = slot_ref[...] == owner
        entry = lax.broadcasted_iota(jnp.int32, (32, lanes), 0)
        to = lax.broadcasted_iota(jnp.int32, (32, lanes), 1) & (rank - 1)

        def spread(t):
            chosen = (entry == to + t * rank).astype(jnp.bfloat16)
            value = jnp.dot(shrink, chosen, preferred_element_type=jnp.float32)
            return jnp.where(hit, value, 0.0).astype(jnp.bfloat16)

        last = (wide_pos & 1) == 1
        parts = [spread(t) for t in range(3)]
        cut = cols - 2 * lanes
        spans = ((0, cut, parts[0]), (cut, cut + lanes, parts[1]), (cut + lanes, cols, parts[2]))
        for lo, hi, own in spans:
            left = parts[0] if lo == 0 else jnp.where(last, own, parts[0])
            up = jnp.concatenate([ref[:, lo:hi] for ref in (a_ref, b_ref, c_ref, d_ref)], axis=0)
            change = jnp.dot(left, up, preferred_element_type=jnp.float32)
            base = p_ref[:, lo:hi] + r_ref[:, lo:hi].astype(jnp.float32)
            acc_ref[:, lo:hi] = base * scale + adapter_scale * change
        for b in range(blocks):
            tall_ref[pl.ds(b, count, stride=blocks), :] = acc_ref[:, b * lanes : (b + 1) * lanes]
        for a in range(4):
            part = slice(a * each * blocks, (a + 1) * each * blocks)
            out_ref[a // 2, a % 2] = tall_ref[part, :].astype(out_ref.dtype)

    return pl.pallas_call(
        kernel,
        in_specs=[WHOLE] * 8,
        out_specs=WHOLE,
        out_shape=jax.ShapeDtypeStruct((2, 2, each * blocks, lanes), jnp.bfloat16),
        scratch_shapes=[
            pltpu.VMEM((count, cols), jnp.float32),
            pltpu.VMEM((count * blocks, lanes), jnp.float32),
        ],
        compiler_params=pltpu.CompilerParams(vmem_limit_bytes=12 * 2**20),
    )(partial, small, received, *ups, slot)


def strided_rows(wide_ref, rows_ref, order):
    pieces, tall, lanes = wide_ref.shape
    count, depth = rows_ref.shape
    blocks = depth // lanes
    for at, piece in order:
        wide_ref[at] = piece.astype(jnp.float32)
    flat = wide_ref.reshape(count * blocks, lanes)
    for j in range(blocks):
        rows_ref[:, j * lanes : (j + 1) * lanes] = flat[
            pl.ds(j, count, stride=blocks), :
        ].astype(rows_ref.dtype)


def ordered_product(groups, offsets, weight, stop, rows):
    tall, lanes = groups[0].shape[1:]
    depth, cols = weight.shape
    pieces = sum(len(at) for at in offsets)
    count = pieces * rows
    chunk = 512
    steps = stop // chunk

    def kernel(*refs):
        group_refs, w_ref = refs[: len(groups)], refs[len(groups)]
        rows_ref, out_ref, wide_ref, buf, sem = refs[len(groups) + 1 :]
        wide_pos = lax.axis_index("wide")
        copies = [
            pltpu.make_async_copy(w_ref.at[pl.ds(i * chunk, chunk)], buf.at[i], sem.at[i])
            for i in range(steps)
        ]
        for copy in copies:
            copy.start()
        placed = [
            (wide_pos ^ offset, ref[p])
            for ref, at in zip(group_refs, offsets)
            for p, offset in enumerate(at)
        ]
        strided_rows(wide_ref, rows_ref, placed)
        total = jnp.zeros((count, cols), jnp.float32)
        out_ref[...] = total

        def body(i, carry):
            pltpu.make_async_copy(
                w_ref.at[pl.ds(i * chunk, chunk)], buf.at[i], sem.at[i]
            ).wait()
            at = pl.multiple_of(i * chunk, chunk)
            out_ref[...] += jnp.dot(
                rows_ref[:, pl.ds(at, chunk)], buf[i], preferred_element_type=jnp.float32
            )
            return carry

        lax.fori_loop(0, steps, body, 0)

    return pl.pallas_call(
        kernel,
        in_specs=[WHOLE] * len(groups) + [pl.BlockSpec(memory_space=pl.ANY)],
        out_specs=[WHOLE, WHOLE],
        out_shape=[
            jax.ShapeDtypeStruct((count, depth), groups[0].dtype),
            jax.ShapeDtypeStruct((count, cols), jnp.float32),
        ],
        scratch_shapes=[
            pltpu.VMEM((pieces, tall, lanes), jnp.float32),
            pltpu.VMEM((steps, chunk, cols), weight.dtype),
            pltpu.SemaphoreType.DMA((steps,)),
        ],
        cost_estimate=pl.CostEstimate(
            flops=2 * count * cols * stop, bytes_accessed=2 * cols * stop, transcendentals=0
        ),
        compiler_params=pltpu.CompilerParams(vmem_limit_bytes=48 * 2**20),
    )(*groups, weight)


def pack_o_z(slot, pieces, downs, up, rows):
    count, tall, lanes = pieces.shape
    rank, depth = downs[0].shape
    span = up.shape[1] // count
    total = count * rows

    def kernel(slot_ref, p_ref, *refs):
        wide_pos = lax.axis_index("wide")
        core, y, z = wide_pos & 1, (wide_pos >> 1) & 1, wide_pos >> 2
        down_refs, up_ref = refs[:4], refs[4]
        out_refs, (wide_ref, rows_ref) = refs[5:9], refs[9:]
        placed = [(z ^ dz, p_ref[dz]) for dz in range(count)]
        strided_rows(wide_ref, rows_ref, placed)
        at = lax.broadcasted_iota(jnp.int32, (total, 1), 0)
        slots = jnp.zeros((total, 1), jnp.int32)
        for r in range(total):
            row = (r // rows * 4 + y * 2 + core) * rows + r % rows
            slots = jnp.where(at == r, slot_ref[row], slots)
        out = jnp.zeros((total, rank), jnp.float32)
        for offset, ref in enumerate(down_refs):
            part = lax.dot_general(
                rows_ref[...], ref[...], (((1,), (1,)), ((), ())),
                preferred_element_type=jnp.float32,
            )
            out = out + jnp.where(slots == (wide_pos ^ offset), part, 0.0)
        for dz, ref in enumerate(out_refs):
            at = pl.multiple_of((z ^ dz) * span, lanes)
            ref[:, :span] = up_ref[:, pl.ds(at, span)]
            ref[:, span:] = jnp.zeros((rank, lanes), ref.dtype)
            for rows_at, at in ((0, span), (rank, span + lanes // 2)):
                left = out[rows_at : min(rows_at + rank, total)]
                for t in range(2):
                    top = left.astype(jnp.bfloat16)
                    ref[: left.shape[0], at + t * rank : at + (t + 1) * rank] = top
                    left = left - top.astype(jnp.float32)

    return pl.pallas_call(
        kernel,
        in_specs=[SCALARS] + [WHOLE] * 6,
        out_specs=[WHOLE] * 4,
        out_shape=[jax.ShapeDtypeStruct((rank, span + lanes), up.dtype)] * 4,
        scratch_shapes=[
            pltpu.VMEM((count, tall, lanes), jnp.float32),
            pltpu.VMEM((total, depth), pieces.dtype),
        ],
        cost_estimate=pl.CostEstimate(
            flops=0, bytes_accessed=4 * total * depth, transcendentals=0
        ),
        compiler_params=pltpu.CompilerParams(vmem_limit_bytes=10 * 2**20),
    )(slot, pieces, *downs, up)


def pack_o_y(parts, total):
    rank = parts[0].shape[0]
    lanes = 128
    span = (parts[0].shape[1] - lanes) // 2

    def kernel(a_ref, b_ref, c_ref, d_ref, away_ref, near_ref, far_ref, sum_ref):
        wide_pos = lax.axis_index("wide")
        core, y = wide_pos & 1, (wide_pos >> 1) & 1
        refs = (a_ref, b_ref, c_ref, d_ref)

        def decoded(ref, rows, at):
            high, low = [
                ref[rows, at + t * rank : at + (t + 1) * rank].astype(jnp.float32)
                for t in range(2)
            ]
            return high + low

        for at, rows in (
            (0, slice(0, rank)),
            (lanes // 2, slice(0, total - rank)),
        ):
            parts_of = [decoded(ref, rows, 2 * span + at) for ref in refs]
            value = (parts_of[0] + parts_of[1]) + (parts_of[2] + parts_of[3])
            sum_ref[pl.ds(0 if at == 0 else rank, value.shape[0]), :] = value
        away_ref[:, span:] = jnp.zeros((4 * rank, lanes), away_ref.dtype)
        left = sum_ref[...]
        for t in range(2):
            top = left.astype(jnp.bfloat16)
            away_ref[:total, span + t * rank : span + (t + 1) * rank] = top
            left = left - top.astype(jnp.float32)

        def write(yb, cb):
            for dz, ref in enumerate(refs):
                rows = slice(dz * rank, (dz + 1) * rank)
                for out, half in ((near_ref, cb), (far_ref, 1 - cb)):
                    lane = yb * span + half * span // 2
                    out[rows, :] = ref[:, lane : lane + span // 2]
                away_ref[rows, :span] = ref[:, (1 - yb) * span : (2 - yb) * span]

        for yb in range(2):
            for cb in range(2):

                @pl.when((y == yb) & (core == cb))
                def _():
                    write(yb, cb)

    dtype = parts[0].dtype
    return pl.pallas_call(
        kernel,
        in_specs=[WHOLE] * 4,
        out_specs=[WHOLE] * 4,
        out_shape=[
            jax.ShapeDtypeStruct((4 * rank, span + lanes), dtype),
            jax.ShapeDtypeStruct((4 * rank, span // 2), dtype),
            jax.ShapeDtypeStruct((4 * rank, span // 2), dtype),
            jax.ShapeDtypeStruct((total, rank), jnp.float32),
        ],
        compiler_params=pltpu.CompilerParams(vmem_limit_bytes=8 * 2**20),
    )(*parts)


def finish(mixed, received, o_rows, slot, ups):
    count, cols = mixed.shape
    half = count // 2
    rank = o_rows.shape[1]
    lanes = 4 * ups[0].shape[0]

    def kernel(m_ref, r_ref, rows_ref, slot_ref, *refs):
        out_ref = refs[-1]
        wide_pos = lax.axis_index("wide")
        at = pl.ds(pl.multiple_of(lax.axis_index("kv") * half, 8), half)
        two = r_ref[:, cols:].astype(jnp.float32)
        total = rows_ref[at, :] + (two[:, :rank] + two[:, rank:])
        lane = lax.broadcasted_iota(jnp.int32, (half, lanes), 1)
        owner = wide_pos ^ (((lane >> 3) & 3) * 4 + ((lane >> 5) & 1) * 2 + (lane >> 6))
        entry = lax.broadcasted_iota(jnp.int32, (rank, lanes), 0)
        to = lax.broadcasted_iota(jnp.int32, (rank, lanes), 1) & (rank - 1)
        chosen = (entry == to).astype(jnp.bfloat16)
        value = jnp.dot(
            total.astype(jnp.bfloat16), chosen, preferred_element_type=jnp.float32
        )
        left = jnp.where(slot_ref[at, :] == owner, value, 0.0).astype(jnp.bfloat16)
        up = jnp.concatenate([ref[...] for ref in refs[:-1]], axis=0)
        change = jnp.dot(left, up, preferred_element_type=jnp.float32)
        base = m_ref[at, :] + r_ref[:, :cols].astype(jnp.float32)
        out_ref[...] = (base + adapter_scale * change).astype(out_ref.dtype)

    return pl.pallas_call(
        kernel,
        in_specs=[WHOLE] * 8,
        out_specs=WHOLE,
        out_shape=jax.ShapeDtypeStruct((half, cols), jnp.bfloat16),
        compiler_params=pltpu.CompilerParams(vmem_limit_bytes=8 * 2**20),
    )(mixed, received, o_rows, slot, *ups)


def in_two(v):
    top = lax.reduce_precision(v, 8, 7)
    return jnp.concatenate([top, v - top], axis=1).astype(jnp.bfloat16)


def from_two(v):
    n = v.shape[1] // 2
    v = v.astype(jnp.float32)
    return v[:, :n] + v[:, n:]


def staged_path(
    hidden_input,
    input_norm_gain,
    joint_projection_weight,
    output_weight,
    key_cache,
    value_cache,
    joint_down_weight,
    query_up_weight,
    key_value_up_weight,
    output_down_weight,
    output_up_weight,
    row_adapter_index,
    adapter_owner_slot,
    lengths,
):
    f32, bf16 = jnp.float32, jnp.bfloat16
    batch = hidden_input.shape[0]
    rows = lengths.shape[0]
    heads = key_cache.shape[1]
    head_dim = key_cache.shape[3]
    rank = query_up_weight.shape[1]
    cols = joint_projection_weight.shape[1]
    out_cols = output_weight.shape[1]
    blocks = cols // head_dim
    group = 2 * blocks - 2
    wide = batch // rows
    kv_pos = lax.axis_index("kv")
    wide_pos = lax.axis_index("wide")
    core = wide_pos & 1
    y = (wide_pos >> 1) & 1
    z = wide_pos >> 2
    right = (z >> 1) == kv_pos

    def is_right(i):
        return ((i % wide) >> 3) == i // wide

    def swap(x, mask, source=None, target=None):
        pairs = [(i, i ^ mask) for i in range(2 * wide)]
        if source is not None:
            pairs = [p for p in pairs if is_right(p[0]) == source]
        if target is not None:
            pairs = [p for p in pairs if is_right(p[1]) == target]
        return lax.ppermute(x, ("kv", "wide"), pairs)

    def pick(x, i, axis=0):
        return lax.dynamic_index_in_dim(x, i, axis, keepdims=False)

    half = batch // 2

    gain = input_norm_gain[None]
    same, flip, small, slot, mine = prepare(
        hidden_input,
        gain,
        joint_down_weight[0].T,
        query_up_weight[0],
        key_value_up_weight[0],
        row_adapter_index[None],
        adapter_owner_slot,
    )
    parts = [same, swap(flip, 4), swap(same, 8), swap(flip, 12)]
    depth = hidden_input.shape[1]
    cut = depth * 5 // 8
    weight = joint_projection_weight
    partial = stream_product(hidden_input, gain, weight, 0, cut, None, None)
    away, ups_near, ups_far, small = pack_y(parts, small, cols)
    away, partial = lax.optimization_barrier((away, partial))
    from_y = swap(away, 2)
    partial = stream_product(hidden_input, gain, weight, cut, depth, partial, away)
    partial, from_y = lax.optimization_barrier((partial, from_y))
    coded = from_y[:, 2 * cols :].reshape(2, 16, 2, 64).transpose(2, 0, 1, 3).reshape(-1, 64)
    small = small + from_two(coded[:batch])
    small = small + swap(small, 1)
    ups_y = from_y[:, : 2 * cols].reshape(-1, 2, cols)
    ups = (
        ups_near,
        pick(ups_y, core, 1),
        swap(ups_far, 1),
        swap(pick(ups_y, 1 - core, 1), 1),
    )
    message = jnp.concatenate([partial.astype(bf16), in_two(small)], axis=1)
    o_down = output_down_weight[0].T
    message, o_down = lax.optimization_barrier((message, o_down))
    from_x = swap(message, 16, target=True)
    o_down_y = swap(o_down, 2)
    merged = merge(partial, small, from_x, ups, slot)

    across = swap(pick(merged, 1 - (z >> 1)), 8, source=True)
    half_rows = jnp.where(right, pick(merged, z >> 1), across)
    beside = swap(pick(half_rows, 1 - (z & 1)), 4)
    near = jnp.stack([pick(half_rows, z & 1), beside])
    span = rows * blocks
    keep = lax.dynamic_slice_in_dim(near, y * 2 * span, 2 * span, 1)
    from_y = swap(lax.dynamic_slice_in_dim(near, (1 - y) * 2 * span, 2 * span, 1), 2)
    near = jnp.stack([keep, from_y])
    far = swap(near, 1)
    near = lax.dynamic_slice_in_dim(near, core * span, span, 2)
    far = lax.dynamic_slice_in_dim(far, core * span, span, 2)
    parts = []
    for first in (jnp.where(core == 0, near, far), jnp.where(core == 0, far, near)):
        at = [pick(first, b ^ y) for b in range(2)]
        parts.append(jnp.stack([pick(v, b ^ (z & 1)) for b in range(2) for v in at]))
    joined = jnp.concatenate(
        [p.reshape(heads, rows, blocks, head_dim) for p in parts], axis=2
    ).astype(f32)
    joined = joined.transpose(1, 0, 2, 3)
    query_vector = rotate(joined[:, :, :group], lengths).astype(bf16)
    fresh_key = rotate(joined[:, :, group], lengths).astype(bf16)
    value_new = joined[:, :, group + 1].astype(bf16)

    inverse_root = jnp.sqrt(f32(head_dim))
    scores = jnp.einsum("rkgd,rkld->rkgl", query_vector, key_cache, preferred_element_type=f32)
    scores = scores / inverse_root
    valid = jnp.arange(key_cache.shape[2], dtype=jnp.int32)[None, :] < lengths[:, None]
    scores = jnp.where(valid[:, None, None, :], scores, -jnp.inf)
    fresh_score = (
        jnp.einsum("rkgd,rkd->rkg", query_vector, fresh_key, preferred_element_type=f32)
        / inverse_root
    )
    top = jnp.maximum(jnp.max(scores, axis=-1), fresh_score)
    expd = jnp.exp(scores - top[..., None])
    exp_new = jnp.exp(fresh_score - top)
    total = jnp.sum(expd, axis=-1) + exp_new
    probs = (expd / total[..., None]).astype(bf16)
    prob_new = (exp_new / total).astype(bf16)
    attended = jnp.einsum("rkgl,rkld->rkgd", probs, value_cache, preferred_element_type=f32)
    attended = (
        attended + prob_new.astype(f32)[..., None] * value_new.astype(f32)[:, :, None, :]
    )
    attended = attended.astype(bf16).reshape(-1, head_dim)

    near = jnp.stack([attended, swap(attended, 4), swap(attended, 8), swap(attended, 12)])
    near_y = swap(near, 2)
    o_downs = (o_down, swap(o_down, 1), o_down_y, swap(o_down_y, 1))
    o_z = pack_o_z(slot[:, 0], near, o_downs, output_up_weight[0], rows)
    near_y, o_z = lax.optimization_barrier((near_y, o_z))
    from_z = [swap(o_z[1], 4), swap(o_z[2], 8), swap(o_z[3], 12)]
    gathered = (near, near_y)
    gathered += tuple(swap(v, 1) for v in gathered)
    first, second = depth * 3 // 8, depth * 3 // 4
    offsets = [(0, 4, 8, 12), (2, 6, 10, 14)]
    offsets += [tuple(v + 1 for v in at) for at in offsets]
    everyone, mixed = ordered_product(gathered, offsets, output_weight, first, rows)
    mixed, from_z = lax.optimization_barrier((mixed, from_z))
    o_away, o_near, o_near_c, o_rows = pack_o_y([o_z[0]] + from_z, 4 * rows)
    o_far = swap(o_away, 2)
    mixed = stream_product(everyone, None, output_weight, first, second, mixed, o_away)
    mixed, o_far = lax.optimization_barrier((mixed, o_far))
    o_rows = jnp.stack([o_rows, from_two(o_far[: 4 * rows, 2 * out_cols :][:, : 2 * rank])])
    o_far_c = lax.dynamic_slice_in_dim(o_far, (1 - core) * out_cols, out_cols, 1)
    o_far_n = lax.dynamic_slice_in_dim(o_far, core * out_cols, out_cols, 1)
    o_ups = (o_near, o_far_n, swap(o_near_c, 1), swap(o_far_c, 1))
    o_rows_c = swap(o_rows, 1)
    mixed = stream_product(everyone, None, output_weight, second, depth, mixed, o_rows)
    o_rows = jnp.stack([o_rows, o_rows_c], axis=1)
    o_rows = jnp.where(y == 0, o_rows, o_rows[::-1])
    o_rows = jnp.where(core == 0, o_rows, o_rows[:, ::-1])
    o_rows = o_rows.reshape(2, 2, 4, rows, rank).transpose(2, 0, 1, 3, 4).reshape(batch, rank)

    give_out = lax.dynamic_slice_in_dim(mixed, (1 - kv_pos) * half, half).astype(bf16)
    o_give = in_two(lax.dynamic_slice_in_dim(o_rows, (1 - kv_pos) * half, half))
    from_x = swap(jnp.concatenate([give_out, o_give], axis=1), 16)
    return finish(mixed, from_x, o_rows, slot, o_ups)


def on_device(*arrays):
    lengths, key_cache, weight = arrays[13], arrays[4], arrays[2]
    batch, rows, heads = arrays[0].shape[0], lengths.shape[0], key_cache.shape[1]
    staged = batch == 16 * rows and heads == 4 and 2 * weight.shape[1] == 18 * key_cache.shape[3]
    return (staged_path if staged else general_path)(*arrays)


def solution(mesh):
    in_specs = (
        P(None, "kv"),
        P("kv"),
        P("kv", "wide"),
        P("kv", "wide"),
        P("wide", "kv", None, None),
        P("wide", "kv", None, None),
        P("wide", "kv", None),
        P("wide", None, "kv"),
        P("wide", None, None, "kv"),
        P("wide", "kv", None),
        P("wide", None, None),
        P(),
        P(),
        P("wide"),
    )
    out_specs = P("kv", "wide")
    return jax.shard_map(
        on_device, mesh=mesh, in_specs=in_specs, out_specs=out_specs, check_vma=False
    )
```

```python
import jax
import jax.numpy as jnp
from jax import lax
from jax.experimental import pallas as pl
from jax.experimental.pallas import tpu as pltpu
from jax.sharding import PartitionSpec as P

MODEL_WIDTH = 16384


rope_base = 500000.0
adapter_scale = 2.0


def rotate(values, positions):
    half = values.shape[-1] // 2
    freq = rope_base ** (-jnp.arange(half, dtype=jnp.float32) * 2.0 / values.shape[-1])
    angle = positions.astype(jnp.float32)[:, None] * freq[None, :]
    array_shape = (angle.shape[0],) + (1,) * (values.ndim - 2) + (half,)
    cosine = jnp.cos(angle).reshape(array_shape)
    sine = jnp.sin(angle).reshape(array_shape)
    first = values[..., :half]
    second = values[..., half:]
    return jnp.concatenate(
        [first * cosine - second * sine, second * cosine + first * sine], axis=-1
    )


def arrange(query_change, key_change, value_change, local_key_value):
    count = query_change.shape[0]
    joined = jnp.concatenate(
        [
            query_change.reshape(count, local_key_value, -1),
            key_change.reshape(count, local_key_value, -1),
            value_change.reshape(count, local_key_value, -1),
        ],
        axis=2,
    )
    return joined.reshape(count, -1)


def general_path(
    hidden_input,
    input_norm_gain,
    joint_projection_weight,
    output_weight,
    key_cache,
    value_cache,
    joint_down_weight,
    query_up_weight,
    key_value_up_weight,
    output_down_weight,
    output_up_weight,
    row_adapter_index,
    adapter_owner_slot,
    lengths,
):
    local_rows = lengths.shape[0]
    local_key_value = key_cache.shape[1]
    head_dim = key_cache.shape[3]
    rank_width = query_up_weight.shape[1]
    wide_pos = lax.axis_index("wide")
    kv_pos = lax.axis_index("kv")
    row_start = wide_pos * local_rows
    table = (
        row_adapter_index[:, None]
        == jnp.arange(adapter_owner_slot.shape[0], dtype=jnp.int32)[None, :]
    )
    row_slot = jnp.sum(jnp.where(table, adapter_owner_slot[None, :], 0), axis=1)
    mine = (row_slot == wide_pos).astype(jnp.float32)
    widened = hidden_input.astype(jnp.float32)
    scaled_hidden = (widened * input_norm_gain[None, :]).astype(jnp.bfloat16)
    partial_sq = jnp.sum(widened * widened, axis=1)
    partial_reduced = jnp.dot(
        scaled_hidden, joint_down_weight[0], preferred_element_type=jnp.float32
    )
    total_sq, reduced_hidden = lax.psum((partial_sq, partial_reduced), "kv")
    scale = lax.rsqrt(total_sq / MODEL_WIDTH + 1e-05)
    shrink_bf = (reduced_hidden * scale[:, None] * mine[:, None]).astype(jnp.bfloat16)
    base_part = jnp.dot(scaled_hidden, joint_projection_weight, preferred_element_type=jnp.float32)
    regrouped = lax.all_to_all(base_part, "wide", split_axis=0, concat_axis=1, tiled=True)
    grouped_heads = lax.psum_scatter(regrouped, "kv", scatter_dimension=1, tiled=True)
    row_scale = lax.dynamic_slice_in_dim(scale, row_start, local_rows)
    grouped_heads = grouped_heads * row_scale[:, None]
    shrinks = lax.all_gather(shrink_bf[None], "wide", axis=0, tiled=True)
    query_sheet = lax.all_gather(query_up_weight, "wide", axis=0, tiled=True)
    key_value_sheet = lax.all_gather(key_value_up_weight, "wide", axis=0, tiled=True)
    own_rows = lax.dynamic_slice_in_dim(shrinks, row_start, local_rows, 1)
    query_change = jnp.einsum(
        "nbr,nrc->bc", own_rows[:, :, :rank_width], query_sheet, preferred_element_type=jnp.float32
    )
    key_change = jnp.einsum(
        "nbr,nrc->bc",
        own_rows[:, :, rank_width : 2 * rank_width],
        key_value_sheet[:, 0],
        preferred_element_type=jnp.float32,
    )
    value_change = jnp.einsum(
        "nbr,nrc->bc",
        own_rows[:, :, 2 * rank_width :],
        key_value_sheet[:, 1],
        preferred_element_type=jnp.float32,
    )
    adapter_change = arrange(query_change, key_change, value_change, local_key_value)
    merged_output = (grouped_heads + adapter_scale * adapter_change).reshape(
        local_rows, local_key_value, -1
    )
    width = merged_output.shape[2] - 2 * head_dim
    heads_per = width // head_dim
    query_vector = rotate(
        merged_output[:, :, :width].reshape(local_rows, local_key_value, heads_per, head_dim),
        lengths,
    ).astype(jnp.bfloat16)
    fresh_key = rotate(merged_output[:, :, width : width + head_dim], lengths).astype(jnp.bfloat16)
    value_new = merged_output[:, :, width + head_dim :].astype(jnp.bfloat16)
    inverse_root = jnp.sqrt(jnp.float32(head_dim))
    scores = (
        jnp.einsum("rkgd,rkld->rkgl", query_vector, key_cache, preferred_element_type=jnp.float32)
        / inverse_root
    )
    valid = jnp.arange(key_cache.shape[2], dtype=jnp.int32)[None, :] < lengths[:, None]
    scores = jnp.where(valid[:, None, None, :], scores, -jnp.inf)
    fresh_score = (
        jnp.einsum("rkgd,rkd->rkg", query_vector, fresh_key, preferred_element_type=jnp.float32)
        / inverse_root
    )
    top = jnp.maximum(jnp.max(scores, axis=-1), fresh_score)
    expd = jnp.exp(scores - top[..., None])
    exp_new = jnp.exp(fresh_score - top)
    total = jnp.sum(expd, axis=-1) + exp_new
    probs = (expd / total[..., None]).astype(jnp.bfloat16)
    prob_new = (exp_new / total).astype(jnp.bfloat16)
    attention_output = jnp.einsum(
        "rkgl,rkld->rkgd", probs, value_cache, preferred_element_type=jnp.float32
    )
    attention_output = (
        attention_output
        + prob_new.astype(jnp.float32)[..., None] * value_new.astype(jnp.float32)[:, :, None, :]
    )
    attention_output = attention_output.astype(jnp.bfloat16).reshape(local_rows, -1)
    out_cols = output_weight.shape[1]
    slice_portion = lax.all_gather(attention_output, "wide", axis=0, tiled=True)
    mixed = jnp.concatenate(
        [
            jnp.dot(slice_portion, output_weight, preferred_element_type=jnp.float32),
            jnp.dot(slice_portion, output_down_weight[0], preferred_element_type=jnp.float32),
        ],
        axis=1,
    )
    output_baseline = lax.psum_scatter(
        mixed[:, :out_cols].astype(jnp.bfloat16), "kv", scatter_dimension=0, tiled=True
    ).astype(jnp.float32)
    output_reduced = lax.psum(mixed[:, out_cols:], "kv")
    block = output_baseline.shape[0]
    own_shrink = lax.dynamic_slice_in_dim(
        output_reduced * mine[:, None], kv_pos * block, block, 0
    ).astype(jnp.bfloat16)
    weight_sheet = output_up_weight[0]
    output_change = lax.psum_scatter(
        jnp.dot(weight_sheet.T, own_shrink.T, preferred_element_type=jnp.float32),
        "wide",
        scatter_dimension=0,
        tiled=True,
    )
    return (output_baseline + adapter_scale * output_change.T).astype(jnp.bfloat16)


WHOLE = pl.BlockSpec(memory_space=pltpu.VMEM)
SCALARS = pl.BlockSpec(memory_space=pltpu.SMEM)


def code_two(ref, at, v):
    width = v.shape[1]
    groups = v.shape[0] // 16
    down = ref.shape[0] // 16
    for g in range(groups):
        rows = slice(g % down * 16, (g % down + 1) * 16)
        left = v[g * 16 : (g + 1) * 16]
        for t in range(2):
            lane = at + (g // down * 2 + t) * width
            top = left.astype(jnp.bfloat16)
            ref[rows, lane : lane + width] = top
            left = left - top.astype(jnp.float32)


def read_two(ref, at, width, groups):
    down = ref.shape[0] // 16
    out = []
    for g in range(groups):
        rows = slice(g % down * 16, (g % down + 1) * 16)
        lane = at + g // down * 2 * width
        part = ref[rows, lane : lane + 2 * width].astype(jnp.float32)
        out.append(part[:, :width] + part[:, width:])
    return jnp.concatenate(out, axis=0)


def prepare(hidden_input, gain, down, query_up, key_value_up, adapters, owners):
    count, width = hidden_input.shape
    entries = down.shape[0]
    rank, heads_width = query_up.shape
    head_dim = 128
    heads = key_value_up.shape[2] // head_dim
    group_width = heads_width // heads
    span = group_width + 2 * head_dim
    chunk = 1024
    quarter = width // 4
    held = (hidden_input, gain, down, query_up, key_value_up)

    def kernel(
        owner_ref, index_ref, x_in, gain_in, down_in, q_in, kv_in,
        same_ref, flip_ref, small_ref, slot_ref, mine_ref,
        x_ref, gain_ref, down_ref, q_ref, kv_ref, sem,
    ):
        def x_copy(i):
            part = (slice(None), pl.ds(i * quarter, quarter))
            return pltpu.make_async_copy(x_in.at[part], x_ref.at[part], sem.at[i])

        pairs = ((gain_in, gain_ref), (down_in, down_ref), (q_in, q_ref), (kv_in, kv_ref))
        copies = [
            pltpu.make_async_copy(src, dst, sem.at[4 + i]) for i, (src, dst) in enumerate(pairs)
        ]
        x_copies = [x_copy(i) for i in range(4)]
        for copy in copies[:2] + x_copies + copies[2:]:
            copy.start()

        wide_pos = lax.axis_index("wide")
        row = lax.broadcasted_iota(jnp.int32, (count, count), 0)
        column = lax.broadcasted_iota(jnp.int32, (count, count), 1)
        across = jnp.where(row == column, index_ref[...].astype(jnp.float32), 0.0)
        index = jnp.sum(across, axis=1, keepdims=True).astype(jnp.int32)
        slot = jnp.zeros((count, 1), jnp.int32)
        for a in range(owners.shape[0]):
            slot = jnp.where(index == a, owner_ref[a], slot)
        slot_ref[...] = slot
        mine = (slot == wide_pos).astype(jnp.float32)
        mine_ref[...] = mine

        for copy in copies[:2]:
            copy.wait()
        total = jnp.zeros((count, 1), jnp.float32)
        for at in range(0, width, chunk):
            part = slice(at, at + chunk)
            if at % quarter == 0:
                x_copies[at // quarter].wait()
            x = x_ref[:, part].astype(jnp.float32)
            total = total + jnp.sum(x * x, axis=1, keepdims=True)
            x_ref[:, part] = (x * gain_ref[:, part]).astype(jnp.bfloat16)
        reduced = lax.dot_general(
            x_ref[...], down_ref[...], (((1,), (1,)), ((), ())),
            preferred_element_type=jnp.float32,
        )
        small_ref[...] = jnp.zeros_like(small_ref)
        small_ref[:, :entries] = reduced * mine
        small_ref[:, entries : entries + 1] = total * mine
        small = small_ref[...]
        for copy in copies[2:]:
            copy.wait()

        low = (wide_pos >> 2) & 1
        for ref, zb in ((same_ref, low), (flip_ref, 1 - low)):
            ref[:, span:] = jnp.zeros((2 * rank, 256), ref.dtype)
            code_two(ref, span, small)
            q = q_ref[:, pl.ds(pl.multiple_of(zb * 2 * group_width, 128), 2 * group_width)]
            ref[:, :group_width] = jnp.concatenate(
                [q[:, :group_width], q[:, group_width:]], axis=0
            )
            for t in range(2):
                kv = kv_ref[t, :, pl.ds(pl.multiple_of(zb * 2 * head_dim, 128), 2 * head_dim)]
                lane = group_width + t * head_dim
                ref[:, lane : lane + head_dim] = jnp.concatenate(
                    [kv[:, :head_dim], kv[:, head_dim:]], axis=0
                )

    message = jax.ShapeDtypeStruct((2 * rank, span + 256), query_up.dtype)
    return pl.pallas_call(
        kernel,
        in_specs=[SCALARS, WHOLE] + [pl.BlockSpec(memory_space=pl.ANY)] * len(held),
        out_specs=[WHOLE] * 5,
        out_shape=[
            message,
            message,
            jax.ShapeDtypeStruct((count, 32), jnp.float32),
            jax.ShapeDtypeStruct((count, 1), jnp.int32),
            jax.ShapeDtypeStruct((count, 1), jnp.float32),
        ],
        scratch_shapes=[pltpu.VMEM(v.shape, v.dtype) for v in held]
        + [pltpu.SemaphoreType.DMA((8,))],
        compiler_params=pltpu.CompilerParams(vmem_limit_bytes=60 * 2**20),
    )(owners, adapters, *held)


def stream_product(rows_in, gain, weight, start, stop, before, marker):
    count, cols = rows_in.shape[0], weight.shape[1]
    chunk = 512
    steps = (stop - start) // chunk
    held = pl.BlockSpec(memory_space=pl.ANY)
    operands, specs = [rows_in, weight], [WHOLE, held]
    for more, spec in ((gain, WHOLE), (marker, held), (before, WHOLE)):
        if more is not None:
            operands += [more]
            specs += [spec]

    def kernel(*refs):
        x_ref, w_ref = refs[:2]
        out_ref, buf, sem = refs[-3:]

        def fetch(i):
            return pltpu.make_async_copy(
                w_ref.at[pl.ds(start + i * chunk, chunk)], buf.at[i], sem.at[i]
            )

        for i in range(steps):
            fetch(i).start()
        if before is None:
            out_ref[...] = jnp.zeros_like(out_ref)
        else:
            out_ref[...] = refs[len(operands) - 1][...]

        def body(i, carry):
            at = pl.multiple_of(start + i * chunk, chunk)
            x = x_ref[:, pl.ds(at, chunk)]
            if gain is not None:
                x = (x.astype(jnp.float32) * refs[2][:, pl.ds(at, chunk)]).astype(jnp.bfloat16)
            fetch(i).wait()
            out_ref[...] += jnp.dot(x, buf[i], preferred_element_type=jnp.float32)
            return carry

        lax.fori_loop(0, steps, body, 0)

    return pl.pallas_call(
        kernel,
        in_specs=specs,
        out_specs=WHOLE,
        out_shape=jax.ShapeDtypeStruct((count, cols), jnp.float32),
        scratch_shapes=[
            pltpu.VMEM((steps, chunk, cols), weight.dtype),
            pltpu.SemaphoreType.DMA((steps,)),
        ],
        cost_estimate=pl.CostEstimate(
            flops=2 * count * cols * (stop - start),
            bytes_accessed=2 * cols * (stop - start),
            transcendentals=0,
        ),
        compiler_params=pltpu.CompilerParams(vmem_limit_bytes=47 * 2**20),
    )(*operands)


def pack_y(parts, small, cols):
    tall = parts[0].shape[0]
    count, entries = small.shape
    rank = tall // 2
    rows = 4 * rank

    def kernel(a_ref, b_ref, c_ref, d_ref, small_ref, away_ref, near_ref, far_ref, sum_ref):
        refs = (a_ref, b_ref, c_ref, d_ref)
        total = small_ref[...]
        for ref in refs[1:]:
            total = total + read_two(ref, 2 * cols, entries, count // 16)
        sum_ref[...] = total
        away_ref[:, 2 * cols :] = jnp.zeros((rows, 128), away_ref.dtype)
        code_two(away_ref, 2 * cols, total)

        wide_pos = lax.axis_index("wide")
        core, y = wide_pos & 1, (wide_pos >> 1) & 1

        def write(yb, cb):
            for out, half in ((near_ref, cb), (far_ref, 1 - cb)):
                out[...] = jnp.concatenate(
                    [
                        ref[yb * rank : (yb + 1) * rank, half * cols : (half + 1) * cols]
                        for ref in refs
                    ],
                    axis=0,
                )
            away_ref[:, : 2 * cols] = jnp.concatenate(
                [ref[(1 - yb) * rank : (2 - yb) * rank, : 2 * cols] for ref in refs], axis=0
            )

        for yb in range(2):
            for cb in range(2):

                @pl.when((y == yb) & (core == cb))
                def _():
                    write(yb, cb)

    dtype = parts[0].dtype
    return pl.pallas_call(
        kernel,
        in_specs=[WHOLE] * 5,
        out_specs=[WHOLE] * 4,
        out_shape=[
            jax.ShapeDtypeStruct((rows, 2 * cols + 128), dtype),
            jax.ShapeDtypeStruct((rows, cols), dtype),
            jax.ShapeDtypeStruct((rows, cols), dtype),
            jax.ShapeDtypeStruct(small.shape, jnp.float32),
        ],
        compiler_params=pltpu.CompilerParams(vmem_limit_bytes=8 * 2**20),
    )(*parts, small)


def merge(partial, small, received, ups, slot):
    count, cols = partial.shape
    lanes = 128
    blocks = cols // lanes
    each = count // 2
    entries = 24
    rank = entries // 3

    def kernel(p_ref, small_ref, r_ref, a_ref, b_ref, c_ref, d_ref, slot_ref, out_ref, acc_ref, tall_ref):
        wide_pos = lax.axis_index("wide")
        other = r_ref[:, cols : cols + 64].astype(jnp.float32)
        small = small_ref[...] + (other[:, :32] + other[:, 32:64])
        scale = lax.rsqrt(small[:, entries : entries + 1] / MODEL_WIDTH + 1e-05)
        shrink = (small * scale).astype(jnp.bfloat16)
        lane = lax.broadcasted_iota(jnp.int32, (count, lanes), 1)
        owner = wide_pos ^ (((lane >> 3) & 3) * 4 + ((lane >> 5) & 1) * 2 + (lane >> 6))
        hit = slot_ref[...] == owner
        entry = lax.broadcasted_iota(jnp.int32, (32, lanes), 0)
        to = lax.broadcasted_iota(jnp.int32, (32, lanes), 1) & (rank - 1)

        def spread(t):
            chosen = (entry == to + t * rank).astype(jnp.bfloat16)
            value = jnp.dot(shrink, chosen, preferred_element_type=jnp.float32)
            return jnp.where(hit, value, 0.0).astype(jnp.bfloat16)

        last = (wide_pos & 1) == 1
        parts = [spread(t) for t in range(3)]
        cut = cols - 2 * lanes
        spans = ((0, cut, parts[0]), (cut, cut + lanes, parts[1]), (cut + lanes, cols, parts[2]))
        for lo, hi, own in spans:
            left = parts[0] if lo == 0 else jnp.where(last, own, parts[0])
            up = jnp.concatenate([ref[:, lo:hi] for ref in (a_ref, b_ref, c_ref, d_ref)], axis=0)
            change = jnp.dot(left, up, preferred_element_type=jnp.float32)
            base = p_ref[:, lo:hi] + r_ref[:, lo:hi].astype(jnp.float32)
            acc_ref[:, lo:hi] = base * scale + adapter_scale * change
        for b in range(blocks):
            tall_ref[pl.ds(b, count, stride=blocks), :] = acc_ref[:, b * lanes : (b + 1) * lanes]
        for a in range(2):
            part = slice(a * each * blocks, (a + 1) * each * blocks)
            out_ref[a] = tall_ref[part, :].astype(out_ref.dtype)

    return pl.pallas_call(
        kernel,
        in_specs=[WHOLE] * 8,
        out_specs=WHOLE,
        out_shape=jax.ShapeDtypeStruct((2, each * blocks, lanes), jnp.bfloat16),
        scratch_shapes=[
            pltpu.VMEM((count, cols), jnp.float32),
            pltpu.VMEM((count * blocks, lanes), jnp.float32),
        ],
        compiler_params=pltpu.CompilerParams(vmem_limit_bytes=12 * 2**20),
    )(partial, small, received, *ups, slot)


def strided_rows(wide_ref, rows_ref, order):
    pieces, tall, lanes = wide_ref.shape
    count, depth = rows_ref.shape
    blocks = depth // lanes
    for at, piece in order:
        wide_ref[at] = piece.astype(jnp.float32)
    flat = wide_ref.reshape(count * blocks, lanes)
    for j in range(blocks):
        rows_ref[:, j * lanes : (j + 1) * lanes] = flat[
            pl.ds(j, count, stride=blocks), :
        ].astype(rows_ref.dtype)


def ordered_product(groups, offsets, weight, stop, rows):
    tall, lanes = groups[0].shape[1:]
    depth, cols = weight.shape
    pieces = sum(len(at) for at in offsets)
    count = pieces * rows
    chunk = 512
    steps = stop // chunk

    def kernel(*refs):
        group_refs, w_ref = refs[: len(groups)], refs[len(groups)]
        rows_ref, out_ref, wide_ref, buf, sem = refs[len(groups) + 1 :]
        wide_pos = lax.axis_index("wide")
        copies = [
            pltpu.make_async_copy(w_ref.at[pl.ds(i * chunk, chunk)], buf.at[i], sem.at[i])
            for i in range(steps)
        ]
        for copy in copies:
            copy.start()
        placed = [
            (wide_pos ^ offset, ref[p])
            for ref, at in zip(group_refs, offsets)
            for p, offset in enumerate(at)
        ]
        strided_rows(wide_ref, rows_ref, placed)
        total = jnp.zeros((count, cols), jnp.float32)
        out_ref[...] = total

        def body(i, carry):
            pltpu.make_async_copy(
                w_ref.at[pl.ds(i * chunk, chunk)], buf.at[i], sem.at[i]
            ).wait()
            at = pl.multiple_of(i * chunk, chunk)
            out_ref[...] += jnp.dot(
                rows_ref[:, pl.ds(at, chunk)], buf[i], preferred_element_type=jnp.float32
            )
            return carry

        lax.fori_loop(0, steps, body, 0)

    return pl.pallas_call(
        kernel,
        in_specs=[WHOLE] * len(groups) + [pl.BlockSpec(memory_space=pl.ANY)],
        out_specs=[WHOLE, WHOLE],
        out_shape=[
            jax.ShapeDtypeStruct((count, depth), groups[0].dtype),
            jax.ShapeDtypeStruct((count, cols), jnp.float32),
        ],
        scratch_shapes=[
            pltpu.VMEM((pieces, tall, lanes), jnp.float32),
            pltpu.VMEM((steps, chunk, cols), weight.dtype),
            pltpu.SemaphoreType.DMA((steps,)),
        ],
        cost_estimate=pl.CostEstimate(
            flops=2 * count * cols * stop, bytes_accessed=2 * cols * stop, transcendentals=0
        ),
        compiler_params=pltpu.CompilerParams(vmem_limit_bytes=48 * 2**20),
    )(*groups, weight)


def pack_o_z(slot, pieces, downs, up, rows):
    count, tall, lanes = pieces.shape
    rank, depth = downs[0].shape
    span = up.shape[1] // count
    total = count * rows

    def kernel(slot_ref, p_ref, *refs):
        wide_pos = lax.axis_index("wide")
        core, y, z = wide_pos & 1, (wide_pos >> 1) & 1, wide_pos >> 2
        down_refs, up_ref = refs[:4], refs[4]
        out_refs, (wide_ref, rows_ref) = refs[5:9], refs[9:]
        placed = [(z ^ dz, p_ref[dz]) for dz in range(count)]
        strided_rows(wide_ref, rows_ref, placed)
        at = lax.broadcasted_iota(jnp.int32, (total, 1), 0)
        slots = jnp.zeros((total, 1), jnp.int32)
        for r in range(total):
            row = (r // rows * 4 + y * 2 + core) * rows + r % rows
            slots = jnp.where(at == r, slot_ref[row], slots)
        out = jnp.zeros((total, rank), jnp.float32)
        for offset, ref in enumerate(down_refs):
            part = lax.dot_general(
                rows_ref[...], ref[...], (((1,), (1,)), ((), ())),
                preferred_element_type=jnp.float32,
            )
            out = out + jnp.where(slots == (wide_pos ^ offset), part, 0.0)
        for dz, ref in enumerate(out_refs):
            at = pl.multiple_of((z ^ dz) * span, lanes)
            ref[:, :span] = up_ref[:, pl.ds(at, span)]
            ref[:, span:] = jnp.zeros((rank, lanes), ref.dtype)
            for rows_at, at in ((0, span), (rank, span + lanes // 2)):
                left = out[rows_at : min(rows_at + rank, total)]
                for t in range(2):
                    top = left.astype(jnp.bfloat16)
                    ref[: left.shape[0], at + t * rank : at + (t + 1) * rank] = top
                    left = left - top.astype(jnp.float32)

    return pl.pallas_call(
        kernel,
        in_specs=[SCALARS] + [WHOLE] * 6,
        out_specs=[WHOLE] * 4,
        out_shape=[jax.ShapeDtypeStruct((rank, span + lanes), up.dtype)] * 4,
        scratch_shapes=[
            pltpu.VMEM((count, tall, lanes), jnp.float32),
            pltpu.VMEM((total, depth), pieces.dtype),
        ],
        cost_estimate=pl.CostEstimate(
            flops=0, bytes_accessed=4 * total * depth, transcendentals=0
        ),
        compiler_params=pltpu.CompilerParams(vmem_limit_bytes=10 * 2**20),
    )(slot, pieces, *downs, up)


def pack_o_y(parts, total):
    rank = parts[0].shape[0]
    lanes = 128
    span = (parts[0].shape[1] - lanes) // 2

    def kernel(a_ref, b_ref, c_ref, d_ref, away_ref, near_ref, far_ref, sum_ref):
        wide_pos = lax.axis_index("wide")
        core, y = wide_pos & 1, (wide_pos >> 1) & 1
        refs = (a_ref, b_ref, c_ref, d_ref)

        def decoded(ref, rows, at):
            high, low = [
                ref[rows, at + t * rank : at + (t + 1) * rank].astype(jnp.float32)
                for t in range(2)
            ]
            return high + low

        for at, rows in (
            (0, slice(0, rank)),
            (lanes // 2, slice(0, total - rank)),
        ):
            parts_of = [decoded(ref, rows, 2 * span + at) for ref in refs]
            value = (parts_of[0] + parts_of[1]) + (parts_of[2] + parts_of[3])
            sum_ref[pl.ds(0 if at == 0 else rank, value.shape[0]), :] = value
        away_ref[:, span:] = jnp.zeros((4 * rank, lanes), away_ref.dtype)
        left = sum_ref[...]
        for t in range(2):
            top = left.astype(jnp.bfloat16)
            away_ref[:total, span + t * rank : span + (t + 1) * rank] = top
            left = left - top.astype(jnp.float32)

        def write(yb, cb):
            for dz, ref in enumerate(refs):
                rows = slice(dz * rank, (dz + 1) * rank)
                for out, half in ((near_ref, cb), (far_ref, 1 - cb)):
                    lane = yb * span + half * span // 2
                    out[rows, :] = ref[:, lane : lane + span // 2]
                away_ref[rows, :span] = ref[:, (1 - yb) * span : (2 - yb) * span]

        for yb in range(2):
            for cb in range(2):

                @pl.when((y == yb) & (core == cb))
                def _():
                    write(yb, cb)

    dtype = parts[0].dtype
    return pl.pallas_call(
        kernel,
        in_specs=[WHOLE] * 4,
        out_specs=[WHOLE] * 4,
        out_shape=[
            jax.ShapeDtypeStruct((4 * rank, span + lanes), dtype),
            jax.ShapeDtypeStruct((4 * rank, span // 2), dtype),
            jax.ShapeDtypeStruct((4 * rank, span // 2), dtype),
            jax.ShapeDtypeStruct((total, rank), jnp.float32),
        ],
        compiler_params=pltpu.CompilerParams(vmem_limit_bytes=8 * 2**20),
    )(*parts)


def finish(mixed, received, o_rows, slot, ups):
    count, cols = mixed.shape
    half = count // 2
    rank = o_rows.shape[1]
    lanes = 4 * ups[0].shape[0]

    def kernel(m_ref, r_ref, rows_ref, slot_ref, *refs):
        out_ref = refs[-1]
        wide_pos = lax.axis_index("wide")
        at = pl.ds(pl.multiple_of(lax.axis_index("kv") * half, 8), half)
        two = r_ref[:, cols:].astype(jnp.float32)
        total = rows_ref[at, :] + (two[:, :rank] + two[:, rank:])
        lane = lax.broadcasted_iota(jnp.int32, (half, lanes), 1)
        owner = wide_pos ^ (((lane >> 3) & 3) * 4 + ((lane >> 5) & 1) * 2 + (lane >> 6))
        entry = lax.broadcasted_iota(jnp.int32, (rank, lanes), 0)
        to = lax.broadcasted_iota(jnp.int32, (rank, lanes), 1) & (rank - 1)
        chosen = (entry == to).astype(jnp.bfloat16)
        value = jnp.dot(
            total.astype(jnp.bfloat16), chosen, preferred_element_type=jnp.float32
        )
        left = jnp.where(slot_ref[at, :] == owner, value, 0.0).astype(jnp.bfloat16)
        up = jnp.concatenate([ref[...] for ref in refs[:-1]], axis=0)
        change = jnp.dot(left, up, preferred_element_type=jnp.float32)
        base = m_ref[at, :] + r_ref[:, :cols].astype(jnp.float32)
        out_ref[...] = (base + adapter_scale * change).astype(out_ref.dtype)

    return pl.pallas_call(
        kernel,
        in_specs=[WHOLE] * 8,
        out_specs=WHOLE,
        out_shape=jax.ShapeDtypeStruct((half, cols), jnp.bfloat16),
        compiler_params=pltpu.CompilerParams(vmem_limit_bytes=8 * 2**20),
    )(mixed, received, o_rows, slot, *ups)


def in_two(v):
    top = lax.reduce_precision(v, 8, 7)
    return jnp.concatenate([top, v - top], axis=1).astype(jnp.bfloat16)


def from_two(v):
    n = v.shape[1] // 2
    v = v.astype(jnp.float32)
    return v[:, :n] + v[:, n:]


def staged_path(
    hidden_input,
    input_norm_gain,
    joint_projection_weight,
    output_weight,
    key_cache,
    value_cache,
    joint_down_weight,
    query_up_weight,
    key_value_up_weight,
    output_down_weight,
    output_up_weight,
    row_adapter_index,
    adapter_owner_slot,
    lengths,
):
    f32, bf16 = jnp.float32, jnp.bfloat16
    batch = hidden_input.shape[0]
    rows = lengths.shape[0]
    heads = key_cache.shape[1]
    head_dim = key_cache.shape[3]
    rank = query_up_weight.shape[1]
    cols = joint_projection_weight.shape[1]
    out_cols = output_weight.shape[1]
    blocks = cols // head_dim
    group = 2 * blocks - 2
    wide = batch // rows
    kv_pos = lax.axis_index("kv")
    wide_pos = lax.axis_index("wide")
    core = wide_pos & 1
    y = (wide_pos >> 1) & 1
    z = wide_pos >> 2
    right = (z >> 1) == kv_pos

    def swap(x, mask):
        return lax.ppermute(x, ("kv", "wide"), [(i, i ^ mask) for i in range(2 * wide)])

    def pick(x, i, axis=0):
        return lax.dynamic_index_in_dim(x, i, axis, keepdims=False)

    half = batch // 2

    gain = input_norm_gain[None]
    same, flip, small, slot, mine = prepare(
        hidden_input,
        gain,
        joint_down_weight[0].T,
        query_up_weight[0],
        key_value_up_weight[0],
        row_adapter_index[None],
        adapter_owner_slot,
    )
    parts = [same, swap(flip, 4), swap(same, 8), swap(flip, 12)]
    depth = hidden_input.shape[1]
    cut = depth * 5 // 8
    weight = joint_projection_weight
    partial = stream_product(hidden_input, gain, weight, 0, cut, None, None)
    away, ups_near, ups_far, small = pack_y(parts, small, cols)
    away, partial = lax.optimization_barrier((away, partial))
    from_y = swap(away, 2)
    partial = stream_product(hidden_input, gain, weight, cut, depth, partial, away)
    partial, from_y = lax.optimization_barrier((partial, from_y))
    coded = from_y[:, 2 * cols :].reshape(2, 16, 2, 64).transpose(2, 0, 1, 3).reshape(-1, 64)
    small = small + from_two(coded[:batch])
    small = small + swap(small, 1)
    ups_y = from_y[:, : 2 * cols].reshape(-1, 2, cols)
    ups = (
        ups_near,
        pick(ups_y, core, 1),
        swap(ups_far, 1),
        swap(pick(ups_y, 1 - core, 1), 1),
    )

    own = lax.dynamic_slice_in_dim(partial, (z >> 1) * half, half)
    away = lax.dynamic_slice_in_dim(partial, (1 - (z >> 1)) * half, half).astype(bf16)
    across = swap(away, 8)
    small_h = lax.dynamic_slice_in_dim(small, (z >> 1) * half, half)
    slot_h = lax.dynamic_slice_in_dim(slot, (z >> 1) * half, half)
    keep = jnp.where(right, own, across.astype(f32))
    message = jnp.where(right, across, own.astype(bf16))
    message = jnp.concatenate([message, in_two(small_h)], axis=1)

    o_down = output_down_weight[0].T
    message, o_down = lax.optimization_barrier((message, o_down))
    from_x = swap(message, 16)
    o_down_y = swap(o_down, 2)
    merged = merge(keep, small_h, from_x, ups, slot_h)

    beside = swap(pick(merged, 1 - (z & 1)), 4)
    near = jnp.stack([pick(merged, z & 1), beside])
    span = rows * blocks
    keep = lax.dynamic_slice_in_dim(near, y * 2 * span, 2 * span, 1)
    from_y = swap(lax.dynamic_slice_in_dim(near, (1 - y) * 2 * span, 2 * span, 1), 2)
    near = jnp.stack([keep, from_y])
    far = swap(near, 1)
    near = lax.dynamic_slice_in_dim(near, core * span, span, 2)
    far = lax.dynamic_slice_in_dim(far, core * span, span, 2)
    parts = []
    for first in (jnp.where(core == 0, near, far), jnp.where(core == 0, far, near)):
        at = [pick(first, b ^ y) for b in range(2)]
        parts.append(jnp.stack([pick(v, b ^ (z & 1)) for b in range(2) for v in at]))
    joined = jnp.concatenate(
        [p.reshape(heads, rows, blocks, head_dim) for p in parts], axis=2
    ).astype(f32)
    joined = joined.transpose(1, 0, 2, 3)
    query_vector = rotate(joined[:, :, :group], lengths).astype(bf16)
    fresh_key = rotate(joined[:, :, group], lengths).astype(bf16)
    value_new = joined[:, :, group + 1].astype(bf16)

    inverse_root = jnp.sqrt(f32(head_dim))
    scores = jnp.einsum("rkgd,rkld->rkgl", query_vector, key_cache, preferred_element_type=f32)
    scores = scores / inverse_root
    valid = jnp.arange(key_cache.shape[2], dtype=jnp.int32)[None, :] < lengths[:, None]
    scores = jnp.where(valid[:, None, None, :], scores, -jnp.inf)
    fresh_score = (
        jnp.einsum("rkgd,rkd->rkg", query_vector, fresh_key, preferred_element_type=f32)
        / inverse_root
    )
    top = jnp.maximum(jnp.max(scores, axis=-1), fresh_score)
    expd = jnp.exp(scores - top[..., None])
    exp_new = jnp.exp(fresh_score - top)
    total = jnp.sum(expd, axis=-1) + exp_new
    probs = (expd / total[..., None]).astype(bf16)
    prob_new = (exp_new / total).astype(bf16)
    attended = jnp.einsum("rkgl,rkld->rkgd", probs, value_cache, preferred_element_type=f32)
    attended = (
        attended + prob_new.astype(f32)[..., None] * value_new.astype(f32)[:, :, None, :]
    )
    attended = attended.astype(bf16).reshape(-1, head_dim)

    near = jnp.stack([attended, swap(attended, 4), swap(attended, 8), swap(attended, 12)])
    near_y = swap(near, 2)
    o_downs = (o_down, swap(o_down, 1), o_down_y, swap(o_down_y, 1))
    o_z = pack_o_z(slot[:, 0], near, o_downs, output_up_weight[0], rows)
    near_y, o_z = lax.optimization_barrier((near_y, o_z))
    from_z = [swap(o_z[1], 4), swap(o_z[2], 8), swap(o_z[3], 12)]
    gathered = (near, near_y)
    gathered += tuple(swap(v, 1) for v in gathered)
    first, second = depth // 2, depth * 7 // 8
    offsets = [(0, 4, 8, 12), (2, 6, 10, 14)]
    offsets += [tuple(v + 1 for v in at) for at in offsets]
    everyone, mixed = ordered_product(gathered, offsets, output_weight, first, rows)
    mixed, from_z = lax.optimization_barrier((mixed, from_z))
    o_away, o_near, o_near_c, o_rows = pack_o_y([o_z[0]] + from_z, 4 * rows)
    o_far = swap(o_away, 2)
    mixed = stream_product(everyone, None, output_weight, first, second, mixed, o_away)
    mixed, o_far = lax.optimization_barrier((mixed, o_far))
    o_rows = jnp.stack([o_rows, from_two(o_far[: 4 * rows, 2 * out_cols :][:, : 2 * rank])])
    o_far_c = lax.dynamic_slice_in_dim(o_far, (1 - core) * out_cols, out_cols, 1)
    o_far_n = lax.dynamic_slice_in_dim(o_far, core * out_cols, out_cols, 1)
    o_ups = (o_near, o_far_n, swap(o_near_c, 1), swap(o_far_c, 1))
    o_rows_c = swap(o_rows, 1)
    mixed = stream_product(everyone, None, output_weight, second, depth, mixed, o_rows)
    o_rows = jnp.stack([o_rows, o_rows_c], axis=1)
    o_rows = jnp.where(y == 0, o_rows, o_rows[::-1])
    o_rows = jnp.where(core == 0, o_rows, o_rows[:, ::-1])
    o_rows = o_rows.reshape(2, 2, 4, rows, rank).transpose(2, 0, 1, 3, 4).reshape(batch, rank)

    give_out = lax.dynamic_slice_in_dim(mixed, (1 - kv_pos) * half, half).astype(bf16)
    o_give = in_two(lax.dynamic_slice_in_dim(o_rows, (1 - kv_pos) * half, half))
    from_x = swap(jnp.concatenate([give_out, o_give], axis=1), 16)
    return finish(mixed, from_x, o_rows, slot, o_ups)


def on_device(*arrays):
    lengths, key_cache, weight = arrays[13], arrays[4], arrays[2]
    batch, rows, heads = arrays[0].shape[0], lengths.shape[0], key_cache.shape[1]
    staged = batch == 16 * rows and heads == 4 and 2 * weight.shape[1] == 18 * key_cache.shape[3]
    return (staged_path if staged else general_path)(*arrays)


def solution(mesh):
    in_specs = (
        P(None, "kv"),
        P("kv"),
        P("kv", "wide"),
        P("kv", "wide"),
        P("wide", "kv", None, None),
        P("wide", "kv", None, None),
        P("wide", "kv", None),
        P("wide", None, "kv"),
        P("wide", None, None, "kv"),
        P("wide", "kv", None),
        P("wide", None, None),
        P(),
        P(),
        P("wide"),
    )
    out_specs = P("kv", "wide")
    return jax.shard_map(
        on_device, mesh=mesh, in_specs=in_specs, out_specs=out_specs, check_vma=False
    )
```

```python
import jax
import jax.numpy as jnp
from jax import lax
from jax.experimental import pallas as pl
from jax.experimental.pallas import tpu as pltpu
from jax.sharding import PartitionSpec as P

MODEL_WIDTH = 16384


rope_base = 500000.0
adapter_scale = 2.0


def rotate(values, positions):
    half = values.shape[-1] // 2
    freq = rope_base ** (-jnp.arange(half, dtype=jnp.float32) * 2.0 / values.shape[-1])
    angle = positions.astype(jnp.float32)[:, None] * freq[None, :]
    array_shape = (angle.shape[0],) + (1,) * (values.ndim - 2) + (half,)
    cosine = jnp.cos(angle).reshape(array_shape)
    sine = jnp.sin(angle).reshape(array_shape)
    first = values[..., :half]
    second = values[..., half:]
    return jnp.concatenate(
        [first * cosine - second * sine, second * cosine + first * sine], axis=-1
    )


def arrange(query_change, key_change, value_change, local_key_value):
    count = query_change.shape[0]
    joined = jnp.concatenate(
        [
            query_change.reshape(count, local_key_value, -1),
            key_change.reshape(count, local_key_value, -1),
            value_change.reshape(count, local_key_value, -1),
        ],
        axis=2,
    )
    return joined.reshape(count, -1)


def general_path(
    hidden_input,
    input_norm_gain,
    joint_projection_weight,
    output_weight,
    key_cache,
    value_cache,
    joint_down_weight,
    query_up_weight,
    key_value_up_weight,
    output_down_weight,
    output_up_weight,
    row_adapter_index,
    adapter_owner_slot,
    lengths,
):
    local_rows = lengths.shape[0]
    local_key_value = key_cache.shape[1]
    head_dim = key_cache.shape[3]
    rank_width = query_up_weight.shape[1]
    wide_pos = lax.axis_index("wide")
    kv_pos = lax.axis_index("kv")
    row_start = wide_pos * local_rows
    table = (
        row_adapter_index[:, None]
        == jnp.arange(adapter_owner_slot.shape[0], dtype=jnp.int32)[None, :]
    )
    row_slot = jnp.sum(jnp.where(table, adapter_owner_slot[None, :], 0), axis=1)
    mine = (row_slot == wide_pos).astype(jnp.float32)
    widened = hidden_input.astype(jnp.float32)
    scaled_hidden = (widened * input_norm_gain[None, :]).astype(jnp.bfloat16)
    partial_sq = jnp.sum(widened * widened, axis=1)
    partial_reduced = jnp.dot(
        scaled_hidden, joint_down_weight[0], preferred_element_type=jnp.float32
    )
    total_sq, reduced_hidden = lax.psum((partial_sq, partial_reduced), "kv")
    scale = lax.rsqrt(total_sq / MODEL_WIDTH + 1e-05)
    shrink_bf = (reduced_hidden * scale[:, None] * mine[:, None]).astype(jnp.bfloat16)
    base_part = jnp.dot(scaled_hidden, joint_projection_weight, preferred_element_type=jnp.float32)
    regrouped = lax.all_to_all(base_part, "wide", split_axis=0, concat_axis=1, tiled=True)
    grouped_heads = lax.psum_scatter(regrouped, "kv", scatter_dimension=1, tiled=True)
    row_scale = lax.dynamic_slice_in_dim(scale, row_start, local_rows)
    grouped_heads = grouped_heads * row_scale[:, None]
    shrinks = lax.all_gather(shrink_bf[None], "wide", axis=0, tiled=True)
    query_sheet = lax.all_gather(query_up_weight, "wide", axis=0, tiled=True)
    key_value_sheet = lax.all_gather(key_value_up_weight, "wide", axis=0, tiled=True)
    own_rows = lax.dynamic_slice_in_dim(shrinks, row_start, local_rows, 1)
    query_change = jnp.einsum(
        "nbr,nrc->bc", own_rows[:, :, :rank_width], query_sheet, preferred_element_type=jnp.float32
    )
    key_change = jnp.einsum(
        "nbr,nrc->bc",
        own_rows[:, :, rank_width : 2 * rank_width],
        key_value_sheet[:, 0],
        preferred_element_type=jnp.float32,
    )
    value_change = jnp.einsum(
        "nbr,nrc->bc",
        own_rows[:, :, 2 * rank_width :],
        key_value_sheet[:, 1],
        preferred_element_type=jnp.float32,
    )
    adapter_change = arrange(query_change, key_change, value_change, local_key_value)
    merged_output = (grouped_heads + adapter_scale * adapter_change).reshape(
        local_rows, local_key_value, -1
    )
    width = merged_output.shape[2] - 2 * head_dim
    heads_per = width // head_dim
    query_vector = rotate(
        merged_output[:, :, :width].reshape(local_rows, local_key_value, heads_per, head_dim),
        lengths,
    ).astype(jnp.bfloat16)
    fresh_key = rotate(merged_output[:, :, width : width + head_dim], lengths).astype(jnp.bfloat16)
    value_new = merged_output[:, :, width + head_dim :].astype(jnp.bfloat16)
    inverse_root = jnp.sqrt(jnp.float32(head_dim))
    scores = (
        jnp.einsum("rkgd,rkld->rkgl", query_vector, key_cache, preferred_element_type=jnp.float32)
        / inverse_root
    )
    valid = jnp.arange(key_cache.shape[2], dtype=jnp.int32)[None, :] < lengths[:, None]
    scores = jnp.where(valid[:, None, None, :], scores, -jnp.inf)
    fresh_score = (
        jnp.einsum("rkgd,rkd->rkg", query_vector, fresh_key, preferred_element_type=jnp.float32)
        / inverse_root
    )
    top = jnp.maximum(jnp.max(scores, axis=-1), fresh_score)
    expd = jnp.exp(scores - top[..., None])
    exp_new = jnp.exp(fresh_score - top)
    total = jnp.sum(expd, axis=-1) + exp_new
    probs = (expd / total[..., None]).astype(jnp.bfloat16)
    prob_new = (exp_new / total).astype(jnp.bfloat16)
    attention_output = jnp.einsum(
        "rkgl,rkld->rkgd", probs, value_cache, preferred_element_type=jnp.float32
    )
    attention_output = (
        attention_output
        + prob_new.astype(jnp.float32)[..., None] * value_new.astype(jnp.float32)[:, :, None, :]
    )
    attention_output = attention_output.astype(jnp.bfloat16).reshape(local_rows, -1)
    out_cols = output_weight.shape[1]
    slice_portion = lax.all_gather(attention_output, "wide", axis=0, tiled=True)
    mixed = jnp.concatenate(
        [
            jnp.dot(slice_portion, output_weight, preferred_element_type=jnp.float32),
            jnp.dot(slice_portion, output_down_weight[0], preferred_element_type=jnp.float32),
        ],
        axis=1,
    )
    output_baseline = lax.psum_scatter(
        mixed[:, :out_cols].astype(jnp.bfloat16), "kv", scatter_dimension=0, tiled=True
    ).astype(jnp.float32)
    output_reduced = lax.psum(mixed[:, out_cols:], "kv")
    block = output_baseline.shape[0]
    own_shrink = lax.dynamic_slice_in_dim(
        output_reduced * mine[:, None], kv_pos * block, block, 0
    ).astype(jnp.bfloat16)
    weight_sheet = output_up_weight[0]
    output_change = lax.psum_scatter(
        jnp.dot(weight_sheet.T, own_shrink.T, preferred_element_type=jnp.float32),
        "wide",
        scatter_dimension=0,
        tiled=True,
    )
    return (output_baseline + adapter_scale * output_change.T).astype(jnp.bfloat16)


WHOLE = pl.BlockSpec(memory_space=pltpu.VMEM)
SCALARS = pl.BlockSpec(memory_space=pltpu.SMEM)


def code_two(ref, at, v):
    width = v.shape[1]
    groups = v.shape[0] // 16
    down = ref.shape[0] // 16
    for g in range(groups):
        rows = slice(g % down * 16, (g % down + 1) * 16)
        left = v[g * 16 : (g + 1) * 16]
        for t in range(2):
            lane = at + (g // down * 2 + t) * width
            top = left.astype(jnp.bfloat16)
            ref[rows, lane : lane + width] = top
            left = left - top.astype(jnp.float32)


def read_two(ref, at, width, groups):
    down = ref.shape[0] // 16
    out = []
    for g in range(groups):
        rows = slice(g % down * 16, (g % down + 1) * 16)
        lane = at + g // down * 2 * width
        part = ref[rows, lane : lane + 2 * width].astype(jnp.float32)
        out.append(part[:, :width] + part[:, width:])
    return jnp.concatenate(out, axis=0)


def prepare(hidden_input, gain, down, query_up, key_value_up, adapters, owners):
    count, width = hidden_input.shape
    entries = down.shape[0]
    rank, heads_width = query_up.shape
    head_dim = 128
    heads = key_value_up.shape[2] // head_dim
    group_width = heads_width // heads
    span = group_width + 2 * head_dim
    chunk = 1024
    quarter = width // 4
    held = (hidden_input, gain, down, query_up, key_value_up, adapters, owners)

    def kernel(
        x_in, gain_in, down_in, q_in, kv_in, index_in, owner_in,
        same_ref, flip_ref, small_ref, slot_ref,
        x_ref, gain_ref, down_ref, q_ref, kv_ref, index_ref, owner_ref, sem,
    ):
        def x_copy(i):
            part = (slice(None), pl.ds(i * quarter, quarter))
            return pltpu.make_async_copy(x_in.at[part], x_ref.at[part], sem.at[i])

        pairs = (
            (index_in, index_ref), (owner_in, owner_ref), (gain_in, gain_ref),
            (down_in, down_ref), (q_in, q_ref), (kv_in, kv_ref),
        )
        copies = [
            pltpu.make_async_copy(src, dst, sem.at[4 + i]) for i, (src, dst) in enumerate(pairs)
        ]
        x_copies = [x_copy(i) for i in range(4)]
        for copy in copies[:3] + x_copies + copies[3:]:
            copy.start()

        wide_pos = lax.axis_index("wide")
        for copy in copies[:3]:
            copy.wait()
        row = lax.broadcasted_iota(jnp.int32, (count, count), 0)
        column = lax.broadcasted_iota(jnp.int32, (count, count), 1)
        across = jnp.where(row == column, index_ref[...].astype(jnp.float32), 0.0)
        index = jnp.sum(across, axis=1, keepdims=True).astype(jnp.int32)
        which = lax.broadcasted_iota(jnp.int32, (count, owners.shape[1]), 1)
        chosen = jnp.where(index == which, owner_ref[...].astype(jnp.float32), 0.0)
        slot = jnp.sum(chosen, axis=1, keepdims=True).astype(jnp.int32)
        slot_ref[...] = slot
        mine = (slot == wide_pos).astype(jnp.float32)

        total = jnp.zeros((count, 1), jnp.float32)
        for at in range(0, width, chunk):
            part = slice(at, at + chunk)
            if at % quarter == 0:
                x_copies[at // quarter].wait()
            x = x_ref[:, part].astype(jnp.float32)
            total = total + jnp.sum(x * x, axis=1, keepdims=True)
            x_ref[:, part] = (x * gain_ref[:, part]).astype(jnp.bfloat16)
        copies[3].wait()
        reduced = lax.dot_general(
            x_ref[...], down_ref[...], (((1,), (1,)), ((), ())),
            preferred_element_type=jnp.float32,
        )
        small_ref[...] = jnp.zeros_like(small_ref)
        small_ref[:, :entries] = reduced * mine
        small_ref[:, entries : entries + 1] = total * mine
        small = small_ref[...]
        for copy in copies[4:]:
            copy.wait()

        low = (wide_pos >> 2) & 1
        for ref, zb in ((same_ref, low), (flip_ref, 1 - low)):
            ref[:, span:] = jnp.zeros((2 * rank, 256), ref.dtype)
            code_two(ref, span, small)
            q = q_ref[:, pl.ds(pl.multiple_of(zb * 2 * group_width, 128), 2 * group_width)]
            ref[:, :group_width] = jnp.concatenate(
                [q[:, :group_width], q[:, group_width:]], axis=0
            )
            for t in range(2):
                kv = kv_ref[t, :, pl.ds(pl.multiple_of(zb * 2 * head_dim, 128), 2 * head_dim)]
                lane = group_width + t * head_dim
                ref[:, lane : lane + head_dim] = jnp.concatenate(
                    [kv[:, :head_dim], kv[:, head_dim:]], axis=0
                )

    message = jax.ShapeDtypeStruct((2 * rank, span + 256), query_up.dtype)
    return pl.pallas_call(
        kernel,
        in_specs=[pl.BlockSpec(memory_space=pl.ANY)] * len(held),
        out_specs=[WHOLE] * 4,
        out_shape=[
            message,
            message,
            jax.ShapeDtypeStruct((count, 32), jnp.float32),
            jax.ShapeDtypeStruct((count, 1), jnp.int32),
        ],
        scratch_shapes=[pltpu.VMEM(v.shape, v.dtype) for v in held]
        + [pltpu.SemaphoreType.DMA((10,))],
        compiler_params=pltpu.CompilerParams(vmem_limit_bytes=60 * 2**20),
    )(*held)


def stream_product(rows_in, gain, weight, start, stop, before, marker):
    count, cols = rows_in.shape[0], weight.shape[1]
    chunk = 512
    steps = (stop - start) // chunk
    held = pl.BlockSpec(memory_space=pl.ANY)
    operands, specs = [rows_in, weight], [WHOLE, held]
    for more, spec in ((gain, WHOLE), (marker, held), (before, WHOLE)):
        if more is not None:
            operands += [more]
            specs += [spec]

    def kernel(*refs):
        x_ref, w_ref = refs[:2]
        out_ref, buf, sem = refs[-3:]

        def fetch(i):
            return pltpu.make_async_copy(
                w_ref.at[pl.ds(start + i * chunk, chunk)], buf.at[i], sem.at[i]
            )

        for i in range(steps):
            fetch(i).start()
        if before is None:
            out_ref[...] = jnp.zeros_like(out_ref)
        else:
            out_ref[...] = refs[len(operands) - 1][...]

        def body(i, carry):
            at = pl.multiple_of(start + i * chunk, chunk)
            x = x_ref[:, pl.ds(at, chunk)]
            if gain is not None:
                x = (x.astype(jnp.float32) * refs[2][:, pl.ds(at, chunk)]).astype(jnp.bfloat16)
            fetch(i).wait()
            out_ref[...] += jnp.dot(x, buf[i], preferred_element_type=jnp.float32)
            return carry

        lax.fori_loop(0, steps, body, 0)

    return pl.pallas_call(
        kernel,
        in_specs=specs,
        out_specs=WHOLE,
        out_shape=jax.ShapeDtypeStruct((count, cols), jnp.float32),
        scratch_shapes=[
            pltpu.VMEM((steps, chunk, cols), weight.dtype),
            pltpu.SemaphoreType.DMA((steps,)),
        ],
        cost_estimate=pl.CostEstimate(
            flops=2 * count * cols * (stop - start),
            bytes_accessed=2 * cols * (stop - start),
            transcendentals=0,
        ),
        compiler_params=pltpu.CompilerParams(vmem_limit_bytes=47 * 2**20),
    )(*operands)


def pack_y(parts, small, cols):
    tall = parts[0].shape[0]
    count, entries = small.shape
    rank = tall // 2
    rows = 4 * rank

    def kernel(a_ref, b_ref, c_ref, d_ref, small_ref, away_ref, near_ref, far_ref, sum_ref):
        refs = (a_ref, b_ref, c_ref, d_ref)
        total = small_ref[...]
        for ref in refs[1:]:
            total = total + read_two(ref, 2 * cols, entries, count // 16)
        sum_ref[...] = total
        away_ref[:, 2 * cols :] = jnp.zeros((rows, 128), away_ref.dtype)
        code_two(away_ref, 2 * cols, total)

        wide_pos = lax.axis_index("wide")
        core, y = wide_pos & 1, (wide_pos >> 1) & 1

        def write(yb, cb):
            for out, half in ((near_ref, cb), (far_ref, 1 - cb)):
                out[...] = jnp.concatenate(
                    [
                        ref[yb * rank : (yb + 1) * rank, half * cols : (half + 1) * cols]
                        for ref in refs
                    ],
                    axis=0,
                )
            away_ref[:, : 2 * cols] = jnp.concatenate(
                [ref[(1 - yb) * rank : (2 - yb) * rank, : 2 * cols] for ref in refs], axis=0
            )

        for yb in range(2):
            for cb in range(2):

                @pl.when((y == yb) & (core == cb))
                def _():
                    write(yb, cb)

    dtype = parts[0].dtype
    return pl.pallas_call(
        kernel,
        in_specs=[WHOLE] * 5,
        out_specs=[WHOLE] * 4,
        out_shape=[
            jax.ShapeDtypeStruct((rows, 2 * cols + 128), dtype),
            jax.ShapeDtypeStruct((rows, cols), dtype),
            jax.ShapeDtypeStruct((rows, cols), dtype),
            jax.ShapeDtypeStruct(small.shape, jnp.float32),
        ],
        compiler_params=pltpu.CompilerParams(vmem_limit_bytes=8 * 2**20),
    )(*parts, small)


def merge(partial, small, received, ups, slot):
    count, cols = partial.shape
    lanes = 128
    blocks = cols // lanes
    each = count // 2
    entries = 24
    rank = entries // 3

    def kernel(p_ref, small_ref, r_ref, a_ref, b_ref, c_ref, d_ref, slot_ref, out_ref, acc_ref, tall_ref):
        wide_pos = lax.axis_index("wide")
        other = r_ref[:, cols : cols + 64].astype(jnp.float32)
        small = small_ref[...] + (other[:, :32] + other[:, 32:64])
        scale = lax.rsqrt(small[:, entries : entries + 1] / MODEL_WIDTH + 1e-05)
        shrink = (small * scale).astype(jnp.bfloat16)
        lane = lax.broadcasted_iota(jnp.int32, (count, lanes), 1)
        owner = wide_pos ^ (((lane >> 3) & 3) * 4 + ((lane >> 5) & 1) * 2 + (lane >> 6))
        hit = slot_ref[...] == owner
        entry = lax.broadcasted_iota(jnp.int32, (32, lanes), 0)
        to = lax.broadcasted_iota(jnp.int32, (32, lanes), 1) & (rank - 1)

        def spread(t):
            chosen = (entry == to + t * rank).astype(jnp.bfloat16)
            value = jnp.dot(shrink, chosen, preferred_element_type=jnp.float32)
            return jnp.where(hit, value, 0.0).astype(jnp.bfloat16)

        last = (wide_pos & 1) == 1
        parts = [spread(t) for t in range(3)]
        cut = cols - 2 * lanes
        spans = ((0, cut, parts[0]), (cut, cut + lanes, parts[1]), (cut + lanes, cols, parts[2]))
        for lo, hi, own in spans:
            left = parts[0] if lo == 0 else jnp.where(last, own, parts[0])
            up = jnp.concatenate([ref[:, lo:hi] for ref in (a_ref, b_ref, c_ref, d_ref)], axis=0)
            change = jnp.dot(left, up, preferred_element_type=jnp.float32)
            base = p_ref[:, lo:hi] + r_ref[:, lo:hi].astype(jnp.float32)
            acc_ref[:, lo:hi] = base * scale + adapter_scale * change
        for b in range(blocks):
            tall_ref[pl.ds(b, count, stride=blocks), :] = acc_ref[:, b * lanes : (b + 1) * lanes]
        tall = each * blocks // 2
        for a in range(4):
            part = slice(a * tall, (a + 1) * tall)
            out_ref[a // 2, a % 2] = tall_ref[part, :].astype(out_ref.dtype)

    return pl.pallas_call(
        kernel,
        in_specs=[WHOLE] * 8,
        out_specs=WHOLE,
        out_shape=jax.ShapeDtypeStruct((2, 2, each * blocks // 2, lanes), jnp.bfloat16),
        scratch_shapes=[
            pltpu.VMEM((count, cols), jnp.float32),
            pltpu.VMEM((count * blocks, lanes), jnp.float32),
        ],
        compiler_params=pltpu.CompilerParams(vmem_limit_bytes=12 * 2**20),
    )(partial, small, received, *ups, slot)


def strided_rows(wide_ref, rows_ref, order):
    pieces, tall, lanes = wide_ref.shape
    count, depth = rows_ref.shape
    blocks = depth // lanes
    for at, piece in order:
        wide_ref[at] = piece.astype(jnp.float32)
    flat = wide_ref.reshape(count * blocks, lanes)
    for j in range(blocks):
        rows_ref[:, j * lanes : (j + 1) * lanes] = flat[
            pl.ds(j, count, stride=blocks), :
        ].astype(rows_ref.dtype)


def ordered_product(groups, offsets, weight, stop, rows):
    tall, lanes = groups[0].shape[1:]
    depth, cols = weight.shape
    pieces = sum(len(at) for at in offsets)
    count = pieces * rows
    chunk = 512
    steps = stop // chunk

    def kernel(*refs):
        group_refs, w_ref = refs[: len(groups)], refs[len(groups)]
        rows_ref, out_ref, wide_ref, buf, sem = refs[len(groups) + 1 :]
        wide_pos = lax.axis_index("wide")
        copies = [
            pltpu.make_async_copy(w_ref.at[pl.ds(i * chunk, chunk)], buf.at[i], sem.at[i])
            for i in range(steps)
        ]
        for copy in copies:
            copy.start()
        placed = [
            (wide_pos ^ offset, ref[p])
            for ref, at in zip(group_refs, offsets)
            for p, offset in enumerate(at)
        ]
        strided_rows(wide_ref, rows_ref, placed)
        total = jnp.zeros((count, cols), jnp.float32)
        out_ref[...] = total

        def body(i, carry):
            pltpu.make_async_copy(
                w_ref.at[pl.ds(i * chunk, chunk)], buf.at[i], sem.at[i]
            ).wait()
            at = pl.multiple_of(i * chunk, chunk)
            out_ref[...] += jnp.dot(
                rows_ref[:, pl.ds(at, chunk)], buf[i], preferred_element_type=jnp.float32
            )
            return carry

        lax.fori_loop(0, steps, body, 0)

    return pl.pallas_call(
        kernel,
        in_specs=[WHOLE] * len(groups) + [pl.BlockSpec(memory_space=pl.ANY)],
        out_specs=[WHOLE, WHOLE],
        out_shape=[
            jax.ShapeDtypeStruct((count, depth), groups[0].dtype),
            jax.ShapeDtypeStruct((count, cols), jnp.float32),
        ],
        scratch_shapes=[
            pltpu.VMEM((pieces, tall, lanes), jnp.float32),
            pltpu.VMEM((steps, chunk, cols), weight.dtype),
            pltpu.SemaphoreType.DMA((steps,)),
        ],
        cost_estimate=pl.CostEstimate(
            flops=2 * count * cols * stop, bytes_accessed=2 * cols * stop, transcendentals=0
        ),
        compiler_params=pltpu.CompilerParams(vmem_limit_bytes=48 * 2**20),
    )(*groups, weight)


def pack_o_z(slot, pieces, downs, up, rows):
    count, tall, lanes = pieces.shape
    rank, depth = downs[0].shape
    span = up.shape[1] // count
    total = count * rows

    def kernel(slot_ref, p_ref, *refs):
        wide_pos = lax.axis_index("wide")
        core, y, z = wide_pos & 1, (wide_pos >> 1) & 1, wide_pos >> 2
        down_refs, up_ref = refs[:4], refs[4]
        out_refs, (wide_ref, rows_ref) = refs[5:9], refs[9:]
        placed = [(z ^ dz, p_ref[dz]) for dz in range(count)]
        strided_rows(wide_ref, rows_ref, placed)
        at = lax.broadcasted_iota(jnp.int32, (total, 1), 0)
        slots = jnp.zeros((total, 1), jnp.int32)
        for r in range(total):
            row = (r // rows * 4 + y * 2 + core) * rows + r % rows
            slots = jnp.where(at == r, slot_ref[row], slots)
        out = jnp.zeros((total, rank), jnp.float32)
        for offset, ref in enumerate(down_refs):
            part = lax.dot_general(
                rows_ref[...], ref[...], (((1,), (1,)), ((), ())),
                preferred_element_type=jnp.float32,
            )
            out = out + jnp.where(slots == (wide_pos ^ offset), part, 0.0)
        for dz, ref in enumerate(out_refs):
            at = pl.multiple_of((z ^ dz) * span, lanes)
            ref[:, :span] = up_ref[:, pl.ds(at, span)]
            ref[:, span:] = jnp.zeros((rank, lanes), ref.dtype)
            for rows_at, at in ((0, span), (rank, span + lanes // 2)):
                left = out[rows_at : min(rows_at + rank, total)]
                for t in range(2):
                    top = left.astype(jnp.bfloat16)
                    ref[: left.shape[0], at + t * rank : at + (t + 1) * rank] = top
                    left = left - top.astype(jnp.float32)

    return pl.pallas_call(
        kernel,
        in_specs=[SCALARS] + [WHOLE] * 6,
        out_specs=[WHOLE] * 4,
        out_shape=[jax.ShapeDtypeStruct((rank, span + lanes), up.dtype)] * 4,
        scratch_shapes=[
            pltpu.VMEM((count, tall, lanes), jnp.float32),
            pltpu.VMEM((total, depth), pieces.dtype),
        ],
        cost_estimate=pl.CostEstimate(
            flops=0, bytes_accessed=4 * total * depth, transcendentals=0
        ),
        compiler_params=pltpu.CompilerParams(vmem_limit_bytes=10 * 2**20),
    )(slot, pieces, *downs, up)


def pack_o_y(parts, total):
    rank = parts[0].shape[0]
    lanes = 128
    span = (parts[0].shape[1] - lanes) // 2

    def kernel(a_ref, b_ref, c_ref, d_ref, away_ref, near_ref, far_ref, sum_ref):
        wide_pos = lax.axis_index("wide")
        core, y = wide_pos & 1, (wide_pos >> 1) & 1
        refs = (a_ref, b_ref, c_ref, d_ref)

        def decoded(ref, rows, at):
            high, low = [
                ref[rows, at + t * rank : at + (t + 1) * rank].astype(jnp.float32)
                for t in range(2)
            ]
            return high + low

        for at, rows in (
            (0, slice(0, rank)),
            (lanes // 2, slice(0, total - rank)),
        ):
            parts_of = [decoded(ref, rows, 2 * span + at) for ref in refs]
            value = (parts_of[0] + parts_of[1]) + (parts_of[2] + parts_of[3])
            sum_ref[pl.ds(0 if at == 0 else rank, value.shape[0]), :] = value
        away_ref[:, span:] = jnp.zeros((4 * rank, lanes), away_ref.dtype)
        left = sum_ref[...]
        for t in range(2):
            top = left.astype(jnp.bfloat16)
            away_ref[:total, span + t * rank : span + (t + 1) * rank] = top
            left = left - top.astype(jnp.float32)

        def write(yb, cb):
            for dz, ref in enumerate(refs):
                rows = slice(dz * rank, (dz + 1) * rank)
                for out, half in ((near_ref, cb), (far_ref, 1 - cb)):
                    lane = yb * span + half * span // 2
                    out[rows, :] = ref[:, lane : lane + span // 2]
                away_ref[rows, :span] = ref[:, (1 - yb) * span : (2 - yb) * span]

        for yb in range(2):
            for cb in range(2):

                @pl.when((y == yb) & (core == cb))
                def _():
                    write(yb, cb)

    dtype = parts[0].dtype
    return pl.pallas_call(
        kernel,
        in_specs=[WHOLE] * 4,
        out_specs=[WHOLE] * 4,
        out_shape=[
            jax.ShapeDtypeStruct((4 * rank, span + lanes), dtype),
            jax.ShapeDtypeStruct((4 * rank, span // 2), dtype),
            jax.ShapeDtypeStruct((4 * rank, span // 2), dtype),
            jax.ShapeDtypeStruct((total, rank), jnp.float32),
        ],
        compiler_params=pltpu.CompilerParams(vmem_limit_bytes=8 * 2**20),
    )(*parts)


def finish(mixed, received, o_rows, slot, ups):
    count, cols = mixed.shape
    half = count // 2
    rank = o_rows.shape[1]
    lanes = 4 * ups[0].shape[0]

    def kernel(m_ref, r_ref, rows_ref, slot_ref, *refs):
        out_ref = refs[-1]
        wide_pos = lax.axis_index("wide")
        at = pl.ds(pl.multiple_of(lax.axis_index("kv") * half, 8), half)
        two = r_ref[:, cols:].astype(jnp.float32)
        total = rows_ref[at, :] + (two[:, :rank] + two[:, rank:])
        lane = lax.broadcasted_iota(jnp.int32, (half, lanes), 1)
        owner = wide_pos ^ (((lane >> 3) & 3) * 4 + ((lane >> 5) & 1) * 2 + (lane >> 6))
        entry = lax.broadcasted_iota(jnp.int32, (rank, lanes), 0)
        to = lax.broadcasted_iota(jnp.int32, (rank, lanes), 1) & (rank - 1)
        chosen = (entry == to).astype(jnp.bfloat16)
        value = jnp.dot(
            total.astype(jnp.bfloat16), chosen, preferred_element_type=jnp.float32
        )
        left = jnp.where(slot_ref[at, :] == owner, value, 0.0).astype(jnp.bfloat16)
        up = jnp.concatenate([ref[...] for ref in refs[:-1]], axis=0)
        change = jnp.dot(left, up, preferred_element_type=jnp.float32)
        base = m_ref[at, :] + r_ref[:, :cols].astype(jnp.float32)
        out_ref[...] = (base + adapter_scale * change).astype(out_ref.dtype)

    return pl.pallas_call(
        kernel,
        in_specs=[WHOLE] * 8,
        out_specs=WHOLE,
        out_shape=jax.ShapeDtypeStruct((half, cols), jnp.bfloat16),
        compiler_params=pltpu.CompilerParams(vmem_limit_bytes=8 * 2**20),
    )(mixed, received, o_rows, slot, *ups)


def in_two(v):
    top = lax.reduce_precision(v, 8, 7)
    return jnp.concatenate([top, v - top], axis=1).astype(jnp.bfloat16)


def from_two(v):
    n = v.shape[1] // 2
    v = v.astype(jnp.float32)
    return v[:, :n] + v[:, n:]


def staged_path(
    hidden_input,
    input_norm_gain,
    joint_projection_weight,
    output_weight,
    key_cache,
    value_cache,
    joint_down_weight,
    query_up_weight,
    key_value_up_weight,
    output_down_weight,
    output_up_weight,
    row_adapter_index,
    adapter_owner_slot,
    lengths,
):
    f32, bf16 = jnp.float32, jnp.bfloat16
    batch = hidden_input.shape[0]
    rows = lengths.shape[0]
    heads = key_cache.shape[1]
    head_dim = key_cache.shape[3]
    rank = query_up_weight.shape[1]
    cols = joint_projection_weight.shape[1]
    out_cols = output_weight.shape[1]
    blocks = cols // head_dim
    group = 2 * blocks - 2
    wide = batch // rows
    kv_pos = lax.axis_index("kv")
    wide_pos = lax.axis_index("wide")
    core = wide_pos & 1
    y = (wide_pos >> 1) & 1
    z = wide_pos >> 2
    right = (z >> 1) == kv_pos

    def swap(x, mask):
        return lax.ppermute(x, ("kv", "wide"), [(i, i ^ mask) for i in range(2 * wide)])

    def pick(x, i, axis=0):
        return lax.dynamic_index_in_dim(x, i, axis, keepdims=False)

    half = batch // 2

    gain = input_norm_gain[None]
    same, flip, small, slot = prepare(
        hidden_input,
        gain,
        joint_down_weight[0].T,
        query_up_weight[0],
        key_value_up_weight[0],
        row_adapter_index[None],
        adapter_owner_slot[None],
    )
    parts = [same, swap(flip, 4), swap(same, 8), swap(flip, 12)]
    depth = hidden_input.shape[1]
    cut = depth * 5 // 8
    weight = joint_projection_weight
    partial = stream_product(hidden_input, gain, weight, 0, cut, None, None)
    away, ups_near, ups_far, small = pack_y(parts, small, cols)
    away, partial = lax.optimization_barrier((away, partial))
    from_y = swap(away, 2)
    partial = stream_product(hidden_input, gain, weight, cut, depth, partial, away)
    partial, from_y = lax.optimization_barrier((partial, from_y))
    coded = from_y[:, 2 * cols :].reshape(2, 16, 2, 64).transpose(2, 0, 1, 3).reshape(-1, 64)
    small = small + from_two(coded[:batch])
    small = small + swap(small, 1)
    ups_y = from_y[:, : 2 * cols].reshape(-1, 2, cols)
    ups = (
        ups_near,
        pick(ups_y, core, 1),
        swap(ups_far, 1),
        swap(pick(ups_y, 1 - core, 1), 1),
    )

    own = lax.dynamic_slice_in_dim(partial, (z >> 1) * half, half)
    away = lax.dynamic_slice_in_dim(partial, (1 - (z >> 1)) * half, half).astype(bf16)
    across = swap(away, 8)
    small_h = lax.dynamic_slice_in_dim(small, (z >> 1) * half, half)
    slot_h = lax.dynamic_slice_in_dim(slot, (z >> 1) * half, half)
    keep = jnp.where(right, own, across.astype(f32))
    message = jnp.where(right, across, own.astype(bf16))
    message = jnp.concatenate([message, in_two(small_h)], axis=1)

    o_down = output_down_weight[0].T
    message, o_down = lax.optimization_barrier((message, o_down))
    from_x = swap(message, 16)
    o_down_y = swap(o_down, 2)
    merged = merge(keep, small_h, from_x, ups, slot_h)

    def rows_of(dz, dy):
        return pick(pick(merged, (z & 1) ^ dz), y ^ dy)

    span = rows * blocks
    near = jnp.stack(
        [rows_of(0, 0), swap(rows_of(1, 0), 4), swap(rows_of(0, 1), 2), swap(rows_of(1, 1), 6)]
    )
    near = near.reshape((2, 2) + near.shape[1:])
    far = swap(near, 1)
    near = lax.dynamic_slice_in_dim(near, core * span, span, 2)
    far = lax.dynamic_slice_in_dim(far, core * span, span, 2)
    parts = []
    for first in (jnp.where(core == 0, near, far), jnp.where(core == 0, far, near)):
        at = [pick(first, b ^ y) for b in range(2)]
        parts.append(jnp.stack([pick(v, b ^ (z & 1)) for b in range(2) for v in at]))
    joined = jnp.concatenate(
        [p.reshape(heads, rows, blocks, head_dim) for p in parts], axis=2
    ).astype(f32)
    joined = joined.transpose(1, 0, 2, 3)
    query_vector = rotate(joined[:, :, :group], lengths).astype(bf16)
    fresh_key = rotate(joined[:, :, group], lengths).astype(bf16)
    value_new = joined[:, :, group + 1].astype(bf16)

    inverse_root = jnp.sqrt(f32(head_dim))
    scores = jnp.einsum("rkgd,rkld->rkgl", query_vector, key_cache, preferred_element_type=f32)
    scores = scores / inverse_root
    valid = jnp.arange(key_cache.shape[2], dtype=jnp.int32)[None, :] < lengths[:, None]
    scores = jnp.where(valid[:, None, None, :], scores, -jnp.inf)
    fresh_score = (
        jnp.einsum("rkgd,rkd->rkg", query_vector, fresh_key, preferred_element_type=f32)
        / inverse_root
    )
    top = jnp.maximum(jnp.max(scores, axis=-1), fresh_score)
    expd = jnp.exp(scores - top[..., None])
    exp_new = jnp.exp(fresh_score - top)
    total = jnp.sum(expd, axis=-1) + exp_new
    probs = (expd / total[..., None]).astype(bf16)
    prob_new = (exp_new / total).astype(bf16)
    attended = jnp.einsum("rkgl,rkld->rkgd", probs, value_cache, preferred_element_type=f32)
    attended = (
        attended + prob_new.astype(f32)[..., None] * value_new.astype(f32)[:, :, None, :]
    )
    attended = attended.astype(bf16).reshape(-1, head_dim)

    near = jnp.stack([attended, swap(attended, 4), swap(attended, 8), swap(attended, 12)])
    near_y = swap(near, 2)
    o_downs = (o_down, swap(o_down, 1), o_down_y, swap(o_down_y, 1))
    o_z = pack_o_z(slot[:, 0], near, o_downs, output_up_weight[0], rows)
    near_y, o_z = lax.optimization_barrier((near_y, o_z))
    from_z = [swap(o_z[1], 4), swap(o_z[2], 8), swap(o_z[3], 12)]
    gathered = (near, near_y)
    gathered += tuple(swap(v, 1) for v in gathered)
    first, second = depth // 2, depth * 7 // 8
    offsets = [(0, 4, 8, 12), (2, 6, 10, 14)]
    offsets += [tuple(v + 1 for v in at) for at in offsets]
    everyone, mixed = ordered_product(gathered, offsets, output_weight, first, rows)
    mixed, from_z = lax.optimization_barrier((mixed, from_z))
    o_away, o_near, o_near_c, o_rows = pack_o_y([o_z[0]] + from_z, 4 * rows)
    o_far = swap(o_away, 2)
    mixed = stream_product(everyone, None, output_weight, first, second, mixed, o_away)
    mixed, o_far = lax.optimization_barrier((mixed, o_far))
    o_rows = jnp.stack([o_rows, from_two(o_far[: 4 * rows, 2 * out_cols :][:, : 2 * rank])])
    o_far_c = lax.dynamic_slice_in_dim(o_far, (1 - core) * out_cols, out_cols, 1)
    o_far_n = lax.dynamic_slice_in_dim(o_far, core * out_cols, out_cols, 1)
    o_ups = (o_near, o_far_n, swap(o_near_c, 1), swap(o_far_c, 1))
    o_rows_c = swap(o_rows, 1)
    mixed = stream_product(everyone, None, output_weight, second, depth, mixed, o_rows)
    o_rows = jnp.stack([o_rows, o_rows_c], axis=1)
    o_rows = jnp.where(y == 0, o_rows, o_rows[::-1])
    o_rows = jnp.where(core == 0, o_rows, o_rows[:, ::-1])
    o_rows = o_rows.reshape(2, 2, 4, rows, rank).transpose(2, 0, 1, 3, 4).reshape(batch, rank)

    give_out = lax.dynamic_slice_in_dim(mixed, (1 - kv_pos) * half, half).astype(bf16)
    o_give = in_two(lax.dynamic_slice_in_dim(o_rows, (1 - kv_pos) * half, half))
    from_x = swap(jnp.concatenate([give_out, o_give], axis=1), 16)
    return finish(mixed, from_x, o_rows, slot, o_ups)


def on_device(*arrays):
    lengths, key_cache, weight = arrays[13], arrays[4], arrays[2]
    batch, rows, heads = arrays[0].shape[0], lengths.shape[0], key_cache.shape[1]
    staged = batch == 16 * rows and heads == 4 and 2 * weight.shape[1] == 18 * key_cache.shape[3]
    return (staged_path if staged else general_path)(*arrays)


def solution(mesh):
    in_specs = (
        P(None, "kv"),
        P("kv"),
        P("kv", "wide"),
        P("kv", "wide"),
        P("wide", "kv", None, None),
        P("wide", "kv", None, None),
        P("wide", "kv", None),
        P("wide", None, "kv"),
        P("wide", None, None, "kv"),
        P("wide", "kv", None),
        P("wide", None, None),
        P(),
        P(),
        P("wide"),
    )
    out_specs = P("kv", "wide")
    return jax.shard_map(
        on_device, mesh=mesh, in_specs=in_specs, out_specs=out_specs, check_vma=False
    )
```

```python
import jax
import jax.numpy as jnp
from jax import lax
from jax.experimental import pallas as pl
from jax.experimental.pallas import tpu as pltpu
from jax.sharding import PartitionSpec as P

MODEL_WIDTH = 16384


rope_base = 500000.0
adapter_scale = 2.0


def rotate(values, positions):
    half = values.shape[-1] // 2
    freq = rope_base ** (-jnp.arange(half, dtype=jnp.float32) * 2.0 / values.shape[-1])
    angle = positions.astype(jnp.float32)[:, None] * freq[None, :]
    array_shape = (angle.shape[0],) + (1,) * (values.ndim - 2) + (half,)
    cosine = jnp.cos(angle).reshape(array_shape)
    sine = jnp.sin(angle).reshape(array_shape)
    first = values[..., :half]
    second = values[..., half:]
    return jnp.concatenate(
        [first * cosine - second * sine, second * cosine + first * sine], axis=-1
    )


def arrange(query_change, key_change, value_change, local_key_value):
    count = query_change.shape[0]
    joined = jnp.concatenate(
        [
            query_change.reshape(count, local_key_value, -1),
            key_change.reshape(count, local_key_value, -1),
            value_change.reshape(count, local_key_value, -1),
        ],
        axis=2,
    )
    return joined.reshape(count, -1)


def general_path(
    hidden_input,
    input_norm_gain,
    joint_projection_weight,
    output_weight,
    key_cache,
    value_cache,
    joint_down_weight,
    query_up_weight,
    key_value_up_weight,
    output_down_weight,
    output_up_weight,
    row_adapter_index,
    adapter_owner_slot,
    lengths,
):
    local_rows = lengths.shape[0]
    local_key_value = key_cache.shape[1]
    head_dim = key_cache.shape[3]
    rank_width = query_up_weight.shape[1]
    wide_pos = lax.axis_index("wide")
    kv_pos = lax.axis_index("kv")
    row_start = wide_pos * local_rows
    table = (
        row_adapter_index[:, None]
        == jnp.arange(adapter_owner_slot.shape[0], dtype=jnp.int32)[None, :]
    )
    row_slot = jnp.sum(jnp.where(table, adapter_owner_slot[None, :], 0), axis=1)
    mine = (row_slot == wide_pos).astype(jnp.float32)
    widened = hidden_input.astype(jnp.float32)
    scaled_hidden = (widened * input_norm_gain[None, :]).astype(jnp.bfloat16)
    partial_sq = jnp.sum(widened * widened, axis=1)
    partial_reduced = jnp.dot(
        scaled_hidden, joint_down_weight[0], preferred_element_type=jnp.float32
    )
    total_sq, reduced_hidden = lax.psum((partial_sq, partial_reduced), "kv")
    scale = lax.rsqrt(total_sq / MODEL_WIDTH + 1e-05)
    shrink_bf = (reduced_hidden * scale[:, None] * mine[:, None]).astype(jnp.bfloat16)
    base_part = jnp.dot(scaled_hidden, joint_projection_weight, preferred_element_type=jnp.float32)
    regrouped = lax.all_to_all(base_part, "wide", split_axis=0, concat_axis=1, tiled=True)
    grouped_heads = lax.psum_scatter(regrouped, "kv", scatter_dimension=1, tiled=True)
    row_scale = lax.dynamic_slice_in_dim(scale, row_start, local_rows)
    grouped_heads = grouped_heads * row_scale[:, None]
    shrinks = lax.all_gather(shrink_bf[None], "wide", axis=0, tiled=True)
    query_sheet = lax.all_gather(query_up_weight, "wide", axis=0, tiled=True)
    key_value_sheet = lax.all_gather(key_value_up_weight, "wide", axis=0, tiled=True)
    own_rows = lax.dynamic_slice_in_dim(shrinks, row_start, local_rows, 1)
    query_change = jnp.einsum(
        "nbr,nrc->bc", own_rows[:, :, :rank_width], query_sheet, preferred_element_type=jnp.float32
    )
    key_change = jnp.einsum(
        "nbr,nrc->bc",
        own_rows[:, :, rank_width : 2 * rank_width],
        key_value_sheet[:, 0],
        preferred_element_type=jnp.float32,
    )
    value_change = jnp.einsum(
        "nbr,nrc->bc",
        own_rows[:, :, 2 * rank_width :],
        key_value_sheet[:, 1],
        preferred_element_type=jnp.float32,
    )
    adapter_change = arrange(query_change, key_change, value_change, local_key_value)
    merged_output = (grouped_heads + adapter_scale * adapter_change).reshape(
        local_rows, local_key_value, -1
    )
    width = merged_output.shape[2] - 2 * head_dim
    heads_per = width // head_dim
    query_vector = rotate(
        merged_output[:, :, :width].reshape(local_rows, local_key_value, heads_per, head_dim),
        lengths,
    ).astype(jnp.bfloat16)
    fresh_key = rotate(merged_output[:, :, width : width + head_dim], lengths).astype(jnp.bfloat16)
    value_new = merged_output[:, :, width + head_dim :].astype(jnp.bfloat16)
    inverse_root = jnp.sqrt(jnp.float32(head_dim))
    scores = (
        jnp.einsum("rkgd,rkld->rkgl", query_vector, key_cache, preferred_element_type=jnp.float32)
        / inverse_root
    )
    valid = jnp.arange(key_cache.shape[2], dtype=jnp.int32)[None, :] < lengths[:, None]
    scores = jnp.where(valid[:, None, None, :], scores, -jnp.inf)
    fresh_score = (
        jnp.einsum("rkgd,rkd->rkg", query_vector, fresh_key, preferred_element_type=jnp.float32)
        / inverse_root
    )
    top = jnp.maximum(jnp.max(scores, axis=-1), fresh_score)
    expd = jnp.exp(scores - top[..., None])
    exp_new = jnp.exp(fresh_score - top)
    total = jnp.sum(expd, axis=-1) + exp_new
    probs = (expd / total[..., None]).astype(jnp.bfloat16)
    prob_new = (exp_new / total).astype(jnp.bfloat16)
    attention_output = jnp.einsum(
        "rkgl,rkld->rkgd", probs, value_cache, preferred_element_type=jnp.float32
    )
    attention_output = (
        attention_output
        + prob_new.astype(jnp.float32)[..., None] * value_new.astype(jnp.float32)[:, :, None, :]
    )
    attention_output = attention_output.astype(jnp.bfloat16).reshape(local_rows, -1)
    out_cols = output_weight.shape[1]
    slice_portion = lax.all_gather(attention_output, "wide", axis=0, tiled=True)
    mixed = jnp.concatenate(
        [
            jnp.dot(slice_portion, output_weight, preferred_element_type=jnp.float32),
            jnp.dot(slice_portion, output_down_weight[0], preferred_element_type=jnp.float32),
        ],
        axis=1,
    )
    output_baseline = lax.psum_scatter(
        mixed[:, :out_cols].astype(jnp.bfloat16), "kv", scatter_dimension=0, tiled=True
    ).astype(jnp.float32)
    output_reduced = lax.psum(mixed[:, out_cols:], "kv")
    block = output_baseline.shape[0]
    own_shrink = lax.dynamic_slice_in_dim(
        output_reduced * mine[:, None], kv_pos * block, block, 0
    ).astype(jnp.bfloat16)
    weight_sheet = output_up_weight[0]
    output_change = lax.psum_scatter(
        jnp.dot(weight_sheet.T, own_shrink.T, preferred_element_type=jnp.float32),
        "wide",
        scatter_dimension=0,
        tiled=True,
    )
    return (output_baseline + adapter_scale * output_change.T).astype(jnp.bfloat16)


WHOLE = pl.BlockSpec(memory_space=pltpu.VMEM)
SCALARS = pl.BlockSpec(memory_space=pltpu.SMEM)


def code_two(ref, at, v):
    width = v.shape[1]
    groups = v.shape[0] // 16
    down = ref.shape[0] // 16
    for g in range(groups):
        rows = slice(g % down * 16, (g % down + 1) * 16)
        left = v[g * 16 : (g + 1) * 16]
        for t in range(2):
            lane = at + (g // down * 2 + t) * width
            top = left.astype(jnp.bfloat16)
            ref[rows, lane : lane + width] = top
            left = left - top.astype(jnp.float32)


def read_two(ref, at, width, groups):
    down = ref.shape[0] // 16
    out = []
    for g in range(groups):
        rows = slice(g % down * 16, (g % down + 1) * 16)
        lane = at + g // down * 2 * width
        part = ref[rows, lane : lane + 2 * width].astype(jnp.float32)
        out.append(part[:, :width] + part[:, width:])
    return jnp.concatenate(out, axis=0)


def prepare(hidden_input, gain, down, query_up, key_value_up, adapters, owners):
    count, width = hidden_input.shape
    entries = down.shape[0]
    rank, heads_width = query_up.shape
    head_dim = 128
    heads = key_value_up.shape[2] // head_dim
    group_width = heads_width // heads
    span = group_width + 2 * head_dim
    chunk = 1024
    quarter = width // 4
    held = (hidden_input, gain, down, query_up, key_value_up, adapters, owners)

    def kernel(
        x_in, gain_in, down_in, q_in, kv_in, index_in, owner_in,
        same_ref, flip_ref, small_ref, slot_ref,
        x_ref, gain_ref, down_ref, q_ref, kv_ref, index_ref, owner_ref, sem,
    ):
        def x_copy(i):
            part = (slice(None), pl.ds(i * quarter, quarter))
            return pltpu.make_async_copy(x_in.at[part], x_ref.at[part], sem.at[i])

        pairs = (
            (index_in, index_ref), (owner_in, owner_ref), (gain_in, gain_ref),
            (down_in, down_ref), (q_in, q_ref), (kv_in, kv_ref),
        )
        copies = [
            pltpu.make_async_copy(src, dst, sem.at[4 + i]) for i, (src, dst) in enumerate(pairs)
        ]
        x_copies = [x_copy(i) for i in range(4)]
        for copy in copies[:3] + x_copies + copies[3:]:
            copy.start()

        wide_pos = lax.axis_index("wide")
        for copy in copies[:3]:
            copy.wait()
        row = lax.broadcasted_iota(jnp.int32, (count, count), 0)
        column = lax.broadcasted_iota(jnp.int32, (count, count), 1)
        across = jnp.where(row == column, index_ref[...].astype(jnp.float32), 0.0)
        index = jnp.sum(across, axis=1, keepdims=True).astype(jnp.int32)
        which = lax.broadcasted_iota(jnp.int32, (count, owners.shape[1]), 1)
        chosen = jnp.where(index == which, owner_ref[...].astype(jnp.float32), 0.0)
        slot = jnp.sum(chosen, axis=1, keepdims=True).astype(jnp.int32)
        slot_ref[...] = slot
        mine = (slot == wide_pos).astype(jnp.float32)

        total = jnp.zeros((count, 1), jnp.float32)
        for at in range(0, width, chunk):
            part = slice(at, at + chunk)
            if at % quarter == 0:
                x_copies[at // quarter].wait()
            x = x_ref[:, part].astype(jnp.float32)
            total = total + jnp.sum(x * x, axis=1, keepdims=True)
            x_ref[:, part] = (x * gain_ref[:, part]).astype(jnp.bfloat16)
        copies[3].wait()
        reduced = lax.dot_general(
            x_ref[...], down_ref[...], (((1,), (1,)), ((), ())),
            preferred_element_type=jnp.float32,
        )
        small_ref[...] = jnp.zeros_like(small_ref)
        small_ref[:, :entries] = reduced * mine
        small_ref[:, entries : entries + 1] = total * mine
        small = small_ref[...]
        for copy in copies[4:]:
            copy.wait()

        low = (wide_pos >> 2) & 1
        for ref, zb in ((same_ref, low), (flip_ref, 1 - low)):
            ref[:, span:] = jnp.zeros((2 * rank, 256), ref.dtype)
            code_two(ref, span, small)
            q = q_ref[:, pl.ds(pl.multiple_of(zb * 2 * group_width, 128), 2 * group_width)]
            ref[:, :group_width] = jnp.concatenate(
                [q[:, :group_width], q[:, group_width:]], axis=0
            )
            for t in range(2):
                kv = kv_ref[t, :, pl.ds(pl.multiple_of(zb * 2 * head_dim, 128), 2 * head_dim)]
                lane = group_width + t * head_dim
                ref[:, lane : lane + head_dim] = jnp.concatenate(
                    [kv[:, :head_dim], kv[:, head_dim:]], axis=0
                )

    message = jax.ShapeDtypeStruct((2 * rank, span + 256), query_up.dtype)
    return pl.pallas_call(
        kernel,
        in_specs=[pl.BlockSpec(memory_space=pl.ANY)] * len(held),
        out_specs=[WHOLE] * 4,
        out_shape=[
            message,
            message,
            jax.ShapeDtypeStruct((count, 32), jnp.float32),
            jax.ShapeDtypeStruct((count, 1), jnp.int32),
        ],
        scratch_shapes=[pltpu.VMEM(v.shape, v.dtype) for v in held]
        + [pltpu.SemaphoreType.DMA((10,))],
        compiler_params=pltpu.CompilerParams(vmem_limit_bytes=60 * 2**20),
    )(*held)


def stream_product(rows_in, gain, weight, start, stop, before, marker):
    count, cols = rows_in.shape[0], weight.shape[1]
    chunk = 512
    steps = (stop - start) // chunk
    held = pl.BlockSpec(memory_space=pl.ANY)
    operands, specs = [rows_in, weight], [WHOLE, held]
    for more, spec in ((gain, WHOLE), (marker, held), (before, WHOLE)):
        if more is not None:
            operands += [more]
            specs += [spec]

    def kernel(*refs):
        x_ref, w_ref = refs[:2]
        out_ref, buf, sem = refs[-3:]

        def fetch(i):
            return pltpu.make_async_copy(
                w_ref.at[pl.ds(start + i * chunk, chunk)], buf.at[i], sem.at[i]
            )

        for i in range(steps):
            fetch(i).start()
        if before is None:
            out_ref[...] = jnp.zeros_like(out_ref)
        else:
            out_ref[...] = refs[len(operands) - 1][...]

        def body(i, carry):
            at = pl.multiple_of(start + i * chunk, chunk)
            x = x_ref[:, pl.ds(at, chunk)]
            if gain is not None:
                x = (x.astype(jnp.float32) * refs[2][:, pl.ds(at, chunk)]).astype(jnp.bfloat16)
            fetch(i).wait()
            out_ref[...] += jnp.dot(x, buf[i], preferred_element_type=jnp.float32)
            return carry

        lax.fori_loop(0, steps, body, 0)

    return pl.pallas_call(
        kernel,
        in_specs=specs,
        out_specs=WHOLE,
        out_shape=jax.ShapeDtypeStruct((count, cols), jnp.float32),
        scratch_shapes=[
            pltpu.VMEM((steps, chunk, cols), weight.dtype),
            pltpu.SemaphoreType.DMA((steps,)),
        ],
        cost_estimate=pl.CostEstimate(
            flops=2 * count * cols * (stop - start),
            bytes_accessed=2 * cols * (stop - start),
            transcendentals=0,
        ),
        compiler_params=pltpu.CompilerParams(vmem_limit_bytes=47 * 2**20),
    )(*operands)


def pack_y(parts, small, cols):
    tall = parts[0].shape[0]
    count, entries = small.shape
    rank = tall // 2
    rows = 4 * rank

    def kernel(a_ref, b_ref, c_ref, d_ref, small_ref, away_ref, near_ref, far_ref, sum_ref):
        refs = (a_ref, b_ref, c_ref, d_ref)
        total = small_ref[...]
        for ref in refs[1:]:
            total = total + read_two(ref, 2 * cols, entries, count // 16)
        sum_ref[...] = total
        away_ref[:, 2 * cols :] = jnp.zeros((rows, 128), away_ref.dtype)
        code_two(away_ref, 2 * cols, total)

        wide_pos = lax.axis_index("wide")
        core, y = wide_pos & 1, (wide_pos >> 1) & 1

        def write(yb, cb):
            for out, half in ((near_ref, cb), (far_ref, 1 - cb)):
                out[...] = jnp.concatenate(
                    [
                        ref[yb * rank : (yb + 1) * rank, half * cols : (half + 1) * cols]
                        for ref in refs
                    ],
                    axis=0,
                )
            away_ref[:, : 2 * cols] = jnp.concatenate(
                [ref[(1 - yb) * rank : (2 - yb) * rank, : 2 * cols] for ref in refs], axis=0
            )

        for yb in range(2):
            for cb in range(2):

                @pl.when((y == yb) & (core == cb))
                def _():
                    write(yb, cb)

    dtype = parts[0].dtype
    return pl.pallas_call(
        kernel,
        in_specs=[WHOLE] * 5,
        out_specs=[WHOLE] * 4,
        out_shape=[
            jax.ShapeDtypeStruct((rows, 2 * cols + 128), dtype),
            jax.ShapeDtypeStruct((rows, cols), dtype),
            jax.ShapeDtypeStruct((rows, cols), dtype),
            jax.ShapeDtypeStruct(small.shape, jnp.float32),
        ],
        compiler_params=pltpu.CompilerParams(vmem_limit_bytes=8 * 2**20),
    )(*parts, small)


def merge(partial, small, received, ups, slot):
    count, cols = partial.shape
    lanes = 128
    blocks = cols // lanes
    each = count // 2
    entries = 24
    rank = entries // 3

    def kernel(p_ref, small_ref, r_ref, a_ref, b_ref, c_ref, d_ref, slot_ref, out_ref, acc_ref, tall_ref):
        wide_pos = lax.axis_index("wide")
        other = r_ref[:, cols : cols + 64].astype(jnp.float32)
        small = small_ref[...] + (other[:, :32] + other[:, 32:64])
        scale = lax.rsqrt(small[:, entries : entries + 1] / MODEL_WIDTH + 1e-05)
        shrink = (small * scale).astype(jnp.bfloat16)
        lane = lax.broadcasted_iota(jnp.int32, (count, lanes), 1)
        owner = wide_pos ^ (((lane >> 3) & 3) * 4 + ((lane >> 5) & 1) * 2 + (lane >> 6))
        hit = slot_ref[...] == owner
        entry = lax.broadcasted_iota(jnp.int32, (32, lanes), 0)
        to = lax.broadcasted_iota(jnp.int32, (32, lanes), 1) & (rank - 1)

        def spread(t):
            chosen = (entry == to + t * rank).astype(jnp.bfloat16)
            value = jnp.dot(shrink, chosen, preferred_element_type=jnp.float32)
            return jnp.where(hit, value, 0.0).astype(jnp.bfloat16)

        last = (wide_pos & 1) == 1
        parts = [spread(t) for t in range(3)]
        cut = cols - 2 * lanes
        spans = ((0, cut, parts[0]), (cut, cut + lanes, parts[1]), (cut + lanes, cols, parts[2]))
        for lo, hi, own in spans:
            left = parts[0] if lo == 0 else jnp.where(last, own, parts[0])
            up = jnp.concatenate([ref[:, lo:hi] for ref in (a_ref, b_ref, c_ref, d_ref)], axis=0)
            change = jnp.dot(left, up, preferred_element_type=jnp.float32)
            base = p_ref[:, lo:hi] + r_ref[:, lo:hi].astype(jnp.float32)
            acc_ref[:, lo:hi] = base * scale + adapter_scale * change
        for b in range(blocks):
            tall_ref[pl.ds(b, count, stride=blocks), :] = acc_ref[:, b * lanes : (b + 1) * lanes]
        tall = each * blocks // 2
        for a in range(4):
            part = slice(a * tall, (a + 1) * tall)
            out_ref[a // 2, a % 2] = tall_ref[part, :].astype(out_ref.dtype)

    return pl.pallas_call(
        kernel,
        in_specs=[WHOLE] * 8,
        out_specs=WHOLE,
        out_shape=jax.ShapeDtypeStruct((2, 2, each * blocks // 2, lanes), jnp.bfloat16),
        scratch_shapes=[
            pltpu.VMEM((count, cols), jnp.float32),
            pltpu.VMEM((count * blocks, lanes), jnp.float32),
        ],
        compiler_params=pltpu.CompilerParams(vmem_limit_bytes=12 * 2**20),
    )(partial, small, received, *ups, slot)


def strided_rows(wide_ref, rows_ref, order):
    pieces, tall, lanes = wide_ref.shape
    count, depth = rows_ref.shape
    blocks = depth // lanes
    for at, piece in order:
        wide_ref[at] = piece.astype(jnp.float32)
    flat = wide_ref.reshape(count * blocks, lanes)
    for j in range(blocks):
        rows_ref[:, j * lanes : (j + 1) * lanes] = flat[
            pl.ds(j, count, stride=blocks), :
        ].astype(rows_ref.dtype)


def ordered_product(groups, offsets, weight, stop, rows):
    tall, lanes = groups[0].shape[1:]
    depth, cols = weight.shape
    pieces = sum(len(at) for at in offsets)
    count = pieces * rows
    chunk = 512
    steps = stop // chunk

    def kernel(*refs):
        group_refs, w_ref = refs[: len(groups)], refs[len(groups)]
        rows_ref, out_ref, wide_ref, buf, sem = refs[len(groups) + 1 :]
        wide_pos = lax.axis_index("wide")
        copies = [
            pltpu.make_async_copy(w_ref.at[pl.ds(i * chunk, chunk)], buf.at[i], sem.at[i])
            for i in range(steps)
        ]
        for copy in copies:
            copy.start()
        placed = [
            (wide_pos ^ offset, ref[p])
            for ref, at in zip(group_refs, offsets)
            for p, offset in enumerate(at)
        ]
        strided_rows(wide_ref, rows_ref, placed)
        total = jnp.zeros((count, cols), jnp.float32)
        out_ref[...] = total

        def body(i, carry):
            pltpu.make_async_copy(
                w_ref.at[pl.ds(i * chunk, chunk)], buf.at[i], sem.at[i]
            ).wait()
            at = pl.multiple_of(i * chunk, chunk)
            out_ref[...] += jnp.dot(
                rows_ref[:, pl.ds(at, chunk)], buf[i], preferred_element_type=jnp.float32
            )
            return carry

        lax.fori_loop(0, steps, body, 0)

    return pl.pallas_call(
        kernel,
        in_specs=[WHOLE] * len(groups) + [pl.BlockSpec(memory_space=pl.ANY)],
        out_specs=[WHOLE, WHOLE],
        out_shape=[
            jax.ShapeDtypeStruct((count, depth), groups[0].dtype),
            jax.ShapeDtypeStruct((count, cols), jnp.float32),
        ],
        scratch_shapes=[
            pltpu.VMEM((pieces, tall, lanes), jnp.float32),
            pltpu.VMEM((steps, chunk, cols), weight.dtype),
            pltpu.SemaphoreType.DMA((steps,)),
        ],
        cost_estimate=pl.CostEstimate(
            flops=2 * count * cols * stop, bytes_accessed=2 * cols * stop, transcendentals=0
        ),
        compiler_params=pltpu.CompilerParams(vmem_limit_bytes=48 * 2**20),
    )(*groups, weight)


def pack_o_z(slot, pieces, downs, up, rows):
    count, tall, lanes = pieces.shape
    rank, depth = downs[0].shape
    span = up.shape[1] // count
    total = count * rows

    def kernel(slot_ref, p_ref, *refs):
        wide_pos = lax.axis_index("wide")
        core, y, z = wide_pos & 1, (wide_pos >> 1) & 1, wide_pos >> 2
        down_refs, up_ref = refs[:4], refs[4]
        out_refs, (wide_ref, rows_ref) = refs[5:9], refs[9:]
        placed = [(z ^ dz, p_ref[dz]) for dz in range(count)]
        strided_rows(wide_ref, rows_ref, placed)
        at = lax.broadcasted_iota(jnp.int32, (total, 1), 0)
        slots = jnp.zeros((total, 1), jnp.int32)
        for r in range(total):
            row = (r // rows * 4 + y * 2 + core) * rows + r % rows
            slots = jnp.where(at == r, slot_ref[row], slots)
        out = jnp.zeros((total, rank), jnp.float32)
        for offset, ref in enumerate(down_refs):
            part = lax.dot_general(
                rows_ref[...], ref[...], (((1,), (1,)), ((), ())),
                preferred_element_type=jnp.float32,
            )
            out = out + jnp.where(slots == (wide_pos ^ offset), part, 0.0)
        for dz, ref in enumerate(out_refs):
            at = pl.multiple_of((z ^ dz) * span, lanes)
            ref[:, :span] = up_ref[:, pl.ds(at, span)]
            ref[:, span:] = jnp.zeros((rank, lanes), ref.dtype)
            for rows_at, at in ((0, span), (rank, span + lanes // 2)):
                left = out[rows_at : min(rows_at + rank, total)]
                for t in range(2):
                    top = left.astype(jnp.bfloat16)
                    ref[: left.shape[0], at + t * rank : at + (t + 1) * rank] = top
                    left = left - top.astype(jnp.float32)

    return pl.pallas_call(
        kernel,
        in_specs=[SCALARS] + [WHOLE] * 6,
        out_specs=[WHOLE] * 4,
        out_shape=[jax.ShapeDtypeStruct((rank, span + lanes), up.dtype)] * 4,
        scratch_shapes=[
            pltpu.VMEM((count, tall, lanes), jnp.float32),
            pltpu.VMEM((total, depth), pieces.dtype),
        ],
        cost_estimate=pl.CostEstimate(
            flops=0, bytes_accessed=4 * total * depth, transcendentals=0
        ),
        compiler_params=pltpu.CompilerParams(vmem_limit_bytes=10 * 2**20),
    )(slot, pieces, *downs, up)


def pack_o_y(parts, total):
    rank = parts[0].shape[0]
    lanes = 128
    span = (parts[0].shape[1] - lanes) // 2

    def kernel(a_ref, b_ref, c_ref, d_ref, away_ref, near_ref, far_ref, sum_ref):
        wide_pos = lax.axis_index("wide")
        core, y = wide_pos & 1, (wide_pos >> 1) & 1
        refs = (a_ref, b_ref, c_ref, d_ref)

        def decoded(ref, rows, at):
            high, low = [
                ref[rows, at + t * rank : at + (t + 1) * rank].astype(jnp.float32)
                for t in range(2)
            ]
            return high + low

        for at, rows in (
            (0, slice(0, rank)),
            (lanes // 2, slice(0, total - rank)),
        ):
            parts_of = [decoded(ref, rows, 2 * span + at) for ref in refs]
            value = (parts_of[0] + parts_of[1]) + (parts_of[2] + parts_of[3])
            sum_ref[pl.ds(0 if at == 0 else rank, value.shape[0]), :] = value
        away_ref[:, span:] = jnp.zeros((4 * rank, lanes), away_ref.dtype)
        left = sum_ref[...]
        for t in range(2):
            top = left.astype(jnp.bfloat16)
            away_ref[:total, span + t * rank : span + (t + 1) * rank] = top
            left = left - top.astype(jnp.float32)

        def write(yb, cb):
            for dz, ref in enumerate(refs):
                rows = slice(dz * rank, (dz + 1) * rank)
                for out, half in ((near_ref, cb), (far_ref, 1 - cb)):
                    lane = yb * span + half * span // 2
                    out[rows, :] = ref[:, lane : lane + span // 2]
                away_ref[rows, :span] = ref[:, (1 - yb) * span : (2 - yb) * span]

        for yb in range(2):
            for cb in range(2):

                @pl.when((y == yb) & (core == cb))
                def _():
                    write(yb, cb)

    dtype = parts[0].dtype
    return pl.pallas_call(
        kernel,
        in_specs=[WHOLE] * 4,
        out_specs=[WHOLE] * 4,
        out_shape=[
            jax.ShapeDtypeStruct((4 * rank, span + lanes), dtype),
            jax.ShapeDtypeStruct((4 * rank, span // 2), dtype),
            jax.ShapeDtypeStruct((4 * rank, span // 2), dtype),
            jax.ShapeDtypeStruct((total, rank), jnp.float32),
        ],
        compiler_params=pltpu.CompilerParams(vmem_limit_bytes=8 * 2**20),
    )(*parts)


def finish(mixed, received, o_rows, slot, ups):
    count, cols = mixed.shape
    half = count // 2
    rank = o_rows.shape[1]
    lanes = 4 * ups[0].shape[0]

    def kernel(m_ref, r_ref, rows_ref, slot_ref, *refs):
        out_ref = refs[-1]
        wide_pos = lax.axis_index("wide")
        at = pl.ds(pl.multiple_of(lax.axis_index("kv") * half, 8), half)
        two = r_ref[:, cols:].astype(jnp.float32)
        total = rows_ref[at, :] + (two[:, :rank] + two[:, rank:])
        lane = lax.broadcasted_iota(jnp.int32, (half, lanes), 1)
        owner = wide_pos ^ (((lane >> 3) & 3) * 4 + ((lane >> 5) & 1) * 2 + (lane >> 6))
        entry = lax.broadcasted_iota(jnp.int32, (rank, lanes), 0)
        to = lax.broadcasted_iota(jnp.int32, (rank, lanes), 1) & (rank - 1)
        chosen = (entry == to).astype(jnp.bfloat16)
        value = jnp.dot(
            total.astype(jnp.bfloat16), chosen, preferred_element_type=jnp.float32
        )
        left = jnp.where(slot_ref[at, :] == owner, value, 0.0).astype(jnp.bfloat16)
        up = jnp.concatenate([ref[...] for ref in refs[:-1]], axis=0)
        change = jnp.dot(left, up, preferred_element_type=jnp.float32)
        base = m_ref[at, :] + r_ref[:, :cols].astype(jnp.float32)
        out_ref[...] = (base + adapter_scale * change).astype(out_ref.dtype)

    return pl.pallas_call(
        kernel,
        in_specs=[WHOLE] * 8,
        out_specs=WHOLE,
        out_shape=jax.ShapeDtypeStruct((half, cols), jnp.bfloat16),
        compiler_params=pltpu.CompilerParams(vmem_limit_bytes=8 * 2**20),
    )(mixed, received, o_rows, slot, *ups)


def in_two(v):
    top = lax.reduce_precision(v, 8, 7)
    return jnp.concatenate([top, v - top], axis=1).astype(jnp.bfloat16)


def from_two(v):
    n = v.shape[1] // 2
    v = v.astype(jnp.float32)
    return v[:, :n] + v[:, n:]


def staged_path(
    hidden_input,
    input_norm_gain,
    joint_projection_weight,
    output_weight,
    key_cache,
    value_cache,
    joint_down_weight,
    query_up_weight,
    key_value_up_weight,
    output_down_weight,
    output_up_weight,
    row_adapter_index,
    adapter_owner_slot,
    lengths,
):
    f32, bf16 = jnp.float32, jnp.bfloat16
    batch = hidden_input.shape[0]
    rows = lengths.shape[0]
    heads = key_cache.shape[1]
    head_dim = key_cache.shape[3]
    rank = query_up_weight.shape[1]
    cols = joint_projection_weight.shape[1]
    out_cols = output_weight.shape[1]
    blocks = cols // head_dim
    group = 2 * blocks - 2
    wide = batch // rows
    kv_pos = lax.axis_index("kv")
    wide_pos = lax.axis_index("wide")
    core = wide_pos & 1
    y = (wide_pos >> 1) & 1
    z = wide_pos >> 2
    right = (z >> 1) == kv_pos

    def swap(x, mask):
        return lax.ppermute(x, ("kv", "wide"), [(i, i ^ mask) for i in range(2 * wide)])

    def pick(x, i, axis=0):
        return lax.dynamic_index_in_dim(x, i, axis, keepdims=False)

    half = batch // 2

    gain = input_norm_gain[None]
    same, flip, small, slot = prepare(
        hidden_input,
        gain,
        joint_down_weight[0].T,
        query_up_weight[0],
        key_value_up_weight[0],
        row_adapter_index[None],
        adapter_owner_slot[None],
    )
    parts = [same, swap(flip, 4), swap(same, 8), swap(flip, 12)]
    depth = hidden_input.shape[1]
    cut = depth * 5 // 8
    weight = joint_projection_weight
    partial = stream_product(hidden_input, gain, weight, 0, cut, None, None)
    away, ups_near, ups_far, small = pack_y(parts, small, cols)
    away, partial = lax.optimization_barrier((away, partial))
    from_y = swap(away, 2)
    partial = stream_product(hidden_input, gain, weight, cut, depth, partial, away)
    partial, from_y = lax.optimization_barrier((partial, from_y))
    coded = from_y[:, 2 * cols :].reshape(2, 16, 2, 64).transpose(2, 0, 1, 3).reshape(-1, 64)
    small = small + from_two(coded[:batch])
    small = small + swap(small, 1)

    own = lax.dynamic_slice_in_dim(partial, (z >> 1) * half, half)
    away = lax.dynamic_slice_in_dim(partial, (1 - (z >> 1)) * half, half).astype(bf16)
    across = swap(away, 8)
    small_h = lax.dynamic_slice_in_dim(small, (z >> 1) * half, half)
    slot_h = lax.dynamic_slice_in_dim(slot, (z >> 1) * half, half)
    keep = jnp.where(right, own, across.astype(f32))
    message = jnp.where(right, across, own.astype(bf16))
    message = jnp.concatenate([message, in_two(small_h)], axis=1)

    o_down = output_down_weight[0].T
    message, o_down, ups_far, from_y = lax.optimization_barrier(
        (message, o_down, ups_far, from_y)
    )
    ups = (
        ups_near,
        lax.dynamic_slice_in_dim(from_y, core * cols, cols, 1),
        swap(ups_far, 1),
        swap(lax.dynamic_slice_in_dim(from_y, (1 - core) * cols, cols, 1), 1),
    )
    from_x = swap(message, 16)
    o_down_y = swap(o_down, 2)
    merged = merge(keep, small_h, from_x, ups, slot_h)

    def rows_of(dz, dy):
        return pick(pick(merged, (z & 1) ^ dz), y ^ dy)

    span = rows * blocks
    near = jnp.stack(
        [rows_of(0, 0), swap(rows_of(1, 0), 4), swap(rows_of(0, 1), 2), swap(rows_of(1, 1), 6)]
    )
    near = near.reshape((2, 2) + near.shape[1:])
    far = swap(near, 1)
    near = lax.dynamic_slice_in_dim(near, core * span, span, 2)
    far = lax.dynamic_slice_in_dim(far, core * span, span, 2)
    parts = []
    for first in (jnp.where(core == 0, near, far), jnp.where(core == 0, far, near)):
        at = [pick(first, b ^ y) for b in range(2)]
        parts.append(jnp.stack([pick(v, b ^ (z & 1)) for b in range(2) for v in at]))
    joined = jnp.concatenate(
        [p.reshape(heads, rows, blocks, head_dim) for p in parts], axis=2
    ).astype(f32)
    joined = joined.transpose(1, 0, 2, 3)
    query_vector = rotate(joined[:, :, :group], lengths).astype(bf16)
    fresh_key = rotate(joined[:, :, group], lengths).astype(bf16)
    value_new = joined[:, :, group + 1].astype(bf16)

    inverse_root = jnp.sqrt(f32(head_dim))
    scores = jnp.einsum("rkgd,rkld->rkgl", query_vector, key_cache, preferred_element_type=f32)
    scores = scores / inverse_root
    valid = jnp.arange(key_cache.shape[2], dtype=jnp.int32)[None, :] < lengths[:, None]
    scores = jnp.where(valid[:, None, None, :], scores, -jnp.inf)
    fresh_score = (
        jnp.einsum("rkgd,rkd->rkg", query_vector, fresh_key, preferred_element_type=f32)
        / inverse_root
    )
    top = jnp.maximum(jnp.max(scores, axis=-1), fresh_score)
    expd = jnp.exp(scores - top[..., None])
    exp_new = jnp.exp(fresh_score - top)
    total = jnp.sum(expd, axis=-1) + exp_new
    probs = (expd / total[..., None]).astype(bf16)
    prob_new = (exp_new / total).astype(bf16)
    attended = jnp.einsum("rkgl,rkld->rkgd", probs, value_cache, preferred_element_type=f32)
    attended = (
        attended + prob_new.astype(f32)[..., None] * value_new.astype(f32)[:, :, None, :]
    )
    attended = attended.astype(bf16).reshape(-1, head_dim)

    near = jnp.stack([attended, swap(attended, 4), swap(attended, 8), swap(attended, 12)])
    near_y = swap(near, 2)
    o_downs = (o_down, swap(o_down, 1), o_down_y, swap(o_down_y, 1))
    o_z = pack_o_z(slot[:, 0], near, o_downs, output_up_weight[0], rows)
    near_y, o_z = lax.optimization_barrier((near_y, o_z))
    from_z = [swap(o_z[1], 4), swap(o_z[2], 8), swap(o_z[3], 12)]
    gathered = (near, near_y)
    gathered += tuple(swap(v, 1) for v in gathered)
    first, second = depth // 2, depth * 7 // 8
    offsets = [(0, 4, 8, 12), (2, 6, 10, 14)]
    offsets += [tuple(v + 1 for v in at) for at in offsets]
    everyone, mixed = ordered_product(gathered, offsets, output_weight, first, rows)
    mixed, from_z = lax.optimization_barrier((mixed, from_z))
    o_away, o_near, o_near_c, o_rows = pack_o_y([o_z[0]] + from_z, 4 * rows)
    o_far = swap(o_away, 2)
    mixed = stream_product(everyone, None, output_weight, first, second, mixed, o_away)
    mixed, o_far = lax.optimization_barrier((mixed, o_far))
    o_rows = jnp.stack([o_rows, from_two(o_far[: 4 * rows, 2 * out_cols :][:, : 2 * rank])])
    o_far_c = lax.dynamic_slice_in_dim(o_far, (1 - core) * out_cols, out_cols, 1)
    o_far_n = lax.dynamic_slice_in_dim(o_far, core * out_cols, out_cols, 1)
    o_near_c = swap(o_near_c, 1)
    o_rows_c = swap(o_rows, 1)
    mixed = stream_product(everyone, None, output_weight, second, depth, mixed, o_rows)
    o_rows = jnp.stack([o_rows, o_rows_c], axis=1)
    o_rows = jnp.where(y == 0, o_rows, o_rows[::-1])
    o_rows = jnp.where(core == 0, o_rows, o_rows[:, ::-1])
    o_rows = o_rows.reshape(2, 2, 4, rows, rank).transpose(2, 0, 1, 3, 4).reshape(batch, rank)

    give_out = lax.dynamic_slice_in_dim(mixed, (1 - kv_pos) * half, half).astype(bf16)
    o_give = in_two(lax.dynamic_slice_in_dim(o_rows, (1 - kv_pos) * half, half))
    message = jnp.concatenate([give_out, o_give], axis=1)
    message, o_far_c = lax.optimization_barrier((message, o_far_c))
    from_x = swap(message, 16)
    o_ups = (o_near, o_far_n, o_near_c, swap(o_far_c, 1))
    return finish(mixed, from_x, o_rows, slot, o_ups)


def on_device(*arrays):
    lengths, key_cache, weight = arrays[13], arrays[4], arrays[2]
    batch, rows, heads = arrays[0].shape[0], lengths.shape[0], key_cache.shape[1]
    staged = batch == 16 * rows and heads == 4 and 2 * weight.shape[1] == 18 * key_cache.shape[3]
    return (staged_path if staged else general_path)(*arrays)


def solution(mesh):
    in_specs = (
        P(None, "kv"),
        P("kv"),
        P("kv", "wide"),
        P("kv", "wide"),
        P("wide", "kv", None, None),
        P("wide", "kv", None, None),
        P("wide", "kv", None),
        P("wide", None, "kv"),
        P("wide", None, None, "kv"),
        P("wide", "kv", None),
        P("wide", None, None),
        P(),
        P(),
        P("wide"),
    )
    out_specs = P("kv", "wide")
    return jax.shard_map(
        on_device, mesh=mesh, in_specs=in_specs, out_specs=out_specs, check_vma=False
    )
```
